128 devices in a mesh: aud: 8 (over z, core), vid: 16 (over y, x).
Axes of the slice: x: 4, y: 4, z: 4, core: 2. Of those that a mesh axis runs over, the one named last changes fastest.
Arguments:
- audio: float32 [16384, 1024], P('aud', 'vid'), may hold values from -8 to 8
- video: float32 [16384, 1024], P('vid', 'aud'), may hold values from -8 to 8
- scale: float32 [], replicated, may hold values from 6 to 12
- bias: float32 [], replicated, may hold values from -7 to -5
Outputs:
- row_loss: float32 [16384], P('aud')
- grad_audio: float32 [16384, 1024], P('aud', 'vid')
- grad_video: float32 [16384, 1024], P('vid', 'aud')
The draws below stay inside these ranges and needn't reach their ends.
All inputs are finite; a program needn't handle non-finite values.
Results may differ from the reference program's by a relative error of at most 0.0003.
Values sent between devices are 32-bit elements; how exact they have to be, the bound alone decides.
No kernel may reach another device: no remote copies, remote signals or barrier semaphores. Data moves between devices by JAX's collectives and lax.ppermute only.
A program may use at most 128 MiB of HBM per device.

```python
import jax
import jax.numpy as jnp
from jax import lax

E = 1024
NA = 16384
NV = 16384


class_count = 64


def shared_latent(key):
    subkeys = jax.random.split(key, 5)
    directions = jax.random.normal(subkeys[0], (class_count, E), jnp.float32)
    first_class = jax.random.randint(subkeys[1], (NA,), 0, class_count)
    second_class = jax.random.randint(subkeys[2], (NA,), 0, class_count)
    weights = jax.random.normal(subkeys[3], (NA, 2), jnp.float32)
    own_part = jax.random.normal(subkeys[4], (NA, E), jnp.float32)
    return weights[:, 0:1] * directions[first_class] + weights[:, 1:2] * directions[second_class] + 0.7 * own_part


def draw_audio(key, part):
    shared = shared_latent(key)
    key = jax.random.fold_in(key, 3)
    jitter_key = jax.random.fold_in(key, 0)
    jitter = jax.random.normal(jitter_key, (NA, E), jnp.float32) * 1.22
    values = (shared + jitter) * 0.5
    return jnp.clip(values, -8.0, 8.0)


def draw_video(key, part):
    shared = shared_latent(key)
    key = jax.random.fold_in(key, 5)
    jitter_key = jax.random.fold_in(key, 0)
    jitter = jax.random.normal(jitter_key, (NV, E), jnp.float32) * 1.22
    values = (shared + jitter) * 0.5
    return jnp.clip(values, -8.0, 8.0)


def setup_inputs(seed: int = 0) -> dict:
    key_list = jax.random.split(jax.random.key(seed), 5)
    return {
        "audio": draw_audio(jax.random.fold_in(key_list[4], 71), 0),
        "video": draw_video(jax.random.fold_in(key_list[4], 71), 0),
        "scale": jnp.clip(jax.random.uniform(key_list[2], (), jnp.float32, 6.0, 12.0), 6.0, 12.0),
        "bias": jnp.clip(jax.random.uniform(key_list[3], (), jnp.float32, -7.0, -5.0), -7.0, -5.0),
    }


def normalize(rows):
    norm = jnp.sqrt(lax.optimization_barrier(jnp.sum(rows * rows, axis=1, keepdims=True)) + 1e-06)
    return (rows / norm, norm)

def project(unit, grad, norm):
    inner = lax.optimization_barrier(jnp.sum(unit * grad, axis=1, keepdims=True))
    return (grad - unit * inner) / norm

def reference(audio, video, scale, bias):
    highest = lax.Precision.HIGHEST
    audio_unit, audio_norm = normalize(audio)
    video_unit, video_norm = normalize(video)
    block = min(512, NA)
    count = NA // block
    columns = jnp.arange(NV, dtype=jnp.int32)

    def step(video_acc, index):
        start = (index * block).astype(jnp.int32)
        rows_a = lax.dynamic_slice_in_dim(audio_unit, start, block, 0)
        logits = scale * jnp.dot(rows_a, video_unit.T, precision=highest, preferred_element_type=jnp.float32) + bias
        paired = (start + jnp.arange(block, dtype=jnp.int32))[:, None] == columns[None, :]
        losses = lax.optimization_barrier(jnp.sum(jax.nn.softplus(jnp.where(paired, -logits, logits)), axis=1))
        pair_grad = jax.nn.sigmoid(logits) - paired.astype(jnp.float32)
        grad_rows = scale * jnp.dot(pair_grad, video_unit, precision=highest, preferred_element_type=jnp.float32)
        video_acc = video_acc + scale * jnp.dot(pair_grad.T, rows_a, precision=highest, preferred_element_type=jnp.float32)
        return (video_acc, (grad_rows, losses))
    video_acc, (audio_grads, losses) = lax.scan(step, jnp.zeros((NV, E), jnp.float32), jnp.arange(count, dtype=jnp.int32))
    audio_grads = audio_grads.reshape(NA, E)
    row_loss = losses.reshape(NA)
    grad_audio = project(audio_unit, audio_grads, audio_norm)
    grad_video = project(video_unit, video_acc, video_norm)
    return (row_loss, grad_audio, grad_video)
```

```python
import jax
import jax.numpy as jnp
from jax import lax
from jax.experimental import pallas as pl
from jax.experimental.pallas import tpu as pltpu
from jax.sharding import Mesh, PartitionSpec as P

F32 = jnp.float32
BF16 = jnp.bfloat16
F8 = jnp.float8_e4m3fn
PARTS = (BF16, F8, F8)
UP_VALUE = 2.0**8
UP_REST = 2.0**17
DOWN = 2.0**-25
EPS = 1e-06
CHUNKS = 2
BLOCK = 512
VMEM = 56 * 2**20
PLANE = ("core", "y", "x")
ROWS = [[4 * i + j for j in range(4)] for i in range(4)]
COLS = [[4 * j + i for j in range(4)] for i in range(4)]
SECOND = lambda groups: [[16 + d for d in g] for g in groups]
INNER = ROWS + SECOND(COLS)
OUTER = COLS + SECOND(ROWS)


def dot(a, b, dims):
    return lax.dot_general(a, b, (dims, ((), ())), preferred_element_type=F32)


def split(x):
    high = x.astype(BF16)
    rest = x - high.astype(F32)
    return high, (x * UP_VALUE).astype(F8), (rest * UP_REST).astype(F8)


def product(a, b, dims):
    a_high, a_value, a_rest = a
    b_high, b_value, b_rest = b
    small = dot(a_value, b_rest, dims) + dot(a_rest, b_value, dims)
    return dot(a_high, b_high, dims) + DOWN * small


def prepare_kernel(place, own_ref, other_ref, inv_ref, unit_t_ref, *parts):
    z, core = place[0], place[1]
    whole, n = parts[-1], parts[-1].shape[0]
    for k, ref in enumerate((own_ref, other_ref)):
        side = jnp.where(k == 0, core, 1 - core)
        for hop in range(4):
            at = lax.rem(z - hop + 4, 4) * 256 + side * 128
            whole[:, pl.ds(pl.multiple_of(at, 128), 128)] = ref[hop]
    v = whole[...]
    inv = lax.rsqrt(jnp.sum(v * v, axis=1, keepdims=True) + EPS)
    inv_ref[...] = inv
    unit = v * inv
    unit_t = unit.T
    unit_t_ref[...] = unit_t
    for ref, part in zip(parts[:3], split(unit)):
        ref[...] = part
    for ref, part in zip(parts[3:6], split(unit_t)):
        ref[...] = part


def prepare(own, other, place):
    _, n, _ = own.shape
    whole = pl.BlockSpec(memory_space=pltpu.VMEM)
    square = lambda dtype: jax.ShapeDtypeStruct((n, 1024), dtype)
    flipped = lambda dtype: jax.ShapeDtypeStruct((1024, n), dtype)
    return pl.pallas_call(
        prepare_kernel,
        in_specs=[pl.BlockSpec(memory_space=pltpu.SMEM), whole, whole],
        out_specs=[whole] * 8,
        out_shape=[jax.ShapeDtypeStruct((n, 1), F32), flipped(F32)]
        + [square(d) for d in PARTS]
        + [flipped(d) for d in PARTS],
        scratch_shapes=[pltpu.VMEM((n, 1024), F32)],
        compiler_params=pltpu.CompilerParams(vmem_limit_bytes=VMEM),
        cost_estimate=pl.CostEstimate(flops=0, bytes_accessed=30 * 2**20, transcendentals=0),
        name="video_parts",
    )(place, own, other)


def pairs_kernel(first, place, scalars, audio_ref, unit_t_ref, *refs):
    video, video_t = refs[0:3], refs[3:6]
    if first:
        loss_ref, grad_a_ref, grad_v_ref, inner_v_ref = refs[6:]
    else:
        before_ref, inner_before_ref, loss_ref, grad_a_ref, grad_v_ref, inner_v_ref = refs[6:]
    step = pl.program_id(0)
    core = place[1]
    scale, bias = scalars[0], scalars[1]
    pieces = [jnp.where(core == 0, 4 * y + x, 4 * x + y) for y in range(4) for x in range(4)]

    @pl.when(step == 0)
    def _():
        if first:
            grad_v_ref[...] = jnp.zeros_like(grad_v_ref)
            inner_v_ref[...] = jnp.zeros_like(inner_v_ref)
        else:
            grad_v_ref[...] = before_ref[...]
            inner_v_ref[...] = inner_before_ref[...]

    audio_t = jnp.concatenate([audio_ref[p] for p in pieces], axis=0)
    inv = lax.rsqrt(jnp.sum(audio_t * audio_t, axis=0, keepdims=True) + EPS)
    unit_t = audio_t * inv
    unit = split(unit_t)
    scaled = scale * product([r[...] for r in video], unit, ((1,), (0,)))
    logits = scaled + bias
    low = jnp.exp(-jnp.abs(logits))
    over = 1.0 / (1.0 + low)
    sig = jnp.where(logits >= 0, over, low * over)
    tail = jnp.where(low < 1e-3, low - 0.5 * low * low, jnp.log(1.0 + low))
    soft = jnp.maximum(logits, 0.0) + tail
    n, block = logits.shape
    offset = place[2] + step * block
    paired = (
        lax.broadcasted_iota(jnp.int32, (n, block), 0)
        - lax.broadcasted_iota(jnp.int32, (n, block), 1)
    ) == offset
    away = jnp.where(paired, 0.0, sig)
    pull = away * scaled
    loss_ref[0:1, :] = jnp.sum(soft, axis=0, keepdims=True)
    loss_ref[1:2, :] = jnp.sum(pull, axis=0, keepdims=True)
    loss_ref[2:3, :] = inv
    inner_v_ref[...] += jnp.sum(pull, axis=1, keepdims=True)
    grads = split(away)
    grad_a = scale * product([r[...] for r in video_t], grads, ((1,), (0,)))
    for k, p in enumerate(pieces):
        grad_a_ref[p] = grad_a[64 * k : 64 * k + 64, :]
    grad_v_ref[...] += scale * product(grads, unit, ((1,), (1,)))

    @pl.when((offset >= 0) & (offset < n))
    def _():
        at = pl.multiple_of(offset, block)
        own = jnp.sum(jnp.where(paired, scaled, 0.0), axis=0, keepdims=True)
        value = own + bias
        low_own = jnp.exp(-jnp.abs(value))
        tail_own = jnp.where(low_own < 1e-3, low_own - 0.5 * low_own * low_own, jnp.log(1.0 + low_own))
        sig_own = jnp.where(value >= 0, 1.0, low_own) / (1.0 + low_own)
        diag = sig_own - 1.0
        loss_ref[0:1, :] += (jnp.maximum(-value, 0.0) + tail_own) - (jnp.maximum(value, 0.0) + tail_own)
        loss_ref[1:2, :] += diag * own
        column = jnp.sum(jnp.where(paired, (sig - 1.0) * scaled, 0.0), axis=1, keepdims=True)
        inner_v_ref[...] += column
        weight = scale * diag
        near = unit_t_ref[:, pl.ds(at, block)] * weight
        for k, p in enumerate(pieces):
            grad_a_ref[p] += near[64 * k : 64 * k + 64, :]
        grad_v_ref[pl.ds(at, block), :] += (unit_t * weight).T


def pairs(audio, video, place, scalars, before):
    count, piece, rows = audio.shape
    first = before is None
    n = video[1].shape[0]
    smem = pl.BlockSpec(memory_space=pltpu.SMEM)
    still = lambda shape: pl.BlockSpec(shape, lambda i: (0, 0), pipeline_mode=pl.Buffered(1))
    moving = lambda: pl.BlockSpec((count, piece, BLOCK), lambda i: (0, 0, i))
    in_specs = [smem, smem, moving(), still((1024, n))] + [still((n, 1024))] * 3 + [still((1024, n))] * 3
    operands = [place, scalars, audio, *video]
    aliases = {}
    if not first:
        aliases = {len(operands): 2, len(operands) + 1: 3}
        in_specs += [still((n, 1024)), still((n, 1))]
        operands += list(before)

    def body(*refs):
        pairs_kernel(first, *refs)

    return pl.pallas_call(
        body,
        grid=(rows // BLOCK,),
        in_specs=in_specs,
        out_specs=[
            pl.BlockSpec((8, BLOCK), lambda i: (0, i)),
            moving(),
            still((n, 1024)),
            still((n, 1)),
        ],
        out_shape=[
            jax.ShapeDtypeStruct((8, rows), F32),
            jax.ShapeDtypeStruct((count, piece, rows), F32),
            jax.ShapeDtypeStruct((n, 1024), F32),
            jax.ShapeDtypeStruct((n, 1), F32),
        ],
        input_output_aliases=aliases,
        compiler_params=pltpu.CompilerParams(vmem_limit_bytes=VMEM),
        cost_estimate=pl.CostEstimate(
            flops=6 * 2 * rows * n * 1024, bytes_accessed=24 * 2**20, transcendentals=3 * rows * n
        ),
        name="pairs_first" if first else "pairs_next",
    )(*operands)


def spread(block, groups):
    copies = jnp.broadcast_to(block[None], (4, *block.shape))
    return lax.all_to_all(copies, PLANE, 0, 0, axis_index_groups=groups)


def total(blocks, groups):
    return jnp.sum(lax.all_to_all(blocks, PLANE, 0, 0, axis_index_groups=groups), axis=0)


def hop(block, k):
    return lax.ppermute(block, "z", [(i, (i + k) % 4) for i in range(4)])


def swap(block):
    return lax.ppermute(block, "core", [(0, 1), (1, 0)])


def local(audio, video, scale, bias):
    z, core = lax.axis_index("z"), lax.axis_index("core")
    vid = lax.axis_index(("y", "x"))
    n = video.shape[0]
    audio_t = audio.T
    piece, rows = audio_t.shape
    part = rows // CHUNKS
    scalars = jnp.stack([scale, bias])

    own = jnp.stack([video] + [hop(video, k) for k in (1, 2, 3)])
    other = swap(own)
    gathered = []
    for c in range(CHUNKS):
        block = audio_t[:, c * part : (c + 1) * part]
        gathered.append(spread(spread(block, INNER).reshape(4 * piece, part), OUTER).reshape(16, piece, part))
    base = (2 * z + core) * rows - vid * n
    place = jnp.stack([z, core, base]).astype(jnp.int32)
    inv_v, *parts = prepare(own, other, place)
    state = None
    sums, pieces = [], []
    for c in range(CHUNKS):
        at = jnp.stack([z, core, base + c * part]).astype(jnp.int32)
        side, grad_a, *state = pairs(gathered[c], parts, at, scalars, state)
        sums.append(side)
        grad_a = total(grad_a.reshape(4, 4 * piece, part), OUTER)
        pieces.append(total(grad_a.reshape(4, piece, part), INNER))
    grad_v, inner_v = state

    side = jnp.concatenate(sums, axis=1)
    both = jnp.broadcast_to(side[None, 0:2], (16, 2, rows))
    both = jnp.sum(lax.all_to_all(both, ("y", "x"), 0, 0), axis=0)
    row_loss, inner_a = both[0], both[1:2]
    inv_a = side[2:3]

    inner = jnp.broadcast_to(inner_v.reshape(1, n // 128, 128), (8, n // 128, 128))
    inner = jnp.sum(lax.all_to_all(inner, ("z", "core"), 0, 0), axis=0).reshape(n, 1)
    by_feature = grad_v.reshape(n, 4, 2, 128)
    mine = lax.dynamic_index_in_dim(by_feature, core, 2, False)
    theirs = lax.dynamic_index_in_dim(by_feature, 1 - core, 2, False)
    half = (mine + swap(theirs)).transpose(1, 0, 2)
    total_v = lax.dynamic_index_in_dim(half, z, 0, False)
    for k in (1, 2, 3):
        total_v = total_v + hop(lax.dynamic_index_in_dim(half, lax.rem(z + k, 4), 0, False), k)

    total_a = jnp.concatenate(pieces, axis=1)
    grad_audio = total_a * inv_a - audio_t * (inv_a * inv_a * inner_a)
    grad_video = total_v * inv_v - video * (inv_v * inv_v * inner)
    return row_loss, grad_audio.T, grad_video


def solution(mesh):
    fine = Mesh(mesh.devices.reshape(4, 2, 4, 4), ("z", "core", "y", "x"))
    aud, vid = ("z", "core"), ("y", "x")
    return jax.shard_map(
        local,
        mesh=fine,
        in_specs=(P(aud, vid), P(vid, aud), P(), P()),
        out_specs=(P(aud), P(aud, vid), P(vid, aud)),
        check_vma=False,
    )
```

```python
import jax
import jax.numpy as jnp
from jax import lax
from jax.experimental import pallas as pl
from jax.experimental.pallas import tpu as pltpu
from jax.sharding import Mesh, PartitionSpec as P

F32 = jnp.float32
BF16 = jnp.bfloat16
F8 = jnp.float8_e4m3fn
UP_VALUE = 2.0**8
UP_REST = 2.0**17
DOWN = 2.0**-25
EPS = 1e-06
CHUNKS = (1024, 1024)
BLOCK = 512
VMEM = 56 * 2**20
PLANE = ("core", "y", "x")
MIB = 2**20


def dot(a, b, dims):
    return lax.dot_general(a, b, (dims, ((), ())), preferred_element_type=F32)


def split(x, axis, value_first):
    high = x.astype(BF16)
    rest = ((x - high.astype(F32)) * UP_REST).astype(F8)
    value = (x * UP_VALUE).astype(F8)
    pair = (value, rest) if value_first else (rest, value)
    return high, jnp.concatenate(pair, axis=axis)


def product(a, b, dims):
    return dot(a[0], b[0], dims) + DOWN * dot(a[1], b[1], dims)


def prepare_kernel(place, own_ref, other_ref, inv_ref, unit_t_ref, v_high, v_small, t_high, t_small, whole, flipped):
    core, y, x, z = place[0], place[1], place[2], place[3]
    n = whole.shape[0]
    for k, ref in enumerate((own_ref, other_ref)):
        side = jnp.where(k == 0, core, 1 - core)
        for hops in range(4):
            at = 256 * lax.rem(z + 4 - hops, 4) + 128 * side
            whole[:, pl.ds(pl.multiple_of(at, 128), 128)] = ref[hops]
    v_t = whole[...].T
    inv = lax.rsqrt(jnp.sum(v_t * v_t, axis=0, keepdims=True) + EPS)
    inv_ref[...] = inv
    flipped[...] = (v_t * inv).reshape(16, 64, n)
    for outer in range(4):
        for inner in range(4):
            row = lax.rem(y + 4 - jnp.where(core == 0, outer, inner), 4)
            column = lax.rem(x + 4 - jnp.where(core == 0, inner, outer), 4)
            at = 64 * (4 * outer + inner)
            unit_t_ref[at : at + 64, :] = flipped[4 * row + column]
    unit_t = unit_t_ref[...]
    for (high, small), part, axis in (((t_high, t_small), unit_t, 1), ((v_high, v_small), unit_t.T, 1)):
        high[...], small[...] = split(part, axis, True)


def prepare(own, other, place):
    _, n, _ = own.shape
    whole = pl.BlockSpec(memory_space=pltpu.VMEM)
    shape = jax.ShapeDtypeStruct
    return pl.pallas_call(
        prepare_kernel,
        in_specs=[pl.BlockSpec(memory_space=pltpu.SMEM), whole, whole],
        out_specs=[whole] * 6,
        out_shape=[
            shape((1, n), F32),
            shape((1024, n), F32),
            shape((n, 1024), BF16),
            shape((n, 2048), F8),
            shape((1024, n), BF16),
            shape((1024, 2 * n), F8),
        ],
        scratch_shapes=[pltpu.VMEM((n, 1024), F32), pltpu.VMEM((16, 64, n), F32)],
        compiler_params=pltpu.CompilerParams(vmem_limit_bytes=VMEM),
        cost_estimate=pl.CostEstimate(flops=0, bytes_accessed=30 * MIB, transcendentals=0),
        name="video_parts",
    )(place, own, other)


def soft_tail(low):
    return jnp.where(low < 1e-3, low - 0.5 * low * low, jnp.log(1.0 + low))


def pairs_kernel(first, last, refs):
    place, scalars, *refs = refs
    audio, refs = refs[:4], refs[4:]
    _, unit_t_hbm, v_high, v_small, t_high, t_small, *refs = refs
    before = None
    if not first:
        before, *refs = refs
    grads_a, inv_ref, refs = refs[:4], refs[4], refs[5:]
    if last:
        mine, theirs, state, near, sem = refs
    else:
        state, near, sem = refs
    step = pl.program_id(0)
    scale, bias = scalars[0], scalars[1]
    n = v_high.shape[0]

    @pl.when(step == 0)
    def _():
        if first:
            state[...] = jnp.zeros_like(state)
        else:
            state[...] = before[...]

    audio_t = jnp.concatenate([r[...] for r in audio], axis=0)
    inv = lax.rsqrt(jnp.sum(audio_t * audio_t, axis=0, keepdims=True) + EPS)
    inv_ref[...] = inv
    unit_t = audio_t * inv
    block = unit_t.shape[1]
    scaled = scale * product((v_high[...], v_small[...]), split(unit_t, 0, False), ((1,), (0,)))
    logits = scaled + bias
    low = jnp.exp(-jnp.abs(logits))
    over = 1.0 / (1.0 + low)
    sig = jnp.where(logits >= 0, over, low * over)
    soft = jnp.maximum(logits, 0.0) + soft_tail(low)
    offset = place[3] + step * block
    paired = (
        lax.broadcasted_iota(jnp.int32, (n, block), 0)
        - lax.broadcasted_iota(jnp.int32, (n, block), 1)
    ) == offset
    away = jnp.where(paired, 0.0, sig)
    loss = jnp.sum(soft, axis=0, keepdims=True)
    grad_a = product((t_high[...], t_small[...]), split(away, 0, False), ((1,), (0,)))
    inner = jnp.sum(grad_a * unit_t, axis=0, keepdims=True)
    for k, ref in enumerate(grads_a):
        ref[0:256, :] = grad_a[256 * k : 256 * k + 256, :]
        ref[256:257, :] = loss
        ref[257:258, :] = inner
        ref[258:264, :] = jnp.zeros((6, block), F32)
    state[...] += product(split(unit_t, 1, True), split(away, 1, False), ((1,), (1,)))

    @pl.when((offset >= 0) & (offset < n))
    def _():
        at = pl.multiple_of(offset, block)
        copy = pltpu.make_async_copy(unit_t_hbm.at[:, pl.ds(at, block)], near, sem)
        copy.start()
        own = jnp.sum(jnp.where(paired, scaled, 0.0), axis=0, keepdims=True)
        value = own + bias
        low_own = jnp.exp(-jnp.abs(value))
        diag = jnp.where(value >= 0, 1.0, low_own) / (1.0 + low_own) - 1.0
        copy.wait()
        pull = near[...] * diag
        inner_own = jnp.sum(pull * unit_t, axis=0, keepdims=True)
        for k, ref in enumerate(grads_a):
            ref[0:256, :] += pull[256 * k : 256 * k + 256, :]
            ref[256:257, :] += -value
            ref[257:258, :] += inner_own
        state[:, pl.ds(at, block)] += unit_t * diag

    if last:

        @pl.when(step == pl.num_programs(0) - 1)
        def _():
            core, y, x, z = place[0], place[1], place[2], place[4]
            for half in range(n // block):
                lanes = pl.ds(half * block, block)
                copy = pltpu.make_async_copy(unit_t_hbm.at[:, lanes], near, sem)
                copy.start()
                copy.wait()
                row = jnp.sum(near[...] * state[:, lanes], axis=0, keepdims=True)
                for ref in (mine, theirs):
                    for owner in range(4):
                        ref[owner, 128:129, lanes] = row
            for k, ref in enumerate((mine, theirs)):
                side = jnp.where(k == 0, core, 1 - core)
                for owner in range(4):
                    ref[owner, 129:136, :] = jnp.zeros((7, n), F32)
                    dy = lax.rem(y + 8 - z - owner, 4)
                    for part in range(2):
                        dx = lax.rem(x + 4 - 2 * side - part, 4)
                        at = jnp.where(core == 0, 4 * dy + dx, 4 * dx + dy) * 64
                        rows = pl.ds(pl.multiple_of(at, 64), 64)
                        ref[owner, 64 * part : 64 * part + 64, :] = state[rows, :]


def pairs(audio, ahead, video, place, scalars, before, last):
    rows = audio[0].shape[1]
    first = before is None
    n = video[1].shape[0]
    smem = pl.BlockSpec(memory_space=pltpu.SMEM)
    still = lambda shape: pl.BlockSpec(shape, lambda i: (0, 0), pipeline_mode=pl.Buffered(1))
    moving = lambda height: pl.BlockSpec((height, BLOCK), lambda i: (0, i))
    shape = jax.ShapeDtypeStruct
    in_specs = [smem, smem] + [moving(256)] * 4 + [pl.BlockSpec(memory_space=pl.ANY)] * 2
    in_specs += [still(v.shape) for v in video[1:]]
    operands = [place, scalars, *audio, ahead, *video]
    out_specs = [moving(264)] * 4 + [moving(1)]
    out_shape = [shape((264, rows), F32)] * 4 + [shape((1, rows), F32)]
    scratch = [pltpu.VMEM((1024, BLOCK), F32), pltpu.SemaphoreType.DMA]
    aliases = {}
    if not first:
        if not last:
            aliases = {len(operands): 5}
        in_specs.append(still((1024, n)))
        operands.append(before)
    if last:
        out_specs += [pl.BlockSpec((4, 136, n), lambda i: (0, 0, 0), pipeline_mode=pl.Buffered(1))] * 2
        out_shape += [shape((4, 136, n), F32)] * 2
        scratch = [pltpu.VMEM((1024, n), F32)] + scratch
    else:
        out_specs.append(still((1024, n)))
        out_shape.append(shape((1024, n), F32))

    def body(*refs):
        pairs_kernel(first, last, refs)

    return pl.pallas_call(
        body,
        grid=(rows // BLOCK,),
        in_specs=in_specs,
        out_specs=out_specs,
        out_shape=out_shape,
        scratch_shapes=scratch,
        input_output_aliases=aliases,
        compiler_params=pltpu.CompilerParams(vmem_limit_bytes=VMEM),
        cost_estimate=pl.CostEstimate(
            flops=6 * 2 * rows * n * 1024, bytes_accessed=24 * MIB, transcendentals=3 * rows * n
        ),
        name="pairs_last" if last else "pairs_first" if first else "pairs_next",
    )(*operands)


def perm(inner, k):
    pairs_of = []
    for core in range(2):
        for y in range(4):
            for x in range(4):
                along_x = (core == 0) == inner
                to = (core, y, (x + k) % 4) if along_x else (core, (y + k) % 4, x)
                pairs_of.append((16 * core + 4 * y + x, 16 * to[0] + 4 * to[1] + to[2]))
    return pairs_of


def move(block, inner, k):
    return lax.ppermute(block, PLANE, perm(inner, k))


def hop(block, k):
    return lax.ppermute(block, "z", [(i, (i + k) % 4) for i in range(4)])


def together(*arrays):
    spec = pl.BlockSpec(memory_space=pl.ANY)
    return pl.pallas_call(
        lambda *refs: None,
        in_specs=[spec] * len(arrays),
        out_specs=[spec] * len(arrays),
        out_shape=[jax.ShapeDtypeStruct(a.shape, a.dtype) for a in arrays],
        input_output_aliases={i: i for i in range(len(arrays))},
        name="together",
    )(*arrays)


def swap(block):
    return lax.ppermute(block, "core", [(0, 1), (1, 0)])


def local(audio, video, scale, bias):
    z, core, y, x = (lax.axis_index(a) for a in ("z", "core", "y", "x"))
    n = video.shape[0]
    audio_t = audio.T
    piece, rows = audio_t.shape
    scalars = jnp.stack([scale, bias])
    base = (2 * z + core) * rows - (4 * y + x) * n

    up, down = hop(video, 1), hop(video, 3)
    row = [audio_t] + [move(audio_t, True, k) for k in (1, 2, 3)]
    gathered, starts, start = [], [], 0
    for part in CHUNKS:
        block = jnp.concatenate([r[:, start : start + part] for r in row], axis=0)
        if start == 0:
            up, down, block = together(up, down, block)
            far = jnp.concatenate([hop(up[: n // 2], 1), hop(down[n // 2 :], 3)], axis=0)
        gathered.append([block] + [move(block, False, k) for k in (1, 2, 3)])
        starts.append(start)
        start += part
    own = jnp.stack([video, up, far, down])
    other = swap(own)
    place = jnp.stack([core, y, x, z]).astype(jnp.int32)
    inv_v, *parts = prepare(own, other, place)
    state = None
    invs, halves = [], []
    for c, blocks in enumerate(gathered):
        at = jnp.stack([core, y, x, base + starts[c], z]).astype(jnp.int32)
        last = c == len(CHUNKS) - 1
        ahead = gathered[min(c + 1, len(CHUNKS) - 1)][0]
        outs = pairs(blocks, ahead, parts, at, scalars, state, last)
        grads, inv, state = outs[:4], outs[4], outs[5]
        invs.append(inv)
        if c > 0:
            *came, second, third, fourth, theirs = together(*came, *grads[1:4], outs[-1])
            halves.append(kept + came[0] + came[1] + came[2])
            grads = [grads[0], second, third, fourth]
        kept = grads[0]
        came = [move(grads[k], False, 4 - k) for k in (1, 2, 3)]
    halves.append(kept + came[0] + came[1] + came[2])
    half = outs[5] + swap(theirs)
    mid = n // 2
    below, above, halves[-1] = together(hop(half[2, :, :mid], 1), hop(half[2, :, mid:], 3), halves[-1])
    to_up = jnp.concatenate([half[1, :, :mid] + below, half[1, :, mid:]], axis=1)
    to_down = jnp.concatenate([half[3, :, :mid], half[3, :, mid:] + above], axis=1)
    total_v = half[0] + hop(to_up, 1) + hop(to_down, 3)
    to = [
        jnp.concatenate(
            [jnp.concatenate([h[64 * k : 64 * k + 64], h[256:264]], axis=0) for h in halves], axis=1
        )
        for k in range(4)
    ]
    total_a = to[0]
    for k in (1, 2, 3):
        total_a = total_a + move(to[k], True, 4 - k)
    inv_a = jnp.concatenate(invs, axis=1)
    row_loss, inner_a = total_a[64], total_a[65:66]
    grad_a = scale * (total_a[0:64] * inv_a - audio_t * (inv_a * inv_a * inner_a))
    grad_v = scale * (total_v[0:128] * inv_v - video.T * (inv_v * inv_v * total_v[128:129]))
    return row_loss, grad_a.T, grad_v.T


def solution(mesh):
    fine = Mesh(mesh.devices.reshape(4, 2, 4, 4), ("z", "core", "y", "x"))
    aud, vid = ("z", "core"), ("y", "x")
    return jax.shard_map(
        local,
        mesh=fine,
        in_specs=(P(aud, vid), P(vid, aud), P(), P()),
        out_specs=(P(aud), P(aud, vid), P(vid, aud)),
        check_vma=False,
    )
```

```python
import jax
import jax.numpy as jnp
from jax import lax
from jax.experimental import pallas as pl
from jax.experimental.pallas import tpu as pltpu
from jax.sharding import Mesh, PartitionSpec as P

F32 = jnp.float32
BF16 = jnp.bfloat16
F8 = jnp.float8_e4m3fn
UP_VALUE = 2.0**8
UP_REST = 2.0**17
DOWN = 2.0**-25
EPS = 1e-06
CHUNKS = (1024, 1024)
BLOCK = 512
SUBS = 2
VMEM = 56 * 2**20
PLANE = ("core", "y", "x")
MIB = 2**20


def dot(a, b, dims):
    return lax.dot_general(a, b, (dims, ((), ())), preferred_element_type=F32)


def split(x, axis, value_first):
    high = x.astype(BF16)
    rest = ((x - high.astype(F32)) * UP_REST).astype(F8)
    value = (x * UP_VALUE).astype(F8)
    pair = (value, rest) if value_first else (rest, value)
    return high, jnp.concatenate(pair, axis=axis)


def product(a, b, dims):
    return dot(a[0], b[0], dims) + DOWN * dot(a[1], b[1], dims)


def prepare_kernel(place, whole, inv_ref, unit_t_ref, v_high, v_small, t_high, t_small, flipped):
    core, y, x = place[0], place[1], place[2]
    n = whole.shape[0]
    v_t = whole[...].T
    inv = lax.rsqrt(jnp.sum(v_t * v_t, axis=0, keepdims=True) + EPS)
    inv_ref[...] = inv
    flipped[...] = (v_t * inv).reshape(16, 64, n)
    for outer in range(4):
        for inner in range(4):
            row = lax.rem(y + 4 - jnp.where(core == 0, outer, inner), 4)
            column = lax.rem(x + 4 - jnp.where(core == 0, inner, outer), 4)
            at = 64 * (4 * outer + inner)
            unit_t_ref[at : at + 64, :] = flipped[4 * row + column]
    unit_t = unit_t_ref[...]
    for (high, small), part, axis in (((t_high, t_small), unit_t, 1), ((v_high, v_small), unit_t.T, 1)):
        high[...], small[...] = split(part, axis, True)


def prepare(video, place):
    n = video.shape[0]
    whole = pl.BlockSpec(memory_space=pltpu.VMEM)
    shape = jax.ShapeDtypeStruct
    return pl.pallas_call(
        prepare_kernel,
        in_specs=[pl.BlockSpec(memory_space=pltpu.SMEM), whole],
        out_specs=[whole] * 6,
        out_shape=[
            shape((1, n), F32),
            shape((1024, n), F32),
            shape((n, 1024), BF16),
            shape((n, 2048), F8),
            shape((1024, n), BF16),
            shape((1024, 2 * n), F8),
        ],
        scratch_shapes=[pltpu.VMEM((16, 64, n), F32)],
        compiler_params=pltpu.CompilerParams(vmem_limit_bytes=VMEM),
        cost_estimate=pl.CostEstimate(flops=0, bytes_accessed=16 * MIB, transcendentals=0),
        name="video_parts",
    )(place, video)


def inverse(d):
    r = pl.reciprocal(d, approx=True)
    return r * (2.0 - d * r)


def soft(power):
    return jnp.where(power < 1e-3, power - 0.5 * power * power, jnp.log(1.0 + power))


def pairs_kernel(first, last, refs):
    place, scalars, *refs = refs
    audio, refs = refs[:4], refs[4:]
    _, unit_t_hbm, *sources = refs[:6]
    refs = refs[6:]
    before = None
    if not first:
        before, *refs = refs
    grads_a, inv_ref, refs = refs[:4], refs[4], refs[5:]
    if last:
        whole, *refs = refs
    state, near, v_high, v_small, t_high, t_small, sem, sems = refs
    step = pl.program_id(0)
    scale, bias = scalars[0], scalars[1]
    n = v_high.shape[0]
    block = inv_ref.shape[1]
    sub = block // SUBS
    offset = place[3] + step * block
    loads = [
        pltpu.make_async_copy(source, to, sems.at[k])
        for k, (source, to) in enumerate(zip(sources, (v_high, v_small, t_high, t_small)))
    ]
    if not first:
        loads.append(pltpu.make_async_copy(before, state, sems.at[4]))

    @pl.when(step == 0)
    def _():
        for load in loads:
            load.start()
        if first:
            state[...] = jnp.zeros_like(state)

    audio_t = jnp.concatenate([r[...] for r in audio], axis=0)
    inv = lax.rsqrt(jnp.sum(audio_t * audio_t, axis=0, keepdims=True) + EPS)
    inv_ref[...] = inv
    unit_t = audio_t * inv

    @pl.when(step == 0)
    def _():
        for load in loads[:2]:
            load.wait()

    def similar(k):
        part = split(unit_t[:, k * sub : (k + 1) * sub], 0, False)
        return scale * product((v_high[...], v_small[...]), part, ((1,), (0,)))

    def judge(k, scaled):
        power = jnp.exp(scaled + bias)
        sig = power * inverse(1.0 + power)
        paired = (
            lax.broadcasted_iota(jnp.int32, (n, sub), 0)
            - lax.broadcasted_iota(jnp.int32, (n, sub), 1)
        ) == offset + k * sub
        loss = jnp.sum(soft(power), axis=0, keepdims=True)
        return paired, split(jnp.where(paired, 0.0, sig), 0, False), loss

    def pull_rows(k, away, loss):
        lanes = slice(k * sub, (k + 1) * sub)
        grad_a = product((t_high[...], t_small[...]), away, ((1,), (0,)))
        inner = jnp.sum(grad_a * unit_t[:, lanes], axis=0, keepdims=True)
        for p, ref in enumerate(grads_a):
            ref[0:256, lanes] = grad_a[256 * p : 256 * p + 256, :]
            ref[256:257, lanes] = loss
            ref[257:258, lanes] = inner
            ref[258:264, lanes] = jnp.zeros((6, sub), F32)

    scores = [similar(k) for k in range(SUBS)]
    judged = [judge(0, scores[0])]

    @pl.when(step == 0)
    def _():
        for load in loads[2:]:
            load.wait()

    for k in range(SUBS):
        if k > 0:
            judged.append(judge(k, scores[k]))
        pull_rows(k, judged[k][1], judged[k][2])
    high = jnp.concatenate([j[1][0] for j in judged], axis=1)
    small = jnp.concatenate([j[1][1][:n] for j in judged] + [j[1][1][n:] for j in judged], axis=1)
    state[...] += product(split(unit_t, 1, True), (high, small), ((1,), (1,)))

    @pl.when((offset >= 0) & (offset < n))
    def _():
        at = pl.multiple_of(offset, block)
        copy = pltpu.make_async_copy(unit_t_hbm.at[:, pl.ds(at, block)], near, sem)
        copy.start()
        own = jnp.concatenate(
            [jnp.sum(jnp.where(j[0], s, 0.0), axis=0, keepdims=True) for j, s in zip(judged, scores)],
            axis=1,
        )
        value = own + bias
        diag = -1.0 / (1.0 + jnp.exp(value))
        copy.wait()
        pull = near[...] * diag
        inner_own = jnp.sum(pull * unit_t, axis=0, keepdims=True)
        for k, ref in enumerate(grads_a):
            ref[0:256, :] += pull[256 * k : 256 * k + 256, :]
            ref[256:257, :] += -value
            ref[257:258, :] += inner_own
        state[:, pl.ds(at, block)] += unit_t * diag

    if last:

        @pl.when(step == pl.num_programs(0) - 1)
        def _():
            core, y, x = place[0], place[1], place[2]
            for half in range(n // block):
                lanes = pl.ds(half * block, block)
                copy = pltpu.make_async_copy(unit_t_hbm.at[:, lanes], near, sem)
                copy.start()
                copy.wait()
                row = jnp.sum(near[...] * state[:, lanes], axis=0, keepdims=True)
                for owner in range(8):
                    whole[owner, 128:129, lanes] = row
            for owner in range(8):
                whole[owner, 129:136, :] = jnp.zeros((7, n), F32)
                for part in range(2):
                    dy = lax.rem(y + 4 - owner // 2, 4)
                    dx = lax.rem(x + 4 - 2 * (owner % 2) - part, 4)
                    at = jnp.where(core == 0, 4 * dy + dx, 4 * dx + dy) * 64
                    rows = pl.ds(pl.multiple_of(at, 64), 64)
                    whole[owner, 64 * part : 64 * part + 64, :] = state[rows, :]


def pairs(audio, ahead, video, place, scalars, before, last):
    rows = audio[0].shape[1]
    first = before is None
    n = video[1].shape[0]
    smem = pl.BlockSpec(memory_space=pltpu.SMEM)
    still = lambda shape: pl.BlockSpec(shape, lambda i: (0, 0), pipeline_mode=pl.Buffered(1))
    moving = lambda height: pl.BlockSpec((height, BLOCK), lambda i: (0, i))
    shape = jax.ShapeDtypeStruct
    anywhere = pl.BlockSpec(memory_space=pl.ANY)
    in_specs = [smem, smem] + [moving(256)] * 4 + [anywhere] * 6
    operands = [place, scalars, *audio, ahead, *video]
    out_specs = [moving(264)] * 4 + [moving(1)]
    out_shape = [shape((264, rows), F32)] * 4 + [shape((1, rows), F32)]
    scratch = [pltpu.VMEM((1024, BLOCK), F32)] + [pltpu.VMEM(v.shape, v.dtype) for v in video[1:]]
    scratch += [pltpu.SemaphoreType.DMA, pltpu.SemaphoreType.DMA((5,))]
    if not first:
        in_specs.append(anywhere)
        operands.append(before)
    if last:
        out_specs.append(pl.BlockSpec((8, 136, n), lambda i: (0, 0, 0), pipeline_mode=pl.Buffered(1)))
        out_shape.append(shape((8, 136, n), F32))
        scratch = [pltpu.VMEM((1024, n), F32)] + scratch
    else:
        out_specs.append(still((1024, n)))
        out_shape.append(shape((1024, n), F32))

    def body(*refs):
        pairs_kernel(first, last, refs)

    return pl.pallas_call(
        body,
        grid=(rows // BLOCK,),
        in_specs=in_specs,
        out_specs=out_specs,
        out_shape=out_shape,
        scratch_shapes=scratch,
        compiler_params=pltpu.CompilerParams(vmem_limit_bytes=VMEM),
        cost_estimate=pl.CostEstimate(
            flops=6 * 2 * rows * n * 1024, bytes_accessed=24 * MIB, transcendentals=3 * rows * n
        ),
        name="pairs_last" if last else "pairs_first" if first else "pairs_next",
    )(*operands)


def perm(inner, k):
    pairs_of = []
    for core in range(2):
        for y in range(4):
            for x in range(4):
                along_x = (core == 0) == inner
                to = (core, y, (x + k) % 4) if along_x else (core, (y + k) % 4, x)
                pairs_of.append((16 * core + 4 * y + x, 16 * to[0] + 4 * to[1] + to[2]))
    return pairs_of


def move(block, inner, k):
    return lax.ppermute(block, PLANE, perm(inner, k))


def after(arrays, late):
    spec = pl.BlockSpec(memory_space=pl.ANY)
    return pl.pallas_call(
        lambda *refs: None,
        in_specs=[spec] * (len(arrays) + len(late)),
        out_specs=[spec] * len(late),
        out_shape=[jax.ShapeDtypeStruct(a.shape, a.dtype) for a in late],
        input_output_aliases={len(arrays) + i: i for i in range(len(late))},
        name="after",
    )(*arrays, *late)


def local(audio, video, scale, bias):
    z, core, y, x = (lax.axis_index(a) for a in ("z", "core", "y", "x"))
    n = video.shape[0]
    audio_t = audio.T
    rows = audio_t.shape[1]
    scalars = jnp.stack([scale, bias])
    base = (2 * z + core) * rows - (4 * y + x) * n

    whole_video = lax.all_gather(video, ("z", "core"), axis=1, tiled=True)
    row = [audio_t] + [move(audio_t, True, k) for k in (1, 2, 3)]
    gathered, starts, start = [], [], 0
    for part in CHUNKS:
        block = jnp.concatenate([r[:, start : start + part] for r in row], axis=0)
        gathered.append([block] + [move(block, False, k) for k in (1, 2, 3)])
        starts.append(start)
        start += part
    place = jnp.stack([core, y, x]).astype(jnp.int32)
    inv_v, *parts = prepare(whole_video, place)
    state = None
    invs, halves = [], []
    for c, blocks in enumerate(gathered):
        at = jnp.stack([core, y, x, base + starts[c]]).astype(jnp.int32)
        last = c == len(CHUNKS) - 1
        ahead = gathered[min(c + 1, len(CHUNKS) - 1)][0]
        outs = pairs(blocks, ahead, parts, at, scalars, state, last)
        grads, inv, state = outs[:4], outs[4], outs[5]
        invs.append(inv)
        if c > 0:
            seen = came[0][256:264] + came[1][256:264] + came[2][256:264]
            *others, state = after([seen], [*grads[1:], state])
            grads = [grads[0], *others]
            halves.append(kept + came[0] + came[1] + came[2])
        kept = grads[0]
        came = [move(grads[k], False, 4 - k) for k in (1, 2, 3)]
    halves.append(kept + came[0] + came[1] + came[2])

    total_v = lax.psum_scatter(state.reshape(1088, n), ("z", "core"), scatter_dimension=0, tiled=True)
    to = [
        jnp.concatenate(
            [jnp.concatenate([h[64 * k : 64 * k + 64], h[256:264]], axis=0) for h in halves], axis=1
        )
        for k in range(4)
    ]
    total_a = to[0]
    for k in (1, 2, 3):
        total_a = total_a + move(to[k], True, 4 - k)
    inv_a = jnp.concatenate(invs, axis=1)
    row_loss, inner_a = total_a[64], total_a[65:66]
    grad_a = scale * (total_a[0:64] * inv_a - audio_t * (inv_a * inv_a * inner_a))
    grad_v = scale * (total_v[0:128] * inv_v - video.T * (inv_v * inv_v * total_v[128:129]))
    return row_loss, grad_a.T, grad_v.T


def solution(mesh):
    fine = Mesh(mesh.devices.reshape(4, 2, 4, 4), ("z", "core", "y", "x"))
    aud, vid = ("z", "core"), ("y", "x")
    return jax.shard_map(
        local,
        mesh=fine,
        in_specs=(P(aud, vid), P(vid, aud), P(), P()),
        out_specs=(P(aud), P(aud, vid), P(vid, aud)),
        check_vma=False,
    )
```

```python
import jax
import jax.numpy as jnp
from jax import lax
from jax.experimental import pallas as pl
from jax.experimental.pallas import tpu as pltpu
from jax.sharding import Mesh, PartitionSpec as P

F32 = jnp.float32
BF16 = jnp.bfloat16
F8 = jnp.float8_e4m3fn
UP_VALUE = 2.0**8
UP_REST = 2.0**17
DOWN = 2.0**-25
EPS = 1e-06
CHUNKS = (512, 1024, 512)
BLOCK = 512
SUBS = 2
VMEM = 56 * 2**20
PLANE = ("core", "y", "x")
MIB = 2**20


def dot(a, b, dims):
    return lax.dot_general(a, b, (dims, ((), ())), preferred_element_type=F32)


def split(x, axis, value_first):
    high = x.astype(BF16)
    rest = ((x - high.astype(F32)) * UP_REST).astype(F8)
    value = (x * UP_VALUE).astype(F8)
    pair = (value, rest) if value_first else (rest, value)
    return high, jnp.concatenate(pair, axis=axis)


def product(a, b, dims):
    return dot(a[0], b[0], dims) + DOWN * dot(a[1], b[1], dims)


def prepare_kernel(place, whole, inv_ref, unit_t_out, v_high_out, v_small_out, t_high_out, t_small_out, *scratch):
    flipped, unit_t_ref, v_high, v_small, t_high, t_small, sems = scratch
    core, y, x = place[0], place[1], place[2]
    n = whole.shape[0]
    outs = (unit_t_out, t_high_out, t_small_out, v_high_out, v_small_out)
    copies = [
        pltpu.make_async_copy(ref, out, sems.at[k])
        for k, (ref, out) in enumerate(zip((unit_t_ref, t_high, t_small, v_high, v_small), outs))
    ]
    v_t = whole[...].T
    inv = lax.rsqrt(jnp.sum(v_t * v_t, axis=0, keepdims=True) + EPS)
    inv_ref[...] = inv
    flipped[...] = (v_t * inv).reshape(16, 64, n)
    for outer in range(4):
        for inner in range(4):
            row = lax.rem(y + 4 - jnp.where(core == 0, outer, inner), 4)
            column = lax.rem(x + 4 - jnp.where(core == 0, inner, outer), 4)
            at = 64 * (4 * outer + inner)
            unit_t_ref[at : at + 64, :] = flipped[4 * row + column]
    copies[0].start()
    unit_t = unit_t_ref[...]
    t_high[...], t_small[...] = split(unit_t, 1, True)
    copies[1].start()
    copies[2].start()
    v_high[...], v_small[...] = split(unit_t.T, 1, True)
    copies[3].start()
    copies[4].start()
    for copy in copies:
        copy.wait()


def prepare(video, place):
    n = video.shape[0]
    whole = pl.BlockSpec(memory_space=pltpu.VMEM)
    shape = jax.ShapeDtypeStruct
    parts = [
        shape((1024, n), F32),
        shape((n, 1024), BF16),
        shape((n, 2048), F8),
        shape((1024, n), BF16),
        shape((1024, 2 * n), F8),
    ]
    return pl.pallas_call(
        prepare_kernel,
        in_specs=[pl.BlockSpec(memory_space=pltpu.SMEM), whole],
        out_specs=[whole] + [pl.BlockSpec(memory_space=pl.ANY)] * 5,
        out_shape=[shape((1, n), F32)] + parts,
        scratch_shapes=[pltpu.VMEM((16, 64, n), F32)]
        + [pltpu.VMEM(p.shape, p.dtype) for p in parts]
        + [pltpu.SemaphoreType.DMA((5,))],
        compiler_params=pltpu.CompilerParams(vmem_limit_bytes=VMEM),
        cost_estimate=pl.CostEstimate(flops=0, bytes_accessed=16 * MIB, transcendentals=0),
        name="video_parts",
    )(place, video)


def inverse(d):
    r = pl.reciprocal(d, approx=True)
    return r * (2.0 - d * r)


def soft(power):
    return jnp.where(power < 1e-3, power - 0.5 * power * power, jnp.log(1.0 + power))


def pairs_kernel(first, last, count, skipped, refs):
    place, scalars, *refs = refs
    audio, refs = refs[:count], refs[count + skipped :]
    unit_t_hbm, *sources = refs[:5]
    refs = refs[5:]
    before = None
    if not first:
        before, *refs = refs
    grads_a, inv_ref, refs = refs[:4], refs[4], refs[5:]
    if last:
        whole, *refs = refs
    state, near, v_high, v_small, t_high, t_small, sem, sems = refs
    step = pl.program_id(0)
    scale, bias = scalars[0], scalars[1]
    n = v_high.shape[0]
    block = inv_ref.shape[1]
    sub = block // SUBS
    offset = place[3] + step * block
    loads = [
        pltpu.make_async_copy(source, to, sems.at[k])
        for k, (source, to) in enumerate(zip(sources, (v_high, v_small, t_high, t_small)))
    ]
    if not first:
        loads.append(pltpu.make_async_copy(before, state, sems.at[4]))

    @pl.when(step == 0)
    def _():
        for load in loads:
            load.start()
        if first:
            state[...] = jnp.zeros_like(state)

    crossing = (offset >= 0) & (offset < n)
    at = pl.multiple_of(jnp.where(crossing, offset, 0), block)
    fetch = pltpu.make_async_copy(unit_t_hbm.at[:, pl.ds(at, block)], near, sem)
    pl.when(crossing)(fetch.start)

    audio_t = jnp.concatenate([r[...] for r in audio], axis=0)
    inv = lax.rsqrt(jnp.sum(audio_t * audio_t, axis=0, keepdims=True) + EPS)
    inv_ref[...] = inv
    unit_t = audio_t * inv

    @pl.when(step == 0)
    def _():
        for load in loads[:2]:
            load.wait()

    def similar(k):
        part = split(unit_t[:, k * sub : (k + 1) * sub], 0, False)
        return scale * product((v_high[...], v_small[...]), part, ((1,), (0,)))

    def judge(k, scaled):
        power = jnp.exp(scaled + bias)
        sig = power * inverse(1.0 + power)
        paired = (
            lax.broadcasted_iota(jnp.int32, (n, sub), 0)
            - lax.broadcasted_iota(jnp.int32, (n, sub), 1)
        ) == offset + k * sub
        loss = jnp.sum(soft(power), axis=0, keepdims=True)
        return paired, split(jnp.where(paired, 0.0, sig), 0, False), loss

    def pull_rows(k, away, loss):
        lanes = slice(k * sub, (k + 1) * sub)
        grad_a = product((t_high[...], t_small[...]), away, ((1,), (0,)))
        inner = jnp.sum(grad_a * unit_t[:, lanes], axis=0, keepdims=True)
        for p, ref in enumerate(grads_a):
            ref[0:256, lanes] = grad_a[256 * p : 256 * p + 256, :]
            ref[256:257, lanes] = loss
            ref[257:258, lanes] = inner
            ref[258:264, lanes] = jnp.zeros((6, sub), F32)

    scores = [similar(k) for k in range(SUBS)]
    judged = [judge(0, scores[0])]

    @pl.when(step == 0)
    def _():
        for load in loads[2:]:
            load.wait()

    for k in range(SUBS):
        if k > 0:
            judged.append(judge(k, scores[k]))
        pull_rows(k, judged[k][1], judged[k][2])
    high = jnp.concatenate([j[1][0] for j in judged], axis=1)
    small = jnp.concatenate([j[1][1][:n] for j in judged] + [j[1][1][n:] for j in judged], axis=1)
    state[...] += product(split(unit_t, 1, True), (high, small), ((1,), (1,)))

    @pl.when(crossing)
    def _():
        own = jnp.concatenate(
            [jnp.sum(jnp.where(j[0], s, 0.0), axis=0, keepdims=True) for j, s in zip(judged, scores)],
            axis=1,
        )
        value = own + bias
        diag = -1.0 / (1.0 + jnp.exp(value))
        fetch.wait()
        pull = near[...] * diag
        inner_own = jnp.sum(pull * unit_t, axis=0, keepdims=True)
        for k, ref in enumerate(grads_a):
            ref[0:256, :] += pull[256 * k : 256 * k + 256, :]
            ref[256:257, :] += -value
            ref[257:258, :] += inner_own
        state[:, pl.ds(at, block)] += unit_t * diag

    if last:

        @pl.when(step == pl.num_programs(0) - 1)
        def _():
            core, y, x = place[0], place[1], place[2]
            for half in range(n // block):
                lanes = pl.ds(half * block, block)
                copy = pltpu.make_async_copy(unit_t_hbm.at[:, lanes], near, sem)
                copy.start()
                copy.wait()
                row = jnp.sum(near[...] * state[:, lanes], axis=0, keepdims=True)
                for owner in range(8):
                    whole[owner, 128:129, lanes] = row
            for owner in range(8):
                whole[owner, 129:136, :] = jnp.zeros((7, n), F32)
                for part in range(2):
                    dy = lax.rem(y + 4 - owner // 2, 4)
                    dx = lax.rem(x + 4 - 2 * (owner % 2) - part, 4)
                    at = jnp.where(core == 0, 4 * dy + dx, 4 * dx + dy) * 64
                    rows = pl.ds(pl.multiple_of(at, 64), 64)
                    whole[owner, 64 * part : 64 * part + 64, :] = state[rows, :]


def pairs(audio, ahead, video, place, scalars, before, last):
    rows = audio[0].shape[1]
    first = before is None
    n = video[1].shape[0]
    smem = pl.BlockSpec(memory_space=pltpu.SMEM)
    still = lambda shape: pl.BlockSpec(shape, lambda i: (0, 0), pipeline_mode=pl.Buffered(1))
    moving = lambda height: pl.BlockSpec((height, BLOCK), lambda i: (0, i))
    shape = jax.ShapeDtypeStruct
    anywhere = pl.BlockSpec(memory_space=pl.ANY)
    in_specs = [smem, smem] + [moving(a.shape[0]) for a in audio] + [anywhere] * (len(ahead) + 5)
    operands = [place, scalars, *audio, *ahead, *video]
    out_specs = [moving(264)] * 4 + [moving(1)]
    out_shape = [shape((264, rows), F32)] * 4 + [shape((1, rows), F32)]
    scratch = [pltpu.VMEM((1024, BLOCK), F32)] + [pltpu.VMEM(v.shape, v.dtype) for v in video[1:]]
    scratch += [pltpu.SemaphoreType.DMA, pltpu.SemaphoreType.DMA((5,))]
    if not first:
        in_specs.append(anywhere)
        operands.append(before)
    if last:
        out_specs.append(pl.BlockSpec((8, 136, n), lambda i: (0, 0, 0), pipeline_mode=pl.Buffered(1)))
        out_shape.append(shape((8, 136, n), F32))
        scratch = [pltpu.VMEM((1024, n), F32)] + scratch
    else:
        out_specs.append(still((1024, n)))
        out_shape.append(shape((1024, n), F32))

    def body(*refs):
        pairs_kernel(first, last, len(audio), len(ahead), refs)

    return pl.pallas_call(
        body,
        grid=(rows // BLOCK,),
        in_specs=in_specs,
        out_specs=out_specs,
        out_shape=out_shape,
        scratch_shapes=scratch,
        compiler_params=pltpu.CompilerParams(vmem_limit_bytes=VMEM),
        cost_estimate=pl.CostEstimate(
            flops=6 * 2 * rows * n * 1024, bytes_accessed=24 * MIB, transcendentals=3 * rows * n
        ),
        name="pairs_last" if last else "pairs_first" if first else "pairs_next",
    )(*operands)


def perm(inner, k):
    pairs_of = []
    for core in range(2):
        for y in range(4):
            for x in range(4):
                along_x = (core == 0) == inner
                to = (core, y, (x + k) % 4) if along_x else (core, (y + k) % 4, x)
                pairs_of.append((16 * core + 4 * y + x, 16 * to[0] + 4 * to[1] + to[2]))
    return pairs_of


def move(block, inner, k):
    return lax.ppermute(block, PLANE, perm(inner, k))


def after(arrays, late):
    spec = pl.BlockSpec(memory_space=pl.ANY)
    return pl.pallas_call(
        lambda *refs: None,
        in_specs=[spec] * (len(arrays) + len(late)),
        out_specs=[spec] * len(late),
        out_shape=[jax.ShapeDtypeStruct(a.shape, a.dtype) for a in late],
        input_output_aliases={len(arrays) + i: i for i in range(len(late))},
        name="after",
    )(*arrays, *late)


def local(audio, video, scale, bias):
    z, core, y, x = (lax.axis_index(a) for a in ("z", "core", "y", "x"))
    n = video.shape[0]
    audio_t = audio.T
    rows = audio_t.shape[1]
    scalars = jnp.stack([scale, bias])
    base = (2 * z + core) * rows - (4 * y + x) * n

    whole_video = lax.all_gather(video, ("z", "core"), axis=1, tiled=True)
    row = [audio_t] + [move(audio_t, True, k) for k in (1, 2, 3)]
    gathered, early, starts, start = [], [], [], 0
    for part in CHUNKS:
        block = jnp.concatenate([r[:, start : start + part] for r in row], axis=0)
        below, above = move(block, False, 1), move(block, False, 3)
        if start + part < rows:
            far = [move(below[:128], False, 1), move(above[128:], False, 3)]
        else:
            far = [move(block, False, 2)]
        gathered.append([block, below, *far, above])
        early.append([below, above] if start + part < rows else [block])
        starts.append(start)
        start += part
    place = jnp.stack([core, y, x]).astype(jnp.int32)
    inv_v, *parts = prepare(whole_video, place)
    state = None
    invs, halves = [], []
    for c, blocks in enumerate(gathered):
        at = jnp.stack([core, y, x, base + starts[c]]).astype(jnp.int32)
        last = c == len(CHUNKS) - 1
        ahead = early[c + 1] if c + 1 < len(CHUNKS) else []
        outs = pairs(blocks, ahead, parts, at, scalars, state, last)
        grads, inv, state = outs[:4], outs[4], outs[5]
        invs.append(inv)
        if c > 0:
            seen = came[0][256:264] + came[1][256:264] + came[2][256:264]
            *others, state = after([seen], [*grads[1:], state])
            grads = [grads[0], *others]
            halves.append(kept + came[0] + came[1] + came[2])
        kept = grads[0]
        came = [move(grads[k], False, 4 - k) for k in (1, 2, 3)]
    halves.append(kept + came[0] + came[1] + came[2])

    total_v = lax.psum_scatter(state.reshape(1088, n), ("z", "core"), scatter_dimension=0, tiled=True)
    to = [
        jnp.concatenate(
            [jnp.concatenate([h[64 * k : 64 * k + 64], h[256:264]], axis=0) for h in halves], axis=1
        )
        for k in range(4)
    ]
    total_a = to[0]
    for k in (1, 2, 3):
        total_a = total_a + move(to[k], True, 4 - k)
    inv_a = jnp.concatenate(invs, axis=1)
    row_loss, inner_a = total_a[64], total_a[65:66]
    grad_a = scale * (total_a[0:64] * inv_a - audio_t * (inv_a * inv_a * inner_a))
    grad_v = scale * (total_v[0:128] * inv_v - video.T * (inv_v * inv_v * total_v[128:129]))
    return row_loss, grad_a.T, grad_v.T


def solution(mesh):
    fine = Mesh(mesh.devices.reshape(4, 2, 4, 4), ("z", "core", "y", "x"))
    aud, vid = ("z", "core"), ("y", "x")
    return jax.shard_map(
        local,
        mesh=fine,
        in_specs=(P(aud, vid), P(vid, aud), P(), P()),
        out_specs=(P(aud), P(aud, vid), P(vid, aud)),
        check_vma=False,
    )
```

```python
import jax
import jax.numpy as jnp
from jax import lax
from jax.experimental import pallas as pl
from jax.experimental.pallas import tpu as pltpu
from jax.sharding import Mesh, PartitionSpec as P

F32 = jnp.float32
BF16 = jnp.bfloat16
F8 = jnp.float8_e4m3fn
UP_VALUE = 2.0**8
UP_REST = 2.0**17
DOWN = 2.0**-25
EPS = 1e-06
CHUNKS = (1024, 1024)
BLOCK = 512
SUBS = 2
VMEM = 56 * 2**20
PLANE = ("core", "y", "x")
MIB = 2**20
ROWS = [[4 * i + j for j in range(4)] for i in range(4)]
COLUMNS = [[16 + 4 * j + i for j in range(4)] for i in range(4)]
INNER = ROWS + COLUMNS


def dot(a, b, dims):
    return lax.dot_general(a, b, (dims, ((), ())), preferred_element_type=F32)


def split(x, axis, value_first):
    high = x.astype(BF16)
    rest = ((x - high.astype(F32)) * UP_REST).astype(F8)
    value = (x * UP_VALUE).astype(F8)
    pair = (value, rest) if value_first else (rest, value)
    return high, jnp.concatenate(pair, axis=axis)


def product(a, b, dims):
    return dot(a[0], b[0], dims) + DOWN * dot(a[1], b[1], dims)


def prepare_kernel(place, whole, inv_ref, unit_t_out, v_high_out, v_small_out, t_high_out, t_small_out, *scratch):
    flipped, unit_t_ref, v_high, v_small, t_high, t_small, sems = scratch
    core, y, x = place[0], place[1], place[2]
    n = whole.shape[0]
    outs = (unit_t_out, t_high_out, t_small_out, v_high_out, v_small_out)
    copies = [
        pltpu.make_async_copy(ref, out, sems.at[k])
        for k, (ref, out) in enumerate(zip((unit_t_ref, t_high, t_small, v_high, v_small), outs))
    ]
    v_t = whole[...].T
    inv = lax.rsqrt(jnp.sum(v_t * v_t, axis=0, keepdims=True) + EPS)
    inv_ref[...] = inv
    flipped[...] = (v_t * inv).reshape(16, 64, n)
    for outer in range(4):
        for inner in range(4):
            row = lax.rem(y + 4 - jnp.where(core == 0, outer, inner), 4)
            column = lax.rem(x + 4 - jnp.where(core == 0, inner, outer), 4)
            at = 64 * (4 * outer + inner)
            unit_t_ref[at : at + 64, :] = flipped[4 * row + column]
    copies[0].start()
    unit_t = unit_t_ref[...]
    t_high[...], t_small[...] = split(unit_t, 1, True)
    copies[1].start()
    copies[2].start()
    v_high[...], v_small[...] = split(unit_t.T, 1, True)
    copies[3].start()
    copies[4].start()
    for copy in copies:
        copy.wait()


def prepare(video, place):
    n = video.shape[0]
    whole = pl.BlockSpec(memory_space=pltpu.VMEM)
    shape = jax.ShapeDtypeStruct
    parts = [
        shape((1024, n), F32),
        shape((n, 1024), BF16),
        shape((n, 2048), F8),
        shape((1024, n), BF16),
        shape((1024, 2 * n), F8),
    ]
    return pl.pallas_call(
        prepare_kernel,
        in_specs=[pl.BlockSpec(memory_space=pltpu.SMEM), whole],
        out_specs=[whole] + [pl.BlockSpec(memory_space=pl.ANY)] * 5,
        out_shape=[shape((1, n), F32)] + parts,
        scratch_shapes=[pltpu.VMEM((16, 64, n), F32)]
        + [pltpu.VMEM(p.shape, p.dtype) for p in parts]
        + [pltpu.SemaphoreType.DMA((5,))],
        compiler_params=pltpu.CompilerParams(vmem_limit_bytes=VMEM),
        cost_estimate=pl.CostEstimate(flops=0, bytes_accessed=16 * MIB, transcendentals=0),
        name="video_parts",
    )(place, video)


def inverse(d):
    r = pl.reciprocal(d, approx=True)
    return r * (2.0 - d * r)


def soft(power):
    return jnp.where(power < 1e-3, power - 0.5 * power * power, jnp.log(1.0 + power))


def pairs_kernel(first, last, count, skipped, refs):
    place, scalars, *refs = refs
    audio, refs = refs[:count], refs[count + skipped :]
    unit_t_hbm, *sources = refs[:5]
    sources.append(unit_t_hbm)
    refs = refs[5:]
    before = None
    if not first:
        before, *refs = refs
    grads_a, inv_ref, refs = refs[:4], refs[4], refs[5:]
    if last:
        whole, *refs = refs
    state, near, v_high, v_small, t_high, t_small, sems = refs
    step = pl.program_id(0)
    scale, bias = scalars[0], scalars[1]
    n = v_high.shape[0]
    block = inv_ref.shape[1]
    sub = block // SUBS
    offset = place[3] + step * block
    loads = [
        pltpu.make_async_copy(source, to, sems.at[k])
        for k, (source, to) in enumerate(zip(sources, (v_high, v_small, t_high, t_small, near)))
    ]
    if not first:
        loads.append(pltpu.make_async_copy(before, state, sems.at[5]))

    @pl.when(step == 0)
    def _():
        for load in loads:
            load.start()
        if first:
            state[...] = jnp.zeros_like(state)

    audio_t = jnp.concatenate([r[...] for r in audio], axis=0)
    inv = lax.rsqrt(jnp.sum(audio_t * audio_t, axis=0, keepdims=True) + EPS)
    inv_ref[...] = inv
    unit_t = audio_t * inv

    @pl.when(step == 0)
    def _():
        for load in loads[:2]:
            load.wait()

    def similar(k):
        part = split(unit_t[:, k * sub : (k + 1) * sub], 0, False)
        return scale * product((v_high[...], v_small[...]), part, ((1,), (0,)))

    def judge(k, scaled):
        power = jnp.exp(scaled + bias)
        sig = power * inverse(1.0 + power)
        paired = (
            lax.broadcasted_iota(jnp.int32, (n, sub), 0)
            - lax.broadcasted_iota(jnp.int32, (n, sub), 1)
        ) == offset + k * sub
        loss = jnp.sum(soft(power), axis=0, keepdims=True)
        return paired, split(jnp.where(paired, 0.0, sig), 0, False), loss

    def pull_rows(k, away, loss):
        lanes = slice(k * sub, (k + 1) * sub)
        grad_a = product((t_high[...], t_small[...]), away, ((1,), (0,)))
        inner = jnp.sum(grad_a * unit_t[:, lanes], axis=0, keepdims=True)
        for p, ref in enumerate(grads_a):
            ref[0:256, lanes] = grad_a[256 * p : 256 * p + 256, :]
            ref[256:257, lanes] = loss
            ref[257:258, lanes] = inner
            ref[258:264, lanes] = jnp.zeros((6, sub), F32)

    scores = [similar(k) for k in range(SUBS)]
    judged = [judge(0, scores[0])]

    @pl.when(step == 0)
    def _():
        for load in loads[2:]:
            load.wait()

    for k in range(SUBS):
        if k > 0:
            judged.append(judge(k, scores[k]))
        pull_rows(k, judged[k][1], judged[k][2])
    high = jnp.concatenate([j[1][0] for j in judged], axis=1)
    small = jnp.concatenate([j[1][1][:n] for j in judged] + [j[1][1][n:] for j in judged], axis=1)
    state[...] += product(split(unit_t, 1, True), (high, small), ((1,), (1,)))

    @pl.when((offset >= 0) & (offset < n))
    def _():
        at = pl.multiple_of(offset, block)
        own = jnp.concatenate(
            [jnp.sum(jnp.where(j[0], s, 0.0), axis=0, keepdims=True) for j, s in zip(judged, scores)],
            axis=1,
        )
        value = own + bias
        diag = -1.0 / (1.0 + jnp.exp(value))
        pull = near[:, pl.ds(at, block)] * diag
        inner_own = jnp.sum(pull * unit_t, axis=0, keepdims=True)
        for k, ref in enumerate(grads_a):
            ref[0:256, :] += pull[256 * k : 256 * k + 256, :]
            ref[256:257, :] += -value
            ref[257:258, :] += inner_own
        state[:, pl.ds(at, block)] += unit_t * diag

    if last:

        @pl.when(step == pl.num_programs(0) - 1)
        def _():
            core, y, x = place[0], place[1], place[2]
            for half in range(n // block):
                lanes = pl.ds(half * block, block)
                row = jnp.sum(near[:, lanes] * state[:, lanes], axis=0, keepdims=True)
                for owner in range(8):
                    whole[owner, 128:129, lanes] = row
            for owner in range(8):
                whole[owner, 129:136, :] = jnp.zeros((7, n), F32)
                for part in range(2):
                    dy = lax.rem(y + 4 - owner // 2, 4)
                    dx = lax.rem(x + 4 - 2 * (owner % 2) - part, 4)
                    at = jnp.where(core == 0, 4 * dy + dx, 4 * dx + dy) * 64
                    rows = pl.ds(pl.multiple_of(at, 64), 64)
                    whole[owner, 64 * part : 64 * part + 64, :] = state[rows, :]


def pairs(audio, ahead, video, place, scalars, before, last):
    rows = audio[0].shape[1]
    first = before is None
    n = video[1].shape[0]
    smem = pl.BlockSpec(memory_space=pltpu.SMEM)
    still = lambda shape: pl.BlockSpec(shape, lambda i: (0, 0), pipeline_mode=pl.Buffered(1))
    moving = lambda height: pl.BlockSpec((height, BLOCK), lambda i: (0, i))
    shape = jax.ShapeDtypeStruct
    anywhere = pl.BlockSpec(memory_space=pl.ANY)
    in_specs = [smem, smem] + [moving(a.shape[0]) for a in audio] + [anywhere] * (len(ahead) + 5)
    operands = [place, scalars, *audio, *ahead, *video]
    out_specs = [moving(264)] * 4 + [moving(1)]
    out_shape = [shape((264, rows), F32)] * 4 + [shape((1, rows), F32)]
    scratch = [pltpu.VMEM((1024, n), F32)] + [pltpu.VMEM(v.shape, v.dtype) for v in video[1:]]
    scratch.append(pltpu.SemaphoreType.DMA((6,)))
    if not first:
        in_specs.append(anywhere)
        operands.append(before)
    if last:
        out_specs.append(pl.BlockSpec((8, 136, n), lambda i: (0, 0, 0), pipeline_mode=pl.Buffered(1)))
        out_shape.append(shape((8, 136, n), F32))
        scratch = [pltpu.VMEM((1024, n), F32)] + scratch
    else:
        out_specs.append(still((1024, n)))
        out_shape.append(shape((1024, n), F32))

    def body(*refs):
        pairs_kernel(first, last, len(audio), len(ahead), refs)

    return pl.pallas_call(
        body,
        grid=(rows // BLOCK,),
        in_specs=in_specs,
        out_specs=out_specs,
        out_shape=out_shape,
        scratch_shapes=scratch,
        compiler_params=pltpu.CompilerParams(vmem_limit_bytes=VMEM),
        cost_estimate=pl.CostEstimate(
            flops=6 * 2 * rows * n * 1024, bytes_accessed=24 * MIB, transcendentals=3 * rows * n
        ),
        name="pairs_last" if last else "pairs_first" if first else "pairs_next",
    )(*operands)


def perm(inner, k):
    pairs_of = []
    for core in range(2):
        for y in range(4):
            for x in range(4):
                along_x = (core == 0) == inner
                to = (core, y, (x + k) % 4) if along_x else (core, (y + k) % 4, x)
                pairs_of.append((16 * core + 4 * y + x, 16 * to[0] + 4 * to[1] + to[2]))
    return pairs_of


def move(block, inner, k):
    return lax.ppermute(block, PLANE, perm(inner, k))


def after(arrays, late):
    spec = pl.BlockSpec(memory_space=pl.ANY)
    return pl.pallas_call(
        lambda *refs: None,
        in_specs=[spec] * (len(arrays) + len(late)),
        out_specs=[spec] * len(late),
        out_shape=[jax.ShapeDtypeStruct(a.shape, a.dtype) for a in late],
        input_output_aliases={len(arrays) + i: i for i in range(len(late))},
        name="after",
    )(*arrays, *late)


def local(audio, video, scale, bias):
    z, core, y, x = (lax.axis_index(a) for a in ("z", "core", "y", "x"))
    n = video.shape[0]
    audio_t = audio.T
    rows = audio_t.shape[1]
    scalars = jnp.stack([scale, bias])
    base = (2 * z + core) * rows - (4 * y + x) * n

    whole_video = lax.all_gather(video, ("z", "core"), axis=1, tiled=True)
    row = [audio_t] + [move(audio_t, True, k) for k in (1, 2, 3)]
    gathered, early, starts, start = [], [], [], 0
    for part in CHUNKS:
        block = jnp.concatenate([r[:, start : start + part] for r in row], axis=0)
        if start > 0:
            (block,) = after([below[:8] + above[:8]], [block])
        below, above = move(block, False, 1), move(block, False, 3)
        if start + part < rows:
            far = [move(below[:128], False, 1), move(above[128:], False, 3)]
        else:
            far = [move(block, False, 2)]
        gathered.append([block, below, *far, above])
        early.append([below, above] if start + part < rows else [block])
        starts.append(start)
        start += part
    place = jnp.stack([core, y, x]).astype(jnp.int32)
    inv_v, *parts = prepare(whole_video, place)
    state = None
    invs, halves = [], []
    for c, blocks in enumerate(gathered):
        at = jnp.stack([core, y, x, base + starts[c]]).astype(jnp.int32)
        last = c == len(CHUNKS) - 1
        ahead = early[c + 1] if c + 1 < len(CHUNKS) else []
        outs = pairs(blocks, ahead, parts, at, scalars, state, last)
        grads, inv, state = outs[:4], outs[4], outs[5]
        invs.append(inv)
        if c > 0:
            seen = came[0][256:264] + came[1][256:264] + came[2][256:264]
            *others, state = after([seen], [*grads[1:], state])
            grads = [grads[0], *others]
            halves.append(kept + came[0] + came[1] + came[2])
        kept = grads[0]
        came = [move(grads[k], False, 4 - k) for k in (1, 2, 3)]
    halves.append(kept + came[0] + came[1] + came[2])

    total_v = lax.psum_scatter(state.reshape(1088, n), ("z", "core"), scatter_dimension=0, tiled=True)
    place_in = jnp.where(core == 0, x, y)
    done = []
    for c, h in enumerate(halves):
        to = [jnp.concatenate([h[64 * k : 64 * k + 64], h[256:264]], axis=0) for k in range(4)]
        if c < len(CHUNKS) - 1:
            ring = jnp.stack([to[0], to[3], to[2], to[1], to[0], to[3], to[2]])
            ring = lax.dynamic_slice_in_dim(ring, lax.rem(4 - place_in, 4), 4, 0)
            done.append(jnp.sum(lax.all_to_all(ring, PLANE, 0, 0, axis_index_groups=INNER), axis=0))
        else:
            done.append(to[0] + sum(move(to[k], True, 4 - k) for k in (1, 2, 3)))
    total_a = jnp.concatenate(done, axis=1)
    inv_a = jnp.concatenate(invs, axis=1)
    row_loss, inner_a = total_a[64], total_a[65:66]
    grad_a = scale * (total_a[0:64] * inv_a - audio_t * (inv_a * inv_a * inner_a))
    grad_v = scale * (total_v[0:128] * inv_v - video.T * (inv_v * inv_v * total_v[128:129]))
    return row_loss, grad_a.T, grad_v.T


def solution(mesh):
    fine = Mesh(mesh.devices.reshape(4, 2, 4, 4), ("z", "core", "y", "x"))
    aud, vid = ("z", "core"), ("y", "x")
    return jax.shard_map(
        local,
        mesh=fine,
        in_specs=(P(aud, vid), P(vid, aud), P(), P()),
        out_specs=(P(aud), P(aud, vid), P(vid, aud)),
        check_vma=False,
    )
```

```python
import jax
import jax.numpy as jnp
from jax import lax
from jax.experimental import pallas as pl
from jax.experimental.pallas import tpu as pltpu
from jax.sharding import Mesh, PartitionSpec as P

F32 = jnp.float32
BF16 = jnp.bfloat16
F8 = jnp.float8_e4m3fn
UP_VALUE = 2.0**8
UP_REST = 2.0**17
DOWN = 2.0**-25
EPS = 1e-06
CHUNKS = (1024, 1024)
BLOCK = 512
SUBS = 2
VMEM = 56 * 2**20
PLANE = ("core", "y", "x")
MIB = 2**20
ROWS = [[4 * i + j for j in range(4)] for i in range(4)]
COLUMNS = [[16 + 4 * j + i for j in range(4)] for i in range(4)]
INNER = ROWS + COLUMNS


def dot(a, b, dims):
    return lax.dot_general(a, b, (dims, ((), ())), preferred_element_type=F32)


def split(x, axis, value_first):
    high = x.astype(BF16)
    rest = ((x - high.astype(F32)) * UP_REST).astype(F8)
    value = (x * UP_VALUE).astype(F8)
    pair = (value, rest) if value_first else (rest, value)
    return high, jnp.concatenate(pair, axis=axis)


def product(a, b, dims):
    return dot(a[0], b[0], dims) + DOWN * dot(a[1], b[1], dims)


def prepare_kernel(place, own_ref, other_ref, inv_ref, unit_t_out, v_high_out, v_small_out, t_high_out, t_small_out, *scratch):
    whole, flipped, unit_t_ref, v_high, v_small, t_high, t_small, sems = scratch
    core, y, x = place[0], place[1], place[2]
    n = whole.shape[0]
    outs = (unit_t_out, t_high_out, t_small_out, v_high_out, v_small_out)
    copies = [
        pltpu.make_async_copy(ref, out, sems.at[k])
        for k, (ref, out) in enumerate(zip((unit_t_ref, t_high, t_small, v_high, v_small), outs))
    ]
    for k, ref in enumerate((own_ref, other_ref)):
        side = jnp.where(k == 0, core, 1 - core)
        for row in range(4):
            whole[:, pl.ds(pl.multiple_of(256 * row + 128 * side, 128), 128)] = ref[row]
    v_t = whole[...].T
    inv = lax.rsqrt(jnp.sum(v_t * v_t, axis=0, keepdims=True) + EPS)
    inv_ref[...] = inv
    flipped[...] = (v_t * inv).reshape(16, 64, n)
    for outer in range(4):
        for inner in range(4):
            row = lax.rem(y + 4 - jnp.where(core == 0, outer, inner), 4)
            column = lax.rem(x + 4 - jnp.where(core == 0, inner, outer), 4)
            at = 64 * (4 * outer + inner)
            unit_t_ref[at : at + 64, :] = flipped[4 * row + column]
    copies[0].start()
    unit_t = unit_t_ref[...]
    t_high[...], t_small[...] = split(unit_t, 1, True)
    copies[1].start()
    copies[2].start()
    v_high[...], v_small[...] = split(unit_t.T, 1, True)
    copies[3].start()
    copies[4].start()
    for copy in copies:
        copy.wait()


def prepare(own, other, place):
    n = own.shape[1]
    whole = pl.BlockSpec(memory_space=pltpu.VMEM)
    shape = jax.ShapeDtypeStruct
    parts = [
        shape((1024, n), F32),
        shape((n, 1024), BF16),
        shape((n, 2048), F8),
        shape((1024, n), BF16),
        shape((1024, 2 * n), F8),
    ]
    return pl.pallas_call(
        prepare_kernel,
        in_specs=[pl.BlockSpec(memory_space=pltpu.SMEM), whole, whole],
        out_specs=[whole] + [pl.BlockSpec(memory_space=pl.ANY)] * 5,
        out_shape=[shape((1, n), F32)] + parts,
        scratch_shapes=[pltpu.VMEM((n, 1024), F32), pltpu.VMEM((16, 64, n), F32)]
        + [pltpu.VMEM(p.shape, p.dtype) for p in parts]
        + [pltpu.SemaphoreType.DMA((5,))],
        compiler_params=pltpu.CompilerParams(vmem_limit_bytes=VMEM),
        cost_estimate=pl.CostEstimate(flops=0, bytes_accessed=16 * MIB, transcendentals=0),
        name="video_parts",
    )(place, own, other)


def inverse(d):
    r = pl.reciprocal(d, approx=True)
    return r * (2.0 - d * r)


def soft(power):
    return jnp.where(power < 1e-3, power - 0.5 * power * power, jnp.log(1.0 + power))


def pairs_kernel(first, last, count, skipped, refs):
    place, scalars, *refs = refs
    audio, refs = refs[:count], refs[count + skipped :]
    unit_t_hbm, *sources = refs[:5]
    sources.append(unit_t_hbm)
    refs = refs[5:]
    before = None
    if not first:
        before, *refs = refs
    grads_a, inv_ref, refs = refs[:4], refs[4], refs[5:]
    if last:
        whole, *refs = refs
    state, near, v_high, v_small, t_high, t_small, sems = refs
    step = pl.program_id(0)
    scale, bias = scalars[0], scalars[1]
    n = v_high.shape[0]
    block = inv_ref.shape[1]
    sub = block // SUBS
    offset = place[3] + step * block
    loads = [
        pltpu.make_async_copy(source, to, sems.at[k])
        for k, (source, to) in enumerate(zip(sources, (v_high, v_small, t_high, t_small, near)))
    ]
    if not first:
        loads.append(pltpu.make_async_copy(before, state, sems.at[5]))

    @pl.when(step == 0)
    def _():
        for load in loads:
            load.start()
        if first:
            state[...] = jnp.zeros_like(state)

    audio_t = jnp.concatenate([r[...] for r in audio], axis=0)
    inv = lax.rsqrt(jnp.sum(audio_t * audio_t, axis=0, keepdims=True) + EPS)
    inv_ref[...] = inv
    unit_t = audio_t * inv

    @pl.when(step == 0)
    def _():
        for load in loads[:2]:
            load.wait()

    def similar(k):
        part = split(unit_t[:, k * sub : (k + 1) * sub], 0, False)
        return scale * product((v_high[...], v_small[...]), part, ((1,), (0,)))

    def judge(k, scaled):
        power = jnp.exp(scaled + bias)
        sig = power * inverse(1.0 + power)
        paired = (
            lax.broadcasted_iota(jnp.int32, (n, sub), 0)
            - lax.broadcasted_iota(jnp.int32, (n, sub), 1)
        ) == offset + k * sub
        loss = jnp.sum(soft(power), axis=0, keepdims=True)
        return paired, split(jnp.where(paired, 0.0, sig), 0, False), loss

    def pull_rows(k, away, loss):
        lanes = slice(k * sub, (k + 1) * sub)
        grad_a = product((t_high[...], t_small[...]), away, ((1,), (0,)))
        inner = jnp.sum(grad_a * unit_t[:, lanes], axis=0, keepdims=True)
        for p, ref in enumerate(grads_a):
            ref[0:256, lanes] = grad_a[256 * p : 256 * p + 256, :]
            ref[256:257, lanes] = loss
            ref[257:258, lanes] = inner
            ref[258:264, lanes] = jnp.zeros((6, sub), F32)

    scores = [similar(k) for k in range(SUBS)]
    judged = [judge(0, scores[0])]

    @pl.when(step == 0)
    def _():
        for load in loads[2:]:
            load.wait()

    for k in range(SUBS):
        if k > 0:
            judged.append(judge(k, scores[k]))
        pull_rows(k, judged[k][1], judged[k][2])
    high = jnp.concatenate([j[1][0] for j in judged], axis=1)
    small = jnp.concatenate([j[1][1][:n] for j in judged] + [j[1][1][n:] for j in judged], axis=1)
    state[...] += product(split(unit_t, 1, True), (high, small), ((1,), (1,)))

    @pl.when((offset >= 0) & (offset < n))
    def _():
        at = pl.multiple_of(offset, block)
        own = jnp.concatenate(
            [jnp.sum(jnp.where(j[0], s, 0.0), axis=0, keepdims=True) for j, s in zip(judged, scores)],
            axis=1,
        )
        value = own + bias
        diag = -1.0 / (1.0 + jnp.exp(value))
        pull = near[:, pl.ds(at, block)] * diag
        inner_own = jnp.sum(pull * unit_t, axis=0, keepdims=True)
        for k, ref in enumerate(grads_a):
            ref[0:256, :] += pull[256 * k : 256 * k + 256, :]
            ref[256:257, :] += -value
            ref[257:258, :] += inner_own
        state[:, pl.ds(at, block)] += unit_t * diag

    if last:

        @pl.when(step == pl.num_programs(0) - 1)
        def _():
            core, y, x = place[0], place[1], place[2]
            for half in range(n // block):
                lanes = pl.ds(half * block, block)
                row = jnp.sum(near[:, lanes] * state[:, lanes], axis=0, keepdims=True)
                for owner in range(8):
                    whole[owner, 128:129, lanes] = row
            for owner in range(8):
                whole[owner, 129:136, :] = jnp.zeros((7, n), F32)
                for part in range(2):
                    dy = lax.rem(y + 4 - owner // 2, 4)
                    dx = lax.rem(x + 4 - 2 * (owner % 2) - part, 4)
                    at = jnp.where(core == 0, 4 * dy + dx, 4 * dx + dy) * 64
                    rows = pl.ds(pl.multiple_of(at, 64), 64)
                    whole[owner, 64 * part : 64 * part + 64, :] = state[rows, :]


def pairs(audio, ahead, video, place, scalars, before, last):
    rows = audio[0].shape[1]
    first = before is None
    n = video[1].shape[0]
    smem = pl.BlockSpec(memory_space=pltpu.SMEM)
    still = lambda shape: pl.BlockSpec(shape, lambda i: (0, 0), pipeline_mode=pl.Buffered(1))
    moving = lambda height: pl.BlockSpec((height, BLOCK), lambda i: (0, i))
    shape = jax.ShapeDtypeStruct
    anywhere = pl.BlockSpec(memory_space=pl.ANY)
    in_specs = [smem, smem] + [moving(a.shape[0]) for a in audio] + [anywhere] * (len(ahead) + 5)
    operands = [place, scalars, *audio, *ahead, *video]
    out_specs = [moving(264)] * 4 + [moving(1)]
    out_shape = [shape((264, rows), F32)] * 4 + [shape((1, rows), F32)]
    scratch = [pltpu.VMEM((1024, n), F32)] + [pltpu.VMEM(v.shape, v.dtype) for v in video[1:]]
    scratch.append(pltpu.SemaphoreType.DMA((6,)))
    if not first:
        in_specs.append(anywhere)
        operands.append(before)
    if last:
        out_specs.append(pl.BlockSpec((8, 136, n), lambda i: (0, 0, 0), pipeline_mode=pl.Buffered(1)))
        out_shape.append(shape((8, 136, n), F32))
        scratch = [pltpu.VMEM((1024, n), F32)] + scratch
    else:
        out_specs.append(still((1024, n)))
        out_shape.append(shape((1024, n), F32))

    def body(*refs):
        pairs_kernel(first, last, len(audio), len(ahead), refs)

    return pl.pallas_call(
        body,
        grid=(rows // BLOCK,),
        in_specs=in_specs,
        out_specs=out_specs,
        out_shape=out_shape,
        scratch_shapes=scratch,
        compiler_params=pltpu.CompilerParams(vmem_limit_bytes=VMEM),
        cost_estimate=pl.CostEstimate(
            flops=6 * 2 * rows * n * 1024, bytes_accessed=24 * MIB, transcendentals=3 * rows * n
        ),
        name="pairs_last" if last else "pairs_first" if first else "pairs_next",
    )(*operands)


def perm(inner, k):
    pairs_of = []
    for core in range(2):
        for y in range(4):
            for x in range(4):
                along_x = (core == 0) == inner
                to = (core, y, (x + k) % 4) if along_x else (core, (y + k) % 4, x)
                pairs_of.append((16 * core + 4 * y + x, 16 * to[0] + 4 * to[1] + to[2]))
    return pairs_of


def move(block, inner, k):
    return lax.ppermute(block, PLANE, perm(inner, k))


def after(arrays, late):
    spec = pl.BlockSpec(memory_space=pl.ANY)
    return pl.pallas_call(
        lambda *refs: None,
        in_specs=[spec] * (len(arrays) + len(late)),
        out_specs=[spec] * len(late),
        out_shape=[jax.ShapeDtypeStruct(a.shape, a.dtype) for a in late],
        input_output_aliases={len(arrays) + i: i for i in range(len(late))},
        name="after",
    )(*arrays, *late)


def local(audio, video, scale, bias):
    z, core, y, x = (lax.axis_index(a) for a in ("z", "core", "y", "x"))
    n = video.shape[0]
    audio_t = audio.T
    rows = audio_t.shape[1]
    scalars = jnp.stack([scale, bias])
    base = (2 * z + core) * rows - (4 * y + x) * n

    own = lax.all_gather(video, "z", axis=0)
    other = lax.ppermute(own, "core", [(0, 1), (1, 0)])
    row = [audio_t] + [move(audio_t, True, k) for k in (1, 2, 3)]
    gathered, early, starts, start = [], [], [], 0
    for part in CHUNKS:
        block = jnp.concatenate([r[:, start : start + part] for r in row], axis=0)
        if start > 0:
            (block,) = after([below[:8] + above[:8]], [block])
        below, above = move(block, False, 1), move(block, False, 3)
        if start + part < rows:
            far = [move(below[:128], False, 1), move(above[128:], False, 3)]
        else:
            far = [move(block, False, 2)]
        gathered.append([block, below, *far, above])
        early.append([below, above] if start + part < rows else [block])
        starts.append(start)
        start += part
    place = jnp.stack([core, y, x]).astype(jnp.int32)
    inv_v, *parts = prepare(own, other, place)
    state = None
    invs, halves = [], []
    for c, blocks in enumerate(gathered):
        at = jnp.stack([core, y, x, base + starts[c]]).astype(jnp.int32)
        last = c == len(CHUNKS) - 1
        ahead = early[c + 1] if c + 1 < len(CHUNKS) else []
        outs = pairs(blocks, ahead, parts, at, scalars, state, last)
        grads, inv, state = outs[:4], outs[4], outs[5]
        invs.append(inv)
        if c > 0:
            seen = came[0][256:264] + came[1][256:264] + came[2][256:264]
            *others, state = after([seen], [*grads[1:], state])
            grads = [grads[0], *others]
            halves.append(kept + came[0] + came[1] + came[2])
        kept = grads[0]
        if not last:
            came = [move(grads[k], False, 4 - k) for k in (1, 2, 3)]
    top, bottom = move(grads[2][:128], False, 3), move(grads[2][128:], False, 1)
    below = jnp.concatenate([grads[1][:128] + top, grads[1][128:]], axis=0)
    above = jnp.concatenate([grads[3][:128], grads[3][128:] + bottom], axis=0)
    halves.append(kept + move(below, False, 3) + move(above, False, 1))

    total_v = lax.psum_scatter(state.reshape(1088, n), ("z", "core"), scatter_dimension=0, tiled=True)
    place_in = jnp.where(core == 0, x, y)
    done = []
    for c, h in enumerate(halves):
        to = [jnp.concatenate([h[64 * k : 64 * k + 64], h[256:264]], axis=0) for k in range(4)]
        if c < len(CHUNKS) - 1:
            ring = jnp.stack([to[0], to[3], to[2], to[1], to[0], to[3], to[2]])
            ring = lax.dynamic_slice_in_dim(ring, lax.rem(4 - place_in, 4), 4, 0)
            done.append(jnp.sum(lax.all_to_all(ring, PLANE, 0, 0, axis_index_groups=INNER), axis=0))
        else:
            done.append(to[0] + sum(move(to[k], True, 4 - k) for k in (1, 2, 3)))
    total_a = jnp.concatenate(done, axis=1)
    inv_a = jnp.concatenate(invs, axis=1)
    row_loss, inner_a = total_a[64], total_a[65:66]
    grad_a = scale * (total_a[0:64] * inv_a - audio_t * (inv_a * inv_a * inner_a))
    grad_v = scale * (total_v[0:128] * inv_v - video.T * (inv_v * inv_v * total_v[128:129]))
    return row_loss, grad_a.T, grad_v.T


def solution(mesh):
    fine = Mesh(mesh.devices.reshape(4, 2, 4, 4), ("z", "core", "y", "x"))
    aud, vid = ("z", "core"), ("y", "x")
    return jax.shard_map(
        local,
        mesh=fine,
        in_specs=(P(aud, vid), P(vid, aud), P(), P()),
        out_specs=(P(aud), P(aud, vid), P(vid, aud)),
        check_vma=False,
    )
```

```python
import jax
import jax.numpy as jnp
from jax import lax
from jax.experimental import pallas as pl
from jax.experimental.pallas import tpu as pltpu
from jax.sharding import Mesh, PartitionSpec as P

F32 = jnp.float32
BF16 = jnp.bfloat16
F8 = jnp.float8_e4m3fn
UP_VALUE = 2.0**8
UP_REST = 2.0**17
DOWN = 2.0**-25
EPS = 1e-06
CHUNKS = (1024, 1024)
BLOCK = 512
SUBS = 2
VMEM = 56 * 2**20
PLANE = ("core", "y", "x")
MIB = 2**20


def dot(a, b, dims):
    return lax.dot_general(a, b, (dims, ((), ())), preferred_element_type=F32)


def split(x, axis, value_first):
    high = x.astype(BF16)
    rest = ((x - high.astype(F32)) * UP_REST).astype(F8)
    value = (x * UP_VALUE).astype(F8)
    pair = (value, rest) if value_first else (rest, value)
    return high, jnp.concatenate(pair, axis=axis)


def product(a, b, dims):
    return dot(a[0], b[0], dims) + DOWN * dot(a[1], b[1], dims)


def prepare_kernel(place, own_ref, other_ref, inv_ref, unit_t_out, v_high_out, v_small_out, t_high_out, t_small_out, *scratch):
    whole, flipped, unit_t_ref, v_high, v_small, t_high, t_small, sems = scratch
    core, y, x, z = place[0], place[1], place[2], place[3]
    n = whole.shape[0]
    outs = (unit_t_out, t_high_out, t_small_out, v_high_out, v_small_out)
    copies = [
        pltpu.make_async_copy(ref, out, sems.at[k])
        for k, (ref, out) in enumerate(zip((unit_t_ref, t_high, t_small, v_high, v_small), outs))
    ]
    for k, ref in enumerate((own_ref, other_ref)):
        side = jnp.where(k == 0, core, 1 - core)
        for hops in range(4):
            at = 256 * lax.rem(z + 4 - hops, 4) + 128 * side
            whole[:, pl.ds(pl.multiple_of(at, 128), 128)] = ref[hops]
    v_t = whole[...].T
    inv = lax.rsqrt(jnp.sum(v_t * v_t, axis=0, keepdims=True) + EPS)
    inv_ref[...] = inv
    flipped[...] = (v_t * inv).reshape(16, 64, n)
    for outer in range(4):
        for inner in range(4):
            row = lax.rem(y + 4 - jnp.where(core == 0, outer, inner), 4)
            column = lax.rem(x + 4 - jnp.where(core == 0, inner, outer), 4)
            at = 64 * (4 * outer + inner)
            unit_t_ref[at : at + 64, :] = flipped[4 * row + column]
    copies[0].start()
    unit_t = unit_t_ref[...]
    t_high[...], t_small[...] = split(unit_t, 1, True)
    copies[1].start()
    copies[2].start()
    v_high[...], v_small[...] = split(unit_t.T, 1, True)
    copies[3].start()
    copies[4].start()
    for copy in copies:
        copy.wait()


def prepare(own, other, place):
    n = own.shape[1]
    whole = pl.BlockSpec(memory_space=pltpu.VMEM)
    shape = jax.ShapeDtypeStruct
    parts = [
        shape((1024, n), F32),
        shape((n, 1024), BF16),
        shape((n, 2048), F8),
        shape((1024, n), BF16),
        shape((1024, 2 * n), F8),
    ]
    return pl.pallas_call(
        prepare_kernel,
        in_specs=[pl.BlockSpec(memory_space=pltpu.SMEM), whole, whole],
        out_specs=[whole] + [pl.BlockSpec(memory_space=pl.ANY)] * 5,
        out_shape=[shape((1, n), F32)] + parts,
        scratch_shapes=[pltpu.VMEM((n, 1024), F32), pltpu.VMEM((16, 64, n), F32)]
        + [pltpu.VMEM(p.shape, p.dtype) for p in parts]
        + [pltpu.SemaphoreType.DMA((5,))],
        compiler_params=pltpu.CompilerParams(vmem_limit_bytes=VMEM),
        cost_estimate=pl.CostEstimate(flops=0, bytes_accessed=16 * MIB, transcendentals=0),
        name="video_parts",
    )(place, own, other)


def inverse(d):
    r = pl.reciprocal(d, approx=True)
    return r * (2.0 - d * r)


def soft(power):
    return jnp.where(power < 1e-3, power - 0.5 * power * power, jnp.log(1.0 + power))


def pairs_kernel(first, last, count, skipped, refs):
    place, scalars, *refs = refs
    audio, refs = refs[:count], refs[count + skipped :]
    unit_t_hbm, *sources = refs[:5]
    sources.append(unit_t_hbm)
    refs = refs[5:]
    before = None
    if not first:
        before, *refs = refs
    grads_a, inv_ref, refs = refs[:4], refs[4], refs[5:]
    if last:
        mine, theirs, *refs = refs
    state, near, v_high, v_small, t_high, t_small, sems = refs
    step = pl.program_id(0)
    scale, bias = scalars[0], scalars[1]
    n = v_high.shape[0]
    block = inv_ref.shape[1]
    sub = block // SUBS
    offset = place[3] + step * block
    loads = [
        pltpu.make_async_copy(source, to, sems.at[k])
        for k, (source, to) in enumerate(zip(sources, (v_high, v_small, t_high, t_small, near)))
    ]
    if not first:
        loads.append(pltpu.make_async_copy(before, state, sems.at[5]))

    @pl.when(step == 0)
    def _():
        for load in loads:
            load.start()
        if first:
            state[...] = jnp.zeros_like(state)

    audio_t = jnp.concatenate([r[...] for r in audio], axis=0)
    inv = lax.rsqrt(jnp.sum(audio_t * audio_t, axis=0, keepdims=True) + EPS)
    inv_ref[...] = inv
    unit_t = audio_t * inv

    @pl.when(step == 0)
    def _():
        for load in loads[:2]:
            load.wait()

    def similar(k):
        part = split(unit_t[:, k * sub : (k + 1) * sub], 0, False)
        return scale * product((v_high[...], v_small[...]), part, ((1,), (0,)))

    def judge(k, scaled):
        power = jnp.exp(scaled + bias)
        sig = power * inverse(1.0 + power)
        paired = (
            lax.broadcasted_iota(jnp.int32, (n, sub), 0)
            - lax.broadcasted_iota(jnp.int32, (n, sub), 1)
        ) == offset + k * sub
        loss = jnp.sum(soft(power), axis=0, keepdims=True)
        return paired, split(jnp.where(paired, 0.0, sig), 0, False), loss

    def pull_rows(k, away, loss):
        lanes = slice(k * sub, (k + 1) * sub)
        grad_a = product((t_high[...], t_small[...]), away, ((1,), (0,)))
        inner = jnp.sum(grad_a * unit_t[:, lanes], axis=0, keepdims=True)
        for p, ref in enumerate(grads_a):
            ref[0:256, lanes] = grad_a[256 * p : 256 * p + 256, :]
            ref[256:257, lanes] = loss
            ref[257:258, lanes] = inner
            ref[258:264, lanes] = jnp.zeros((6, sub), F32)

    scores = [similar(k) for k in range(SUBS)]
    judged = [judge(0, scores[0])]

    @pl.when(step == 0)
    def _():
        for load in loads[2:]:
            load.wait()

    for k in range(SUBS):
        if k > 0:
            judged.append(judge(k, scores[k]))
        pull_rows(k, judged[k][1], judged[k][2])
    high = jnp.concatenate([j[1][0] for j in judged], axis=1)
    small = jnp.concatenate([j[1][1][:n] for j in judged] + [j[1][1][n:] for j in judged], axis=1)
    state[...] += product(split(unit_t, 1, True), (high, small), ((1,), (1,)))

    @pl.when((offset >= 0) & (offset < n))
    def _():
        at = pl.multiple_of(offset, block)
        own = jnp.concatenate(
            [jnp.sum(jnp.where(j[0], s, 0.0), axis=0, keepdims=True) for j, s in zip(judged, scores)],
            axis=1,
        )
        value = own + bias
        diag = -1.0 / (1.0 + jnp.exp(value))
        pull = near[:, pl.ds(at, block)] * diag
        inner_own = jnp.sum(pull * unit_t, axis=0, keepdims=True)
        for k, ref in enumerate(grads_a):
            ref[0:256, :] += pull[256 * k : 256 * k + 256, :]
            ref[256:257, :] += -value
            ref[257:258, :] += inner_own
        state[:, pl.ds(at, block)] += unit_t * diag

    if last:

        @pl.when(step == pl.num_programs(0) - 1)
        def _():
            core, y, x, z = place[0], place[1], place[2], place[4]
            for half in range(n // block):
                lanes = pl.ds(half * block, block)
                row = jnp.sum(near[:, lanes] * state[:, lanes], axis=0, keepdims=True)
                for ref in (mine, theirs):
                    for owner in range(4):
                        ref[owner, 128:129, lanes] = row
            for k, ref in enumerate((mine, theirs)):
                side = jnp.where(k == 0, core, 1 - core)
                for owner in range(4):
                    ref[owner, 129:136, :] = jnp.zeros((7, n), F32)
                    dy = lax.rem(y + 8 - z - owner, 4)
                    for part in range(2):
                        dx = lax.rem(x + 4 - 2 * side - part, 4)
                        at = jnp.where(core == 0, 4 * dy + dx, 4 * dx + dy) * 64
                        rows = pl.ds(pl.multiple_of(at, 64), 64)
                        ref[owner, 64 * part : 64 * part + 64, :] = state[rows, :]


def pairs(audio, ahead, video, place, scalars, before, last):
    rows = audio[0].shape[1]
    first = before is None
    n = video[1].shape[0]
    smem = pl.BlockSpec(memory_space=pltpu.SMEM)
    still = lambda shape: pl.BlockSpec(shape, lambda i: (0, 0), pipeline_mode=pl.Buffered(1))
    moving = lambda height: pl.BlockSpec((height, BLOCK), lambda i: (0, i))
    shape = jax.ShapeDtypeStruct
    anywhere = pl.BlockSpec(memory_space=pl.ANY)
    in_specs = [smem, smem] + [moving(a.shape[0]) for a in audio] + [anywhere] * (len(ahead) + 5)
    operands = [place, scalars, *audio, *ahead, *video]
    out_specs = [moving(264)] * 4 + [moving(1)]
    out_shape = [shape((264, rows), F32)] * 4 + [shape((1, rows), F32)]
    scratch = [pltpu.VMEM((1024, n), F32)] + [pltpu.VMEM(v.shape, v.dtype) for v in video[1:]]
    scratch.append(pltpu.SemaphoreType.DMA((6,)))
    if not first:
        in_specs.append(anywhere)
        operands.append(before)
    if last:
        out_specs += [pl.BlockSpec((4, 136, n), lambda i: (0, 0, 0), pipeline_mode=pl.Buffered(1))] * 2
        out_shape += [shape((4, 136, n), F32)] * 2
        scratch = [pltpu.VMEM((1024, n), F32)] + scratch
    else:
        out_specs.append(still((1024, n)))
        out_shape.append(shape((1024, n), F32))

    def body(*refs):
        pairs_kernel(first, last, len(audio), len(ahead), refs)

    return pl.pallas_call(
        body,
        grid=(rows // BLOCK,),
        in_specs=in_specs,
        out_specs=out_specs,
        out_shape=out_shape,
        scratch_shapes=scratch,
        compiler_params=pltpu.CompilerParams(vmem_limit_bytes=VMEM),
        cost_estimate=pl.CostEstimate(
            flops=6 * 2 * rows * n * 1024, bytes_accessed=24 * MIB, transcendentals=3 * rows * n
        ),
        name="pairs_last" if last else "pairs_first" if first else "pairs_next",
    )(*operands)


def perm(inner, k):
    pairs_of = []
    for core in range(2):
        for y in range(4):
            for x in range(4):
                along_x = (core == 0) == inner
                to = (core, y, (x + k) % 4) if along_x else (core, (y + k) % 4, x)
                pairs_of.append((16 * core + 4 * y + x, 16 * to[0] + 4 * to[1] + to[2]))
    return pairs_of


def move(block, inner, k):
    return lax.ppermute(block, PLANE, perm(inner, k))


def hop(block, k):
    return lax.ppermute(block, "z", [(i, (i + k) % 4) for i in range(4)])


def swap(block):
    return lax.ppermute(block, "core", [(0, 1), (1, 0)])


def after(arrays, late):
    spec = pl.BlockSpec(memory_space=pl.ANY)
    return pl.pallas_call(
        lambda *refs: None,
        in_specs=[spec] * (len(arrays) + len(late)),
        out_specs=[spec] * len(late),
        out_shape=[jax.ShapeDtypeStruct(a.shape, a.dtype) for a in late],
        input_output_aliases={len(arrays) + i: i for i in range(len(late))},
        name="after",
    )(*arrays, *late)


def local(audio, video, scale, bias):
    z, core, y, x = (lax.axis_index(a) for a in ("z", "core", "y", "x"))
    n = video.shape[0]
    audio_t = audio.T
    rows = audio_t.shape[1]
    scalars = jnp.stack([scale, bias])
    base = (2 * z + core) * rows - (4 * y + x) * n

    up, down = hop(video, 1), hop(video, 3)
    row = [audio_t] + [move(audio_t, True, k) for k in (1, 2, 3)]
    gathered, starts, start, mid = [], [], 0, n // 2
    for part in CHUNKS:
        block = jnp.concatenate([r[:, start : start + part] for r in row], axis=0)
        if start > 0:
            (block,) = after([seen], [block])
        below, above = move(block, False, 1), move(block, False, 3)
        if start == 0:
            far = [move(below[:128], False, 1), move(above[128:], False, 3)]
            seen = below[:8] + above[:8]
            halves_z = after([block[:8]], [up[:mid], down[mid:]])
            far_z = jnp.concatenate([hop(halves_z[0], 1), hop(halves_z[1], 3)], axis=0)
            own = jnp.stack([video, up, far_z, down])
            (own,) = after([seen], [own])
        else:
            far = [move(block, False, 2)]
        gathered.append([block, below, *far, above])
        starts.append(start)
        start += part
    early = [[g[0]] for g in gathered]
    place = jnp.stack([core, y, x, z]).astype(jnp.int32)
    inv_v, *parts = prepare(own, swap(own), place)
    state = None
    invs, halves = [], []
    for c, blocks in enumerate(gathered):
        at = jnp.stack([core, y, x, base + starts[c], z]).astype(jnp.int32)
        last = c == len(CHUNKS) - 1
        ahead = early[c + 1] if c + 1 < len(CHUNKS) else []
        outs = pairs(blocks, ahead, parts, at, scalars, state, last)
        grads, inv, state = outs[:4], outs[4], outs[5]
        invs.append(inv)
        if c > 0:
            seen = came[0][256:264] + came[1][256:264] + came[2][256:264]
            *others, theirs = after([seen], [*grads[1:], outs[6]])
            grads = [grads[0], *others]
            halves.append(kept + came[0] + came[1] + came[2])
        kept = grads[0]
        came = [move(grads[k], False, 4 - k) for k in (1, 2, 3)]
    halves.append(kept + came[0] + came[1] + came[2])

    half = state + swap(theirs)
    below, above = hop(half[2, :, :mid], 1), hop(half[2, :, mid:], 3)
    (halves[-1],) = after([below[:8] + above[:8]], [halves[-1]])
    to_up = jnp.concatenate([half[1, :, :mid] + below, half[1, :, mid:]], axis=1)
    to_down = jnp.concatenate([half[3, :, :mid], half[3, :, mid:] + above], axis=1)
    total_v = half[0] + hop(to_up, 1) + hop(to_down, 3)
    to = [
        jnp.concatenate(
            [jnp.concatenate([h[64 * k : 64 * k + 64], h[256:264]], axis=0) for h in halves], axis=1
        )
        for k in range(4)
    ]
    total_a = to[0] + sum(move(to[k], True, 4 - k) for k in (1, 2, 3))
    inv_a = jnp.concatenate(invs, axis=1)
    row_loss, inner_a = total_a[64], total_a[65:66]
    grad_a = scale * (total_a[0:64] * inv_a - audio_t * (inv_a * inv_a * inner_a))
    grad_v = scale * (total_v[0:128] * inv_v - video.T * (inv_v * inv_v * total_v[128:129]))
    return row_loss, grad_a.T, grad_v.T


def solution(mesh):
    fine = Mesh(mesh.devices.reshape(4, 2, 4, 4), ("z", "core", "y", "x"))
    aud, vid = ("z", "core"), ("y", "x")
    return jax.shard_map(
        local,
        mesh=fine,
        in_specs=(P(aud, vid), P(vid, aud), P(), P()),
        out_specs=(P(aud), P(aud, vid), P(vid, aud)),
        check_vma=False,
    )
```

```python
import jax
import jax.numpy as jnp
from jax import lax
from jax.experimental import pallas as pl
from jax.experimental.pallas import tpu as pltpu
from jax.sharding import Mesh, PartitionSpec as P

F32 = jnp.float32
BF16 = jnp.bfloat16
F8 = jnp.float8_e4m3fn
UP_VALUE = 2.0**8
UP_REST = 2.0**17
DOWN = 2.0**-25
EPS = 1e-06
BLOCK = 512
SUBS = 2
VMEM = 56 * 2**20
PLANE = ("core", "y", "x")
MIB = 2**20
COLUMNS = [[4 * j + i for j in range(4)] for i in range(4)]
ROWS = [[16 + 4 * i + j for j in range(4)] for i in range(4)]
OUTER = COLUMNS + ROWS


def dot(a, b, dims):
    return lax.dot_general(a, b, (dims, ((), ())), preferred_element_type=F32)


def split(x, axis, value_first):
    high = x.astype(BF16)
    rest = ((x - high.astype(F32)) * UP_REST).astype(F8)
    value = (x * UP_VALUE).astype(F8)
    pair = (value, rest) if value_first else (rest, value)
    return high, jnp.concatenate(pair, axis=axis)


def product(a, b, dims):
    return dot(a[0], b[0], dims) + DOWN * dot(a[1], b[1], dims)


def prepare_kernel(place, whole, inv_ref, unit_t_out, v_high_out, v_small_out, t_high_out, t_small_out, *scratch):
    flipped, unit_t_ref, v_high, v_small, t_high, t_small, sems = scratch
    core, y, x = place[0], place[1], place[2]
    n = whole.shape[0]
    outs = (unit_t_out, t_high_out, t_small_out, v_high_out, v_small_out)
    copies = [
        pltpu.make_async_copy(ref, out, sems.at[k])
        for k, (ref, out) in enumerate(zip((unit_t_ref, t_high, t_small, v_high, v_small), outs))
    ]
    v_t = whole[...].T
    inv = lax.rsqrt(jnp.sum(v_t * v_t, axis=0, keepdims=True) + EPS)
    inv_ref[...] = inv
    flipped[...] = (v_t * inv).reshape(16, 64, n)
    for outer in range(4):
        for inner in range(4):
            row = lax.rem(y + 4 - jnp.where(core == 0, outer, inner), 4)
            column = lax.rem(x + 4 - jnp.where(core == 0, inner, outer), 4)
            at = 64 * (4 * outer + inner)
            unit_t_ref[at : at + 64, :] = flipped[4 * row + column]
    copies[0].start()
    unit_t = unit_t_ref[...]
    t_high[...], t_small[...] = split(unit_t, 1, True)
    copies[1].start()
    copies[2].start()
    v_high[...], v_small[...] = split(unit_t.T, 1, True)
    copies[3].start()
    copies[4].start()
    for copy in copies:
        copy.wait()


def prepare(video, place):
    n = video.shape[0]
    whole = pl.BlockSpec(memory_space=pltpu.VMEM)
    shape = jax.ShapeDtypeStruct
    parts = [
        shape((1024, n), F32),
        shape((n, 1024), BF16),
        shape((n, 2048), F8),
        shape((1024, n), BF16),
        shape((1024, 2 * n), F8),
    ]
    return pl.pallas_call(
        prepare_kernel,
        in_specs=[pl.BlockSpec(memory_space=pltpu.SMEM), whole],
        out_specs=[whole] + [pl.BlockSpec(memory_space=pl.ANY)] * 5,
        out_shape=[shape((1, n), F32)] + parts,
        scratch_shapes=[pltpu.VMEM((16, 64, n), F32)]
        + [pltpu.VMEM(p.shape, p.dtype) for p in parts]
        + [pltpu.SemaphoreType.DMA((5,))],
        compiler_params=pltpu.CompilerParams(vmem_limit_bytes=VMEM),
        cost_estimate=pl.CostEstimate(flops=0, bytes_accessed=16 * MIB, transcendentals=0),
        name="video_parts",
    )(place, video)


def inverse(d):
    r = pl.reciprocal(d, approx=True)
    return r * (2.0 - d * r)


def soft(power):
    return jnp.where(power < 1e-3, power - 0.5 * power * power, jnp.log(1.0 + power))


def pairs_kernel(first, last, refs):
    place, scalars, *refs = refs
    audio, refs = refs[:4], refs[4:]
    unit_t_hbm, *sources = refs[:5]
    sources.append(unit_t_hbm)
    refs = refs[5:]
    before = None
    if not first:
        before, *refs = refs
    if last:
        grads_a, refs = refs[:4], refs[4:]
    else:
        grads_a = [refs[0].at[lax.rem(place[4] + 4 - k, 4)] for k in range(4)]
        refs = refs[1:]
    inv_ref, *refs = refs
    if last:
        whole, *refs = refs
    state, near, v_high, v_small, t_high, t_small, sems = refs
    step = pl.program_id(0)
    scale, bias = scalars[0], scalars[1]
    n = v_high.shape[0]
    block = inv_ref.shape[1]
    sub = block // SUBS
    offset = place[3] + step * block
    loads = [
        pltpu.make_async_copy(source, to, sems.at[k])
        for k, (source, to) in enumerate(zip(sources, (v_high, v_small, t_high, t_small, near)))
    ]
    if not first:
        loads.append(pltpu.make_async_copy(before, state, sems.at[5]))

    @pl.when(step == 0)
    def _():
        for load in loads:
            load.start()
        if first:
            state[...] = jnp.zeros_like(state)

    audio_t = jnp.concatenate([r[...] for r in audio], axis=0)
    inv = lax.rsqrt(jnp.sum(audio_t * audio_t, axis=0, keepdims=True) + EPS)
    inv_ref[...] = inv
    unit_t = audio_t * inv

    @pl.when(step == 0)
    def _():
        for load in loads[:2]:
            load.wait()

    def similar(k):
        part = split(unit_t[:, k * sub : (k + 1) * sub], 0, False)
        return scale * product((v_high[...], v_small[...]), part, ((1,), (0,)))

    def judge(k, scaled):
        power = jnp.exp(scaled + bias)
        sig = power * inverse(1.0 + power)
        paired = (
            lax.broadcasted_iota(jnp.int32, (n, sub), 0)
            - lax.broadcasted_iota(jnp.int32, (n, sub), 1)
        ) == offset + k * sub
        loss = jnp.sum(soft(power), axis=0, keepdims=True)
        return paired, split(jnp.where(paired, 0.0, sig), 0, False), loss

    def pull_rows(k, away, loss):
        lanes = slice(k * sub, (k + 1) * sub)
        grad_a = product((t_high[...], t_small[...]), away, ((1,), (0,)))
        inner = jnp.sum(grad_a * unit_t[:, lanes], axis=0, keepdims=True)
        for p, ref in enumerate(grads_a):
            ref[0:256, lanes] = grad_a[256 * p : 256 * p + 256, :]
            ref[256:257, lanes] = loss
            ref[257:258, lanes] = inner
            ref[258:264, lanes] = jnp.zeros((6, sub), F32)

    scores = [similar(k) for k in range(SUBS)]
    judged = [judge(0, scores[0])]

    @pl.when(step == 0)
    def _():
        for load in loads[2:]:
            load.wait()

    for k in range(SUBS):
        if k > 0:
            judged.append(judge(k, scores[k]))
        pull_rows(k, judged[k][1], judged[k][2])
    high = jnp.concatenate([j[1][0] for j in judged], axis=1)
    small = jnp.concatenate([j[1][1][:n] for j in judged] + [j[1][1][n:] for j in judged], axis=1)
    state[...] += product(split(unit_t, 1, True), (high, small), ((1,), (1,)))

    @pl.when((offset >= 0) & (offset < n))
    def _():
        at = pl.multiple_of(offset, block)
        own = jnp.concatenate(
            [jnp.sum(jnp.where(j[0], s, 0.0), axis=0, keepdims=True) for j, s in zip(judged, scores)],
            axis=1,
        )
        value = own + bias
        diag = -1.0 / (1.0 + jnp.exp(value))
        pull = near[:, pl.ds(at, block)] * diag
        inner_own = jnp.sum(pull * unit_t, axis=0, keepdims=True)
        for k, ref in enumerate(grads_a):
            ref[0:256, :] += pull[256 * k : 256 * k + 256, :]
            ref[256:257, :] += -value
            ref[257:258, :] += inner_own
        state[:, pl.ds(at, block)] += unit_t * diag

    if last:

        @pl.when(step == pl.num_programs(0) - 1)
        def _():
            core, y, x = place[0], place[1], place[2]
            for half in range(n // block):
                lanes = pl.ds(half * block, block)
                row = jnp.sum(near[:, lanes] * state[:, lanes], axis=0, keepdims=True)
                for owner in range(8):
                    whole[owner, 128:129, lanes] = row
            for owner in range(8):
                whole[owner, 129:136, :] = jnp.zeros((7, n), F32)
                for part in range(2):
                    dy = lax.rem(y + 4 - owner // 2, 4)
                    dx = lax.rem(x + 4 - 2 * (owner % 2) - part, 4)
                    at = jnp.where(core == 0, 4 * dy + dx, 4 * dx + dy) * 64
                    rows = pl.ds(pl.multiple_of(at, 64), 64)
                    whole[owner, 64 * part : 64 * part + 64, :] = state[rows, :]


def pairs(audio, video, place, scalars, before, last):
    rows = audio[0].shape[1]
    first = before is None
    n = video[1].shape[0]
    smem = pl.BlockSpec(memory_space=pltpu.SMEM)
    anywhere = pl.BlockSpec(memory_space=pl.ANY)
    shape = jax.ShapeDtypeStruct

    def still(shape):
        return pl.BlockSpec(shape, lambda i, at: (0,) * len(shape), pipeline_mode=pl.Buffered(1))

    def moving(height):
        return pl.BlockSpec((height, BLOCK), lambda i, at: (0, i))

    def turned(k):
        return pl.BlockSpec((256, BLOCK), lambda i, at: (lax.rem(at[4] + 4 - k, 4), i))

    if len(audio) == 1:
        blocks = [turned(k) for k in range(4)]
    else:
        blocks = [moving(256)] * 4
    in_specs = [smem] + blocks + [anywhere] * 5
    operands = [scalars, *(audio * (4 // len(audio))), *video]
    parts = [pltpu.VMEM(v.shape, v.dtype) for v in (video[0], *video[1:])]
    parts.append(pltpu.SemaphoreType.DMA((6,)))
    if not first:
        in_specs.append(anywhere)
        operands.append(before)
    if last:
        out_specs = [moving(264)] * 4 + [moving(1), still((8, 136, n))]
        out_shape = [shape((264, rows), F32)] * 4 + [shape((1, rows), F32), shape((8, 136, n), F32)]
        scratch = [pltpu.VMEM((1024, n), F32)] + parts
    else:
        whole = pl.BlockSpec((4, 264, BLOCK), lambda i, at: (0, 0, i))
        out_specs = [whole, moving(1), still((1024, n))]
        out_shape = [shape((4, 264, rows), F32), shape((1, rows), F32), shape((1024, n), F32)]
        scratch = parts

    def body(*refs):
        pairs_kernel(first, last, refs)

    return pl.pallas_call(
        body,
        grid_spec=pltpu.PrefetchScalarGridSpec(
            num_scalar_prefetch=1,
            grid=(rows // BLOCK,),
            in_specs=in_specs,
            out_specs=out_specs,
            scratch_shapes=scratch,
        ),
        out_shape=out_shape,
        compiler_params=pltpu.CompilerParams(vmem_limit_bytes=VMEM),
        cost_estimate=pl.CostEstimate(
            flops=6 * 2 * rows * n * 1024, bytes_accessed=24 * MIB, transcendentals=3 * rows * n
        ),
        name="pairs_last" if last else "pairs_first",
    )(place, *operands)


def perm(inner, k):
    pairs_of = []
    for core in range(2):
        for y in range(4):
            for x in range(4):
                along_x = (core == 0) == inner
                to = (core, y, (x + k) % 4) if along_x else (core, (y + k) % 4, x)
                pairs_of.append((16 * core + 4 * y + x, 16 * to[0] + 4 * to[1] + to[2]))
    return pairs_of


def move(block, inner, k):
    return lax.ppermute(block, PLANE, perm(inner, k))


def after(arrays, late):
    spec = pl.BlockSpec(memory_space=pl.ANY)
    return pl.pallas_call(
        lambda *refs: None,
        in_specs=[spec] * (len(arrays) + len(late)),
        out_specs=[spec] * len(late),
        out_shape=[jax.ShapeDtypeStruct(a.shape, a.dtype) for a in late],
        input_output_aliases={len(arrays) + i: i for i in range(len(late))},
        name="after",
    )(*arrays, *late)


def local(audio, video, scale, bias):
    z, core, y, x = (lax.axis_index(a) for a in ("z", "core", "y", "x"))
    n = video.shape[0]
    audio_t = audio.T
    rows = audio_t.shape[1]
    scalars = jnp.stack([scale, bias])
    base = (2 * z + core) * rows - (4 * y + x) * n

    whole_video = lax.all_gather(video, ("z", "core"), axis=1, tiled=True)
    row = [audio_t] + [move(audio_t, True, k) for k in (1, 2, 3)]
    part = rows // 2
    near, late = (jnp.concatenate([r[:, c * part : (c + 1) * part] for r in row], axis=0) for c in (0, 1))
    near = [near] + [move(near, False, k) for k in (1, 2, 3)]
    late = [lax.all_gather(late, PLANE, axis=0, tiled=True, axis_index_groups=OUTER)]
    inv_v, *parts = prepare(whole_video, jnp.stack([core, y, x]).astype(jnp.int32))
    outer = jnp.where(core == 0, y, x)
    places = [jnp.stack([core, y, x, base + c * part, outer]).astype(jnp.int32) for c in (0, 1)]
    whole, inv_near, state = pairs(near, parts, places[0], scalars, None, False)
    *grads, inv_late, state = pairs(late, parts, places[1], scalars, state, True)
    whole = whole.reshape(1056, part)
    halves = [
        lax.psum_scatter(whole, PLANE, scatter_dimension=0, tiled=True, axis_index_groups=OUTER),
        grads[0] + sum(move(grads[k], False, 4 - k) for k in (1, 2, 3)),
    ]

    total_v = lax.psum_scatter(state.reshape(1088, n), ("z", "core"), scatter_dimension=0, tiled=True)
    grad_v = scale * (total_v[0:128] * inv_v - video.T * (inv_v * inv_v * total_v[128:129]))
    to = [
        jnp.concatenate(
            [jnp.concatenate([h[64 * k : 64 * k + 64], h[256:264]], axis=0) for h in halves], axis=1
        )
        for k in range(4)
    ]
    (kept,) = after([grad_v[:8]], [to[0]])
    total_a = kept + sum(move(to[k], True, 4 - k) for k in (1, 2, 3))
    inv_a = jnp.concatenate([inv_near, inv_late], axis=1)
    row_loss, inner_a = total_a[64], total_a[65:66]
    grad_a = scale * (total_a[0:64] * inv_a - audio_t * (inv_a * inv_a * inner_a))
    return row_loss, grad_a.T, grad_v.T


def solution(mesh):
    fine = Mesh(mesh.devices.reshape(4, 2, 4, 4), ("z", "core", "y", "x"))
    aud, vid = ("z", "core"), ("y", "x")
    return jax.shard_map(
        local,
        mesh=fine,
        in_specs=(P(aud, vid), P(vid, aud), P(), P()),
        out_specs=(P(aud), P(aud, vid), P(vid, aud)),
        check_vma=False,
    )
```

```python
import jax
import jax.numpy as jnp
from jax import lax
from jax.experimental import pallas as pl
from jax.experimental.pallas import tpu as pltpu
from jax.sharding import Mesh, PartitionSpec as P

F32 = jnp.float32
BF16 = jnp.bfloat16
F8 = jnp.float8_e4m3fn
UP_VALUE = 2.0**8
UP_REST = 2.0**17
DOWN = 2.0**-25
EPS = 1e-06
BLOCK = 512
SUBS = 2
VMEM = 56 * 2**20
PLANE = ("core", "y", "x")
MIB = 2**20
COLUMNS = [[4 * j + i for j in range(4)] for i in range(4)]
ROWS = [[16 + 4 * i + j for j in range(4)] for i in range(4)]
OUTER = COLUMNS + ROWS


def dot(a, b, dims):
    return lax.dot_general(a, b, (dims, ((), ())), preferred_element_type=F32)


def split(x, axis, value_first):
    high = x.astype(BF16)
    rest = ((x - high.astype(F32)) * UP_REST).astype(F8)
    value = (x * UP_VALUE).astype(F8)
    pair = (value, rest) if value_first else (rest, value)
    return high, jnp.concatenate(pair, axis=axis)


def product(a, b, dims):
    return dot(a[0], b[0], dims) + DOWN * dot(a[1], b[1], dims)


def prepare_kernel(place, whole, inv_ref, unit_t_out, v_high_out, v_small_out, t_high_out, t_small_out, *scratch):
    flipped, unit_t_ref, v_high, v_small, t_high, t_small, sems = scratch
    core, y, x = place[0], place[1], place[2]
    n = whole.shape[0]
    outs = (unit_t_out, t_high_out, t_small_out, v_high_out, v_small_out)
    copies = [
        pltpu.make_async_copy(ref, out, sems.at[k])
        for k, (ref, out) in enumerate(zip((unit_t_ref, t_high, t_small, v_high, v_small), outs))
    ]
    v_t = whole[...].T
    inv = lax.rsqrt(jnp.sum(v_t * v_t, axis=0, keepdims=True) + EPS)
    inv_ref[...] = inv
    flipped[...] = (v_t * inv).reshape(16, 64, n)
    for outer in range(4):
        for inner in range(4):
            row = lax.rem(y + 4 - jnp.where(core == 0, outer, inner), 4)
            column = lax.rem(x + 4 - jnp.where(core == 0, inner, outer), 4)
            at = 64 * (4 * outer + inner)
            unit_t_ref[at : at + 64, :] = flipped[4 * row + column]
    copies[0].start()
    unit_t = unit_t_ref[...]
    t_high[...], t_small[...] = split(unit_t, 1, True)
    copies[1].start()
    copies[2].start()
    v_high[...], v_small[...] = split(unit_t.T, 1, True)
    copies[3].start()
    copies[4].start()
    for copy in copies:
        copy.wait()


def prepare(video, place):
    n = video.shape[0]
    whole = pl.BlockSpec(memory_space=pltpu.VMEM)
    shape = jax.ShapeDtypeStruct
    parts = [
        shape((1024, n), F32),
        shape((n, 1024), BF16),
        shape((n, 2048), F8),
        shape((1024, n), BF16),
        shape((1024, 2 * n), F8),
    ]
    return pl.pallas_call(
        prepare_kernel,
        in_specs=[pl.BlockSpec(memory_space=pltpu.SMEM), whole],
        out_specs=[whole] + [pl.BlockSpec(memory_space=pl.ANY)] * 5,
        out_shape=[shape((1, n), F32)] + parts,
        scratch_shapes=[pltpu.VMEM((16, 64, n), F32)]
        + [pltpu.VMEM(p.shape, p.dtype) for p in parts]
        + [pltpu.SemaphoreType.DMA((5,))],
        compiler_params=pltpu.CompilerParams(vmem_limit_bytes=VMEM),
        cost_estimate=pl.CostEstimate(flops=0, bytes_accessed=16 * MIB, transcendentals=0),
        name="video_parts",
    )(place, video)


def inverse(d):
    r = pl.reciprocal(d, approx=True)
    return r * (2.0 - d * r)


def soft(power):
    return jnp.where(power < 1e-3, power - 0.5 * power * power, jnp.log(1.0 + power))


def pairs_kernel(first, refs):
    place, scalars, *refs = refs
    audio, refs = refs[:4], refs[4:]
    sources, refs = refs[:5], refs[5 if first else 9 :]
    if first:
        grads_a = [refs[0].at[lax.rem(place[4] + 4 - k, 4)] for k in range(4)]
        refs = refs[1:]
    else:
        grads_a, refs = refs[:4], refs[4:]
    side_ref, unit_high, unit_small, away_high, away_small, *refs = refs
    near, v_high, v_small, t_high, t_small, sems = refs
    step = pl.program_id(0)
    scale, bias = scalars[0], scalars[1]
    n = v_high.shape[0]
    block = side_ref.shape[1]
    sub = block // SUBS
    offset = place[3] + step * block
    loads = [
        pltpu.make_async_copy(source, to, sems.at[k])
        for k, (source, to) in enumerate(zip(sources, (near, v_high, v_small, t_high, t_small)))
    ]

    @pl.when(step == 0)
    def _():
        for load in (*loads[1:], loads[0]):
            load.start()

    audio_t = jnp.concatenate([r[...] for r in audio], axis=0)
    inv = lax.rsqrt(jnp.sum(audio_t * audio_t, axis=0, keepdims=True) + EPS)
    side_ref[0:1, :] = inv
    side_ref[1:8, :] = jnp.zeros((7, block), F32)
    unit_t = audio_t * inv

    @pl.when(step == 0)
    def _():
        for load in loads[1:3]:
            load.wait()

    def similar(k):
        lanes = slice(k * sub, (k + 1) * sub)
        part = split(unit_t[:, lanes], 0, False)
        unit_high[:, lanes], unit_small[:, lanes] = part
        return scale * product((v_high[...], v_small[...]), part, ((1,), (0,)))

    def judge(k, scaled):
        lanes = slice(k * sub, (k + 1) * sub)
        power = jnp.exp(scaled + bias)
        sig = power * inverse(1.0 + power)
        paired = (
            lax.broadcasted_iota(jnp.int32, (n, sub), 0)
            - lax.broadcasted_iota(jnp.int32, (n, sub), 1)
        ) == offset + k * sub
        away = split(jnp.where(paired, 0.0, sig), 0, False)
        away_high[:, lanes], away_small[:, lanes] = away
        return paired, away, jnp.sum(soft(power), axis=0, keepdims=True)

    def pull_rows(k, away, loss):
        lanes = slice(k * sub, (k + 1) * sub)
        grad_a = product((t_high[...], t_small[...]), away, ((1,), (0,)))
        inner = jnp.sum(grad_a * unit_t[:, lanes], axis=0, keepdims=True)
        for p, ref in enumerate(grads_a):
            ref[0:256, lanes] = grad_a[256 * p : 256 * p + 256, :]
            ref[256:257, lanes] = loss
            ref[257:258, lanes] = inner
            ref[258:264, lanes] = jnp.zeros((6, sub), F32)

    scores = [similar(k) for k in range(SUBS)]
    judged = [judge(0, scores[0])]

    @pl.when(step == 0)
    def _():
        for load in (*loads[3:], loads[0]):
            load.wait()

    for k in range(SUBS):
        if k > 0:
            judged.append(judge(k, scores[k]))
        pull_rows(k, judged[k][1], judged[k][2])

    @pl.when((offset >= 0) & (offset < n))
    def _():
        at = pl.multiple_of(offset, block)
        own = jnp.concatenate(
            [jnp.sum(jnp.where(j[0], s, 0.0), axis=0, keepdims=True) for j, s in zip(judged, scores)],
            axis=1,
        )
        value = own + bias
        diag = -1.0 / (1.0 + jnp.exp(value))
        side_ref[1:2, :] = diag
        pull = near[:, pl.ds(at, block)] * diag
        inner_own = jnp.sum(pull * unit_t, axis=0, keepdims=True)
        for k, ref in enumerate(grads_a):
            ref[0:256, :] += pull[256 * k : 256 * k + 256, :]
            ref[256:257, :] += -value
            ref[257:258, :] += inner_own


def pairs(audio, video, place, scalars, before):
    rows = audio[0].shape[1]
    first = before is None
    n = video[1].shape[0]
    smem = pl.BlockSpec(memory_space=pltpu.SMEM)
    anywhere = pl.BlockSpec(memory_space=pl.ANY)
    shape = jax.ShapeDtypeStruct
    skip = 0 if first else rows // BLOCK

    def moving(height):
        return pl.BlockSpec((height, BLOCK), lambda i, at: (0, i))

    def shared(height):
        return pl.BlockSpec((height, BLOCK), lambda i, at: (0, i + skip))

    def turned(k):
        return pl.BlockSpec((256, BLOCK), lambda i, at: (lax.rem(at[4] + 4 - k, 4), i))

    if len(audio) == 1:
        blocks = [turned(k) for k in range(4)]
    else:
        blocks = [moving(256)] * 4
    in_specs = [smem] + blocks + [anywhere] * 5
    operands = [scalars, *(audio * (4 // len(audio))), *video]
    if first:
        out_specs = [pl.BlockSpec((4, 264, BLOCK), lambda i, at: (0, 0, i))]
        out_shape = [shape((4, 264, rows), F32)]
        aliases = {}
    else:
        aliases = {1 + len(operands) + k: 5 + k for k in range(4)}
        in_specs += [anywhere] * 4
        operands += before
        out_specs = [moving(264)] * 4
        out_shape = [shape((264, rows), F32)] * 4
    out_specs += [moving(8), shared(1024), shared(2048), shared(n), shared(2 * n)]
    out_shape += [
        shape((8, rows), F32),
        shape((1024, 2 * rows), BF16),
        shape((2048, 2 * rows), F8),
        shape((n, 2 * rows), BF16),
        shape((2 * n, 2 * rows), F8),
    ]

    def body(*refs):
        pairs_kernel(first, refs)

    return pl.pallas_call(
        body,
        grid_spec=pltpu.PrefetchScalarGridSpec(
            num_scalar_prefetch=1,
            grid=(rows // BLOCK,),
            in_specs=in_specs,
            out_specs=out_specs,
            scratch_shapes=[pltpu.VMEM(v.shape, v.dtype) for v in video] + [pltpu.SemaphoreType.DMA((5,))],
        ),
        out_shape=out_shape,
        input_output_aliases=aliases,
        compiler_params=pltpu.CompilerParams(vmem_limit_bytes=VMEM),
        cost_estimate=pl.CostEstimate(
            flops=4 * 2 * rows * n * 1024, bytes_accessed=32 * MIB, transcendentals=3 * rows * n
        ),
        name="pairs_first" if first else "pairs_last",
    )(place, *operands)


def video_kernel(place, unit_high, unit_small, away_high, away_small, near_side, late_side, *refs):
    early, (late, unit_t_hbm, whole), refs = refs[:4], refs[4:7], refs[7:]
    state, unit_t, rows_ref, sems = refs
    step = pl.program_id(0)
    n = away_high.shape[0]
    block = near_side.shape[1]
    half = pl.num_programs(0) // 2
    offset = place[3] + step * block
    crossing = (offset >= 0) & (offset < n)
    load = pltpu.make_async_copy(unit_t_hbm, unit_t, sems.at[4])
    from_early, from_late = [], []
    for k in range(4):
        to = rows_ref.at[pl.ds(256 * k, 256), :]
        lanes = pl.ds(pl.multiple_of(lax.rem(step, half) * block, block), block)
        turn = pl.multiple_of(lax.rem(place[4] + 4 - k, 4) * 256, 256)
        from_early.append(pltpu.make_async_copy(early[k].at[:, lanes], to, sems.at[k]))
        from_late.append(pltpu.make_async_copy(late.at[pl.ds(turn, 256), lanes], to, sems.at[k]))

    @pl.when(step == 0)
    def _():
        load.start()
        state[...] = jnp.zeros_like(state)

    @pl.when(crossing & (step < half))
    def _():
        for copy in from_early:
            copy.start()

    @pl.when(crossing & (step >= half))
    def _():
        for copy in from_late:
            copy.start()

    dims = ((1,), (1,))
    small = dot(unit_small[1024:], away_small[:n], dims) + dot(unit_small[:1024], away_small[n:], dims)
    state[...] += dot(unit_high[...], away_high[...], dims) + DOWN * small

    @pl.when(crossing)
    def _():
        for copy in from_early:
            copy.wait()
        side = jnp.where(step < half, near_side[0:2, :], late_side[0:2, :])
        at = pl.multiple_of(offset, block)
        state[:, pl.ds(at, block)] += rows_ref[...] * (side[0:1, :] * side[1:2, :])

    @pl.when(step == pl.num_programs(0) - 1)
    def _():
        load.wait()
        core, y, x = place[0], place[1], place[2]
        row = jnp.sum(unit_t[...] * state[...], axis=0, keepdims=True)
        for owner in range(8):
            whole[owner, 128:129, :] = row
            whole[owner, 129:136, :] = jnp.zeros((7, n), F32)
            for part in range(2):
                dy = lax.rem(y + 4 - owner // 2, 4)
                dx = lax.rem(x + 4 - 2 * (owner % 2) - part, 4)
                at = jnp.where(core == 0, 4 * dy + dx, 4 * dx + dy) * 64
                piece = pl.ds(pl.multiple_of(at, 64), 64)
                whole[owner, 64 * part : 64 * part + 64, :] = state[piece, :]


def video_sums(shared, sides, early, late, unit_t, place):
    n = shared[2].shape[0]
    count = shared[0].shape[1] // BLOCK
    anywhere = pl.BlockSpec(memory_space=pl.ANY)
    moving = lambda height: pl.BlockSpec((height, BLOCK), lambda i, at: (0, i))
    first = pl.BlockSpec((8, BLOCK), lambda i, at: (0, jnp.minimum(i, count // 2 - 1)))
    second = pl.BlockSpec((8, BLOCK), lambda i, at: (0, jnp.maximum(i - count // 2, 0)))
    return pl.pallas_call(
        video_kernel,
        grid_spec=pltpu.PrefetchScalarGridSpec(
            num_scalar_prefetch=1,
            grid=(count,),
            in_specs=[moving(s.shape[0]) for s in shared] + [first, second] + [anywhere] * 6,
            out_specs=pl.BlockSpec((8, 136, n), lambda i, at: (0, 0, 0), pipeline_mode=pl.Buffered(1)),
            scratch_shapes=[
                pltpu.VMEM((1024, n), F32),
                pltpu.VMEM((1024, n), F32),
                pltpu.VMEM((1024, BLOCK), F32),
                pltpu.SemaphoreType.DMA((5,)),
            ],
        ),
        out_shape=jax.ShapeDtypeStruct((8, 136, n), F32),
        compiler_params=pltpu.CompilerParams(vmem_limit_bytes=VMEM),
        cost_estimate=pl.CostEstimate(
            flops=2 * 2 * BLOCK * count * n * 1024, bytes_accessed=32 * MIB, transcendentals=0
        ),
        name="video_sums",
    )(place, *shared, *sides, *early, late, unit_t)


def perm(inner, k):
    pairs_of = []
    for core in range(2):
        for y in range(4):
            for x in range(4):
                along_x = (core == 0) == inner
                to = (core, y, (x + k) % 4) if along_x else (core, (y + k) % 4, x)
                pairs_of.append((16 * core + 4 * y + x, 16 * to[0] + 4 * to[1] + to[2]))
    return pairs_of


def move(block, inner, k):
    return lax.ppermute(block, PLANE, perm(inner, k))


def after(arrays, late):
    spec = pl.BlockSpec(memory_space=pl.ANY)
    return pl.pallas_call(
        lambda *refs: None,
        in_specs=[spec] * (len(arrays) + len(late)),
        out_specs=[spec] * len(late),
        out_shape=[jax.ShapeDtypeStruct(a.shape, a.dtype) for a in late],
        input_output_aliases={len(arrays) + i: i for i in range(len(late))},
        name="after",
    )(*arrays, *late)


def local(audio, video, scale, bias):
    z, core, y, x = (lax.axis_index(a) for a in ("z", "core", "y", "x"))
    n = video.shape[0]
    audio_t = audio.T
    rows = audio_t.shape[1]
    scalars = jnp.stack([scale, bias])
    base = (2 * z + core) * rows - (4 * y + x) * n

    whole_video = lax.all_gather(video, ("z", "core"), axis=1, tiled=True)
    row = [audio_t] + [move(audio_t, True, k) for k in (1, 2, 3)]
    part = rows // 2
    near, late = (jnp.concatenate([r[:, c * part : (c + 1) * part] for r in row], axis=0) for c in (0, 1))
    near = [near] + [move(near, False, k) for k in (1, 2, 3)]
    late = [lax.all_gather(late, PLANE, axis=0, tiled=True, axis_index_groups=OUTER)]
    inv_v, *parts = prepare(whole_video, jnp.stack([core, y, x]).astype(jnp.int32))
    outer = jnp.where(core == 0, y, x)
    places = [jnp.stack([core, y, x, base + c * part, outer]).astype(jnp.int32) for c in (0, 1)]
    whole, side_near, *shared = pairs(near, parts, places[0], scalars, None)
    *grads, side_late = (outs := pairs(late, parts, places[1], scalars, shared))[:5]
    state = video_sums(outs[5:], [side_near, side_late], near, late[0], parts[0], places[0])
    whole = whole.reshape(1056, part)
    came = [move(grads[k], False, 4 - k) for k in (1, 2, 3)]
    halves = [
        lax.psum_scatter(whole, PLANE, scatter_dimension=0, tiled=True, axis_index_groups=OUTER),
        grads[0] + came[0] + came[1] + came[2],
    ]
    (state,) = after([came[0][256:264] + came[2][256:264]], [state])

    total_v = lax.psum_scatter(state.reshape(1088, n), ("z", "core"), scatter_dimension=0, tiled=True)
    grad_v = scale * (total_v[0:128] * inv_v - video.T * (inv_v * inv_v * total_v[128:129]))
    to = [
        jnp.concatenate(
            [jnp.concatenate([h[64 * k : 64 * k + 64], h[256:264]], axis=0) for h in halves], axis=1
        )
        for k in range(4)
    ]
    (kept,) = after([grad_v[:8]], [to[0]])
    total_a = kept + sum(move(to[k], True, 4 - k) for k in (1, 2, 3))
    inv_a = jnp.concatenate([side_near[0:1], side_late[0:1]], axis=1)
    row_loss, inner_a = total_a[64], total_a[65:66]
    grad_a = scale * (total_a[0:64] * inv_a - audio_t * (inv_a * inv_a * inner_a))
    return row_loss, grad_a.T, grad_v.T


def solution(mesh):
    fine = Mesh(mesh.devices.reshape(4, 2, 4, 4), ("z", "core", "y", "x"))
    aud, vid = ("z", "core"), ("y", "x")
    return jax.shard_map(
        local,
        mesh=fine,
        in_specs=(P(aud, vid), P(vid, aud), P(), P()),
        out_specs=(P(aud), P(aud, vid), P(vid, aud)),
        check_vma=False,
    )
```

```python
import jax
import jax.numpy as jnp
from jax import lax
from jax.experimental import pallas as pl
from jax.experimental.pallas import tpu as pltpu
from jax.sharding import Mesh, PartitionSpec as P

F32 = jnp.float32
BF16 = jnp.bfloat16
F8 = jnp.float8_e4m3fn
UP_VALUE = 2.0**8
UP_REST = 2.0**17
DOWN = 2.0**-25
EPS = 1e-06
BLOCK = 512
SUBS = 2
VMEM = 56 * 2**20
PLANE = ("core", "y", "x")
MIB = 2**20
COLUMNS = [[4 * j + i for j in range(4)] for i in range(4)]
ROWS = [[16 + 4 * i + j for j in range(4)] for i in range(4)]
OUTER = COLUMNS + ROWS


def dot(a, b, dims):
    return lax.dot_general(a, b, (dims, ((), ())), preferred_element_type=F32)


def split(x, axis, value_first):
    high = x.astype(BF16)
    rest = ((x - high.astype(F32)) * UP_REST).astype(F8)
    value = (x * UP_VALUE).astype(F8)
    pair = (value, rest) if value_first else (rest, value)
    return high, jnp.concatenate(pair, axis=axis)


def product(a, b, dims):
    return dot(a[0], b[0], dims) + DOWN * dot(a[1], b[1], dims)


def prepare_kernel(place, whole, inv_ref, unit_t_out, v_high_out, v_small_out, t_high_out, t_small_out, *scratch):
    flipped, unit_t_ref, v_high, v_small, t_high, t_small, sems = scratch
    core, y, x = place[0], place[1], place[2]
    n = whole.shape[0]
    outs = (unit_t_out, t_high_out, t_small_out, v_high_out, v_small_out)
    copies = [
        pltpu.make_async_copy(ref, out, sems.at[k])
        for k, (ref, out) in enumerate(zip((unit_t_ref, t_high, t_small, v_high, v_small), outs))
    ]
    v_t = whole[...].T
    inv = lax.rsqrt(jnp.sum(v_t * v_t, axis=0, keepdims=True) + EPS)
    inv_ref[...] = inv
    flipped[...] = (v_t * inv).reshape(16, 64, n)
    for outer in range(4):
        for inner in range(4):
            row = lax.rem(y + 4 - jnp.where(core == 0, outer, inner), 4)
            column = lax.rem(x + 4 - jnp.where(core == 0, inner, outer), 4)
            at = 64 * (4 * outer + inner)
            unit_t_ref[at : at + 64, :] = flipped[4 * row + column]
    copies[0].start()
    unit_t = unit_t_ref[...]
    t_high[...], t_small[...] = split(unit_t, 1, True)
    copies[1].start()
    copies[2].start()
    v_high[...], v_small[...] = split(unit_t.T, 1, True)
    copies[3].start()
    copies[4].start()
    for copy in copies:
        copy.wait()


def prepare(video, place):
    n = video.shape[0]
    whole = pl.BlockSpec(memory_space=pltpu.VMEM)
    shape = jax.ShapeDtypeStruct
    parts = [
        shape((1024, n), F32),
        shape((n, 1024), BF16),
        shape((n, 2048), F8),
        shape((1024, n), BF16),
        shape((1024, 2 * n), F8),
    ]
    return pl.pallas_call(
        prepare_kernel,
        in_specs=[pl.BlockSpec(memory_space=pltpu.SMEM), whole],
        out_specs=[whole] + [pl.BlockSpec(memory_space=pl.ANY)] * 5,
        out_shape=[shape((1, n), F32)] + parts,
        scratch_shapes=[pltpu.VMEM((16, 64, n), F32)]
        + [pltpu.VMEM(p.shape, p.dtype) for p in parts]
        + [pltpu.SemaphoreType.DMA((5,))],
        compiler_params=pltpu.CompilerParams(vmem_limit_bytes=VMEM),
        cost_estimate=pl.CostEstimate(flops=0, bytes_accessed=16 * MIB, transcendentals=0),
        name="video_parts",
    )(place, video)


def inverse(d):
    r = pl.reciprocal(d, approx=True)
    return r * (2.0 - d * r)


def soft(power):
    return jnp.where(power < 1e-3, power - 0.5 * power * power, jnp.log(1.0 + power))


def pairs_kernel(first, refs):
    place, scalars, *refs = refs
    audio, refs = refs[:4], refs[4:]
    sources, refs = refs[:5], refs[5 if first else 9 :]
    if first:
        grads_a = [refs[0].at[lax.rem(place[4] + 4 - k, 4)] for k in range(4)]
        refs = refs[1:]
    else:
        grads_a, refs = refs[:4], refs[4:]
    side_ref, unit_high, unit_small, away_high, away_small, *refs = refs
    near, v_high, v_small, t_high, t_small, sems = refs
    step = pl.program_id(0)
    scale, bias = scalars[0], scalars[1]
    n = v_high.shape[0]
    block = side_ref.shape[1]
    sub = block // SUBS
    offset = place[3] + step * block
    loads = [
        pltpu.make_async_copy(source, to, sems.at[k])
        for k, (source, to) in enumerate(zip(sources, (near, v_high, v_small, t_high, t_small)))
    ]

    @pl.when(step == 0)
    def _():
        for load in (*loads[1:], loads[0]):
            load.start()

    audio_t = jnp.concatenate([r[...] for r in audio], axis=0)
    inv = lax.rsqrt(jnp.sum(audio_t * audio_t, axis=0, keepdims=True) + EPS)
    side_ref[0:1, :] = inv
    side_ref[1:8, :] = jnp.zeros((7, block), F32)
    unit_t = audio_t * inv

    @pl.when(step == 0)
    def _():
        for load in loads[1:3]:
            load.wait()

    def similar(k):
        lanes = slice(k * sub, (k + 1) * sub)
        part = split(unit_t[:, lanes], 0, False)
        unit_high[:, lanes], unit_small[:, lanes] = part
        return scale * product((v_high[...], v_small[...]), part, ((1,), (0,)))

    def judge(k, scaled):
        lanes = slice(k * sub, (k + 1) * sub)
        power = jnp.exp(scaled + bias)
        sig = power * inverse(1.0 + power)
        paired = (
            lax.broadcasted_iota(jnp.int32, (n, sub), 0)
            - lax.broadcasted_iota(jnp.int32, (n, sub), 1)
        ) == offset + k * sub
        away = split(jnp.where(paired, 0.0, sig), 0, False)
        away_high[:, lanes], away_small[:, lanes] = away
        return paired, away, jnp.sum(soft(power), axis=0, keepdims=True)

    def pull_rows(k, away, loss):
        lanes = slice(k * sub, (k + 1) * sub)
        grad_a = product((t_high[...], t_small[...]), away, ((1,), (0,)))
        inner = jnp.sum(grad_a * unit_t[:, lanes], axis=0, keepdims=True)
        for p, ref in enumerate(grads_a):
            ref[0:256, lanes] = grad_a[256 * p : 256 * p + 256, :]
            ref[256:257, lanes] = loss
            ref[257:258, lanes] = inner
            ref[258:264, lanes] = jnp.zeros((6, sub), F32)

    scores = [similar(k) for k in range(SUBS)]
    judged = [judge(0, scores[0])]

    @pl.when(step == 0)
    def _():
        for load in (*loads[3:], loads[0]):
            load.wait()

    for k in range(SUBS):
        if k > 0:
            judged.append(judge(k, scores[k]))
        pull_rows(k, judged[k][1], judged[k][2])

    @pl.when((offset >= 0) & (offset < n))
    def _():
        at = pl.multiple_of(offset, block)
        own = jnp.concatenate(
            [jnp.sum(jnp.where(j[0], s, 0.0), axis=0, keepdims=True) for j, s in zip(judged, scores)],
            axis=1,
        )
        value = own + bias
        diag = -1.0 / (1.0 + jnp.exp(value))
        side_ref[1:2, :] = diag
        pull = near[:, pl.ds(at, block)] * diag
        inner_own = jnp.sum(pull * unit_t, axis=0, keepdims=True)
        for k, ref in enumerate(grads_a):
            ref[0:256, :] += pull[256 * k : 256 * k + 256, :]
            ref[256:257, :] += -value
            ref[257:258, :] += inner_own


def pairs(audio, video, place, scalars, before):
    rows = audio[0].shape[1]
    first = before is None
    n = video[1].shape[0]
    smem = pl.BlockSpec(memory_space=pltpu.SMEM)
    anywhere = pl.BlockSpec(memory_space=pl.ANY)
    shape = jax.ShapeDtypeStruct
    skip = 0 if first else rows // BLOCK

    def moving(height):
        return pl.BlockSpec((height, BLOCK), lambda i, at: (0, i))

    def shared(height):
        return pl.BlockSpec((height, BLOCK), lambda i, at: (0, i + skip))

    def turned(k):
        return pl.BlockSpec((256, BLOCK), lambda i, at: (lax.rem(at[4] + 4 - k, 4), i))

    if len(audio) == 1:
        blocks = [turned(k) for k in range(4)]
    else:
        blocks = [moving(256)] * 4
    in_specs = [smem] + blocks + [anywhere] * 5
    operands = [scalars, *(audio * (4 // len(audio))), *video]
    if first:
        out_specs = [pl.BlockSpec((4, 264, BLOCK), lambda i, at: (0, 0, i))]
        out_shape = [shape((4, 264, rows), F32)]
        aliases = {}
    else:
        aliases = {1 + len(operands) + k: 5 + k for k in range(4)}
        in_specs += [anywhere] * 4
        operands += before
        out_specs = [moving(264)] * 4
        out_shape = [shape((264, rows), F32)] * 4
    out_specs += [moving(8), shared(1024), shared(2048), shared(n), shared(2 * n)]
    out_shape += [
        shape((8, rows), F32),
        shape((1024, 2 * rows), BF16),
        shape((2048, 2 * rows), F8),
        shape((n, 2 * rows), BF16),
        shape((2 * n, 2 * rows), F8),
    ]

    def body(*refs):
        pairs_kernel(first, refs)

    return pl.pallas_call(
        body,
        grid_spec=pltpu.PrefetchScalarGridSpec(
            num_scalar_prefetch=1,
            grid=(rows // BLOCK,),
            in_specs=in_specs,
            out_specs=out_specs,
            scratch_shapes=[pltpu.VMEM(v.shape, v.dtype) for v in video] + [pltpu.SemaphoreType.DMA((5,))],
        ),
        out_shape=out_shape,
        input_output_aliases=aliases,
        compiler_params=pltpu.CompilerParams(vmem_limit_bytes=VMEM),
        cost_estimate=pl.CostEstimate(
            flops=4 * 2 * rows * n * 1024, bytes_accessed=32 * MIB, transcendentals=3 * rows * n
        ),
        name="pairs_first" if first else "pairs_last",
    )(place, *operands)


def video_kernel(place, unit_high, unit_small, away_high, away_small, near_side, late_side, *refs):
    early, (late, unit_t_hbm, whole), refs = refs[:4], refs[4:7], refs[7:]
    state, unit_t, rows_ref, sems = refs
    step = pl.program_id(0)
    n = away_high.shape[0]
    block = near_side.shape[1]
    half = pl.num_programs(0) // 2
    offset = place[3] + step * block
    crossing = (offset >= 0) & (offset < n)
    load = pltpu.make_async_copy(unit_t_hbm, unit_t, sems.at[4])
    from_early, from_late = [], []
    for k in range(4):
        to = rows_ref.at[pl.ds(256 * k, 256), :]
        lanes = pl.ds(pl.multiple_of(lax.rem(step, half) * block, block), block)
        turn = pl.multiple_of(lax.rem(place[4] + 4 - k, 4) * 256, 256)
        from_early.append(pltpu.make_async_copy(early[k].at[:, lanes], to, sems.at[k]))
        from_late.append(pltpu.make_async_copy(late.at[pl.ds(turn, 256), lanes], to, sems.at[k]))

    @pl.when(step == 0)
    def _():
        load.start()
        state[...] = jnp.zeros_like(state)

    @pl.when(crossing & (step < half))
    def _():
        for copy in from_early:
            copy.start()

    @pl.when(crossing & (step >= half))
    def _():
        for copy in from_late:
            copy.start()

    dims = ((1,), (1,))
    small = dot(unit_small[1024:], away_small[:n], dims) + dot(unit_small[:1024], away_small[n:], dims)
    state[...] += dot(unit_high[...], away_high[...], dims) + DOWN * small

    @pl.when(crossing)
    def _():
        for copy in from_early:
            copy.wait()
        side = jnp.where(step < half, near_side[0:2, :], late_side[0:2, :])
        at = pl.multiple_of(offset, block)
        state[:, pl.ds(at, block)] += rows_ref[...] * (side[0:1, :] * side[1:2, :])

    @pl.when(step == pl.num_programs(0) - 1)
    def _():
        load.wait()
        core, y, x = place[0], place[1], place[2]
        row = jnp.sum(unit_t[...] * state[...], axis=0, keepdims=True)
        for owner in range(8):
            whole[owner, 128:129, :] = row
            whole[owner, 129:136, :] = jnp.zeros((7, n), F32)
            for part in range(2):
                dy = lax.rem(y + 4 - owner // 2, 4)
                dx = lax.rem(x + 4 - 2 * (owner % 2) - part, 4)
                at = jnp.where(core == 0, 4 * dy + dx, 4 * dx + dy) * 64
                piece = pl.ds(pl.multiple_of(at, 64), 64)
                whole[owner, 64 * part : 64 * part + 64, :] = state[piece, :]


def video_sums(shared, sides, early, late, unit_t, place):
    n = shared[2].shape[0]
    count = shared[0].shape[1] // BLOCK
    anywhere = pl.BlockSpec(memory_space=pl.ANY)
    moving = lambda height: pl.BlockSpec((height, BLOCK), lambda i, at: (0, i))
    first = pl.BlockSpec((8, BLOCK), lambda i, at: (0, jnp.minimum(i, count // 2 - 1)))
    second = pl.BlockSpec((8, BLOCK), lambda i, at: (0, jnp.maximum(i - count // 2, 0)))
    return pl.pallas_call(
        video_kernel,
        grid_spec=pltpu.PrefetchScalarGridSpec(
            num_scalar_prefetch=1,
            grid=(count,),
            in_specs=[moving(s.shape[0]) for s in shared] + [first, second] + [anywhere] * 6,
            out_specs=pl.BlockSpec((8, 136, n), lambda i, at: (0, 0, 0), pipeline_mode=pl.Buffered(1)),
            scratch_shapes=[
                pltpu.VMEM((1024, n), F32),
                pltpu.VMEM((1024, n), F32),
                pltpu.VMEM((1024, BLOCK), F32),
                pltpu.SemaphoreType.DMA((5,)),
            ],
        ),
        out_shape=jax.ShapeDtypeStruct((8, 136, n), F32),
        compiler_params=pltpu.CompilerParams(vmem_limit_bytes=VMEM),
        cost_estimate=pl.CostEstimate(
            flops=2 * 2 * BLOCK * count * n * 1024, bytes_accessed=32 * MIB, transcendentals=0
        ),
        name="video_sums",
    )(place, *shared, *sides, *early, late, unit_t)


def perm(inner, k):
    pairs_of = []
    for core in range(2):
        for y in range(4):
            for x in range(4):
                along_x = (core == 0) == inner
                to = (core, y, (x + k) % 4) if along_x else (core, (y + k) % 4, x)
                pairs_of.append((16 * core + 4 * y + x, 16 * to[0] + 4 * to[1] + to[2]))
    return pairs_of


def move(block, inner, k):
    return lax.ppermute(block, PLANE, perm(inner, k))


def after(arrays, late):
    spec = pl.BlockSpec(memory_space=pl.ANY)
    return pl.pallas_call(
        lambda *refs: None,
        in_specs=[spec] * (len(arrays) + len(late)),
        out_specs=[spec] * len(late),
        out_shape=[jax.ShapeDtypeStruct(a.shape, a.dtype) for a in late],
        input_output_aliases={len(arrays) + i: i for i in range(len(late))},
        name="after",
    )(*arrays, *late)


def local(audio, video, scale, bias):
    z, core, y, x = (lax.axis_index(a) for a in ("z", "core", "y", "x"))
    n = video.shape[0]
    audio_t = audio.T
    rows = audio_t.shape[1]
    scalars = jnp.stack([scale, bias])
    base = (2 * z + core) * rows - (4 * y + x) * n

    whole_video = lax.all_gather(video, ("z", "core"), axis=1, tiled=True)
    row = [audio_t] + [move(audio_t, True, k) for k in (1, 2, 3)]
    part = rows // 2
    near, late = (jnp.concatenate([r[:, c * part : (c + 1) * part] for r in row], axis=0) for c in (0, 1))
    near = [near] + [move(near, False, k) for k in (1, 2, 3)]
    late = [lax.all_gather(late, PLANE, axis=0, tiled=True, axis_index_groups=OUTER)]
    inv_v, *parts = prepare(whole_video, jnp.stack([core, y, x]).astype(jnp.int32))
    outer = jnp.where(core == 0, y, x)
    places = [jnp.stack([core, y, x, base + c * part, outer]).astype(jnp.int32) for c in (0, 1)]
    whole, side_near, *shared = pairs(near, parts, places[0], scalars, None)
    *grads, side_late = (outs := pairs(late, parts, places[1], scalars, shared))[:5]
    state = video_sums(outs[5:], [side_near, side_late], near, late[0], parts[0], places[0])
    whole = whole.reshape(1056, part)
    came = [move(grads[k], False, 4 - k) for k in (1, 2, 3)]

    def inward(h):
        to = [jnp.concatenate([h[64 * k : 64 * k + 64], h[256:264]], axis=0) for k in range(4)]
        return [to[0]] + [move(to[k], True, 4 - k) for k in (1, 2, 3)]

    early = inward(lax.psum_scatter(whole, PLANE, scatter_dimension=0, tiled=True, axis_index_groups=OUTER))
    (kept,) = after([early[1][64:72] + early[2][64:72] + early[3][64:72]], [grads[0]])
    late = inward(kept + came[0] + came[1] + came[2])
    (state,) = after([came[0][256:264] + came[2][256:264]], [state])

    total_v = lax.psum_scatter(state.reshape(1088, n), ("z", "core"), scatter_dimension=0, tiled=True)
    grad_v = scale * (total_v[0:128] * inv_v - video.T * (inv_v * inv_v * total_v[128:129]))
    total_a = jnp.concatenate([sum(early[1:], early[0]), sum(late[1:], late[0])], axis=1)
    inv_a = jnp.concatenate([side_near[0:1], side_late[0:1]], axis=1)
    row_loss, inner_a = total_a[64], total_a[65:66]
    grad_a = scale * (total_a[0:64] * inv_a - audio_t * (inv_a * inv_a * inner_a))
    return row_loss, grad_a.T, grad_v.T


def solution(mesh):
    fine = Mesh(mesh.devices.reshape(4, 2, 4, 4), ("z", "core", "y", "x"))
    aud, vid = ("z", "core"), ("y", "x")
    return jax.shard_map(
        local,
        mesh=fine,
        in_specs=(P(aud, vid), P(vid, aud), P(), P()),
        out_specs=(P(aud), P(aud, vid), P(vid, aud)),
        check_vma=False,
    )
```

```python
import jax
import jax.numpy as jnp
from jax import lax
from jax.experimental import pallas as pl
from jax.experimental.pallas import tpu as pltpu
from jax.sharding import Mesh, PartitionSpec as P

F32 = jnp.float32
BF16 = jnp.bfloat16
F8 = jnp.float8_e4m3fn
UP_VALUE = 2.0**8
UP_REST = 2.0**17
DOWN = 2.0**-25
EPS = 1e-06
BLOCK = 512
SUBS = 2
VMEM = 56 * 2**20
PLANE = ("core", "y", "x")
MIB = 2**20
COLUMNS = [[4 * j + i for j in range(4)] for i in range(4)]
ROWS = [[16 + 4 * i + j for j in range(4)] for i in range(4)]
OUTER = COLUMNS + ROWS


def dot(a, b, dims):
    return lax.dot_general(a, b, (dims, ((), ())), preferred_element_type=F32)


def split(x, axis, value_first):
    high = x.astype(BF16)
    rest = ((x - high.astype(F32)) * UP_REST).astype(F8)
    value = (x * UP_VALUE).astype(F8)
    pair = (value, rest) if value_first else (rest, value)
    return high, jnp.concatenate(pair, axis=axis)


def product(a, b, dims):
    return dot(a[0], b[0], dims) + DOWN * dot(a[1], b[1], dims)


def prepare_kernel(place, video, inv_ref, unit_t_out, v_high_out, v_small_out, t_high_out, t_small_out, *scratch):
    whole, unit_t_ref, v_high, v_small, t_high, t_small, in_sems, sems, quarter_sems = scratch
    core, y, x = place[0], place[1], place[2]
    n = whole.shape[0]
    quarter = n // 4
    columns = [pl.ds(256 * row, 256) for row in range(4)]
    loads = [
        pltpu.make_async_copy(video.at[:, c], whole.at[:, c], in_sems.at[row]) for row, c in enumerate(columns)
    ]
    outs = (unit_t_out, t_high_out, t_small_out)
    copies = [
        pltpu.make_async_copy(ref, out, sems.at[k])
        for k, (ref, out) in enumerate(zip((unit_t_ref, t_high, t_small), outs))
    ]
    for load in loads:
        load.start()
    v_t = []
    for row, c in enumerate(columns):
        loads[row].wait()
        v_t.append(whole[:, c].T)
    inv = lax.rsqrt(sum(jnp.sum(v * v, axis=0, keepdims=True) for v in v_t) + EPS)
    inv_ref[...] = inv
    for row in range(4):
        for column in range(4):
            dy, dx = lax.rem(y + 4 - row, 4), lax.rem(x + 4 - column, 4)
            at = jnp.where(core == 0, 4 * dy + dx, 4 * dx + dy) * 64
            piece = v_t[row][64 * column : 64 * column + 64, :]
            unit_t_ref[pl.ds(pl.multiple_of(at, 64), 64), :] = piece * inv
    copies[0].start()
    t_high[...], t_small[...] = split(unit_t_ref[...], 1, True)
    copies[1].start()
    copies[2].start()
    for k in range(4):
        rows = pl.ds(quarter * k, quarter)
        v_high[rows, :], v_small[rows, :] = split(unit_t_ref[:, rows].T, 1, True)
        for j, (ref, out) in enumerate(((v_high, v_high_out), (v_small, v_small_out))):
            copies.append(pltpu.make_async_copy(ref.at[rows, :], out.at[rows, :], quarter_sems.at[2 * k + j]))
            copies[-1].start()
    for copy in copies:
        copy.wait()


def prepare(video, place):
    n = video.shape[0]
    whole = pl.BlockSpec(memory_space=pltpu.VMEM)
    shape = jax.ShapeDtypeStruct
    parts = [
        shape((1024, n), F32),
        shape((n, 1024), BF16),
        shape((n, 2048), F8),
        shape((1024, n), BF16),
        shape((1024, 2 * n), F8),
    ]
    return pl.pallas_call(
        prepare_kernel,
        in_specs=[pl.BlockSpec(memory_space=pltpu.SMEM), pl.BlockSpec(memory_space=pl.ANY)],
        out_specs=[whole] + [pl.BlockSpec(memory_space=pl.ANY)] * 5,
        out_shape=[shape((1, n), F32)] + parts,
        scratch_shapes=[pltpu.VMEM((n, 1024), F32)]
        + [pltpu.VMEM(p.shape, p.dtype) for p in parts]
        + [pltpu.SemaphoreType.DMA((4,)), pltpu.SemaphoreType.DMA((3,)), pltpu.SemaphoreType.DMA((8,))],
        compiler_params=pltpu.CompilerParams(vmem_limit_bytes=VMEM),
        cost_estimate=pl.CostEstimate(flops=0, bytes_accessed=16 * MIB, transcendentals=0),
        name="video_parts",
    )(place, video)


def inverse(d):
    r = pl.reciprocal(d, approx=True)
    return r * (2.0 - d * r)


def soft(power):
    return jnp.where(power < 1e-3, power - 0.5 * power * power, jnp.log(1.0 + power))


def pairs_kernel(first, last, refs):
    place, scalars, *refs = refs
    audio, refs = refs[:4], refs[4:]
    unit_t_hbm, *sources = refs[:5]
    sources.append(unit_t_hbm)
    refs = refs[5:]
    before = None
    if not first:
        before, *refs = refs
    if last:
        grads_a, refs = refs[:4], refs[4:]
    else:
        grads_a = [refs[0].at[lax.rem(place[4] + 4 - k, 4)] for k in range(4)]
        refs = refs[1:]
    inv_ref, *refs = refs
    if last:
        whole, *refs = refs
    state, near, v_high, v_small, t_high, t_small, sems = refs
    step = pl.program_id(0)
    scale, bias = scalars[0], scalars[1]
    n = v_high.shape[0]
    block = inv_ref.shape[1]
    sub = block // SUBS
    offset = place[3] + step * block
    loads = [
        pltpu.make_async_copy(source, to, sems.at[k])
        for k, (source, to) in enumerate(zip(sources, (v_high, v_small, t_high, t_small, near)))
    ]
    if not first:
        loads.append(pltpu.make_async_copy(before, state, sems.at[5]))

    @pl.when(step == 0)
    def _():
        for load in loads:
            load.start()
        if first:
            state[...] = jnp.zeros_like(state)

    audio_t = jnp.concatenate([r[...] for r in audio], axis=0)
    inv = lax.rsqrt(jnp.sum(audio_t * audio_t, axis=0, keepdims=True) + EPS)
    inv_ref[...] = inv
    unit_t = audio_t * inv

    @pl.when(step == 0)
    def _():
        for load in loads[:2]:
            load.wait()

    def similar(k):
        part = split(unit_t[:, k * sub : (k + 1) * sub], 0, False)
        return scale * product((v_high[...], v_small[...]), part, ((1,), (0,)))

    def judge(k, scaled):
        power = jnp.exp(scaled + bias)
        sig = power * inverse(1.0 + power)
        paired = (
            lax.broadcasted_iota(jnp.int32, (n, sub), 0)
            - lax.broadcasted_iota(jnp.int32, (n, sub), 1)
        ) == offset + k * sub
        loss = jnp.sum(soft(power), axis=0, keepdims=True)
        return paired, split(jnp.where(paired, 0.0, sig), 0, False), loss

    def pull_rows(k, away, loss):
        lanes = slice(k * sub, (k + 1) * sub)
        grad_a = product((t_high[...], t_small[...]), away, ((1,), (0,)))
        inner = jnp.sum(grad_a * unit_t[:, lanes], axis=0, keepdims=True)
        for p, ref in enumerate(grads_a):
            ref[0:256, lanes] = grad_a[256 * p : 256 * p + 256, :]
            ref[256:257, lanes] = loss
            ref[257:258, lanes] = inner
            ref[258:264, lanes] = jnp.zeros((6, sub), F32)

    scores = [similar(k) for k in range(SUBS)]
    judged = [judge(0, scores[0])]

    @pl.when(step == 0)
    def _():
        for load in loads[2:]:
            load.wait()

    for k in range(SUBS):
        if k > 0:
            judged.append(judge(k, scores[k]))
        pull_rows(k, judged[k][1], judged[k][2])
    high = jnp.concatenate([j[1][0] for j in judged], axis=1)
    small = jnp.concatenate([j[1][1][:n] for j in judged] + [j[1][1][n:] for j in judged], axis=1)
    state[...] += product(split(unit_t, 1, True), (high, small), ((1,), (1,)))

    @pl.when((offset >= 0) & (offset < n))
    def _():
        at = pl.multiple_of(offset, block)
        own = jnp.concatenate(
            [jnp.sum(jnp.where(j[0], s, 0.0), axis=0, keepdims=True) for j, s in zip(judged, scores)],
            axis=1,
        )
        value = own + bias
        diag = -1.0 / (1.0 + jnp.exp(value))
        pull = near[:, pl.ds(at, block)] * diag
        inner_own = jnp.sum(pull * unit_t, axis=0, keepdims=True)
        for k, ref in enumerate(grads_a):
            ref[0:256, :] += pull[256 * k : 256 * k + 256, :]
            ref[256:257, :] += -value
            ref[257:258, :] += inner_own
        state[:, pl.ds(at, block)] += unit_t * diag

    if last:

        @pl.when(step == pl.num_programs(0) - 1)
        def _():
            core, y, x = place[0], place[1], place[2]
            for half in range(n // block):
                lanes = pl.ds(half * block, block)
                row = jnp.sum(near[:, lanes] * state[:, lanes], axis=0, keepdims=True)
                for owner in range(8):
                    whole[owner, 128:129, lanes] = row
            for owner in range(8):
                whole[owner, 129:136, :] = jnp.zeros((7, n), F32)
                for part in range(2):
                    dy = lax.rem(y + 4 - owner // 2, 4)
                    dx = lax.rem(x + 4 - 2 * (owner % 2) - part, 4)
                    at = jnp.where(core == 0, 4 * dy + dx, 4 * dx + dy) * 64
                    rows = pl.ds(pl.multiple_of(at, 64), 64)
                    whole[owner, 64 * part : 64 * part + 64, :] = state[rows, :]


def pairs(audio, video, place, scalars, before, last):
    rows = audio[0].shape[1]
    first = before is None
    n = video[1].shape[0]
    smem = pl.BlockSpec(memory_space=pltpu.SMEM)
    anywhere = pl.BlockSpec(memory_space=pl.ANY)
    shape = jax.ShapeDtypeStruct

    def still(shape):
        return pl.BlockSpec(shape, lambda i, at: (0,) * len(shape), pipeline_mode=pl.Buffered(1))

    def moving(height):
        return pl.BlockSpec((height, BLOCK), lambda i, at: (0, i))

    def turned(k):
        return pl.BlockSpec((256, BLOCK), lambda i, at: (lax.rem(at[4] + 4 - k, 4), i))

    if len(audio) == 1:
        blocks = [turned(k) for k in range(4)]
    else:
        blocks = [moving(256)] * 4
    in_specs = [smem] + blocks + [anywhere] * 5
    operands = [scalars, *(audio * (4 // len(audio))), *video]
    parts = [pltpu.VMEM(v.shape, v.dtype) for v in (video[0], *video[1:])]
    parts.append(pltpu.SemaphoreType.DMA((6,)))
    if not first:
        in_specs.append(anywhere)
        operands.append(before)
    if last:
        out_specs = [moving(264)] * 4 + [moving(1), still((8, 136, n))]
        out_shape = [shape((264, rows), F32)] * 4 + [shape((1, rows), F32), shape((8, 136, n), F32)]
        scratch = [pltpu.VMEM((1024, n), F32)] + parts
    else:
        whole = pl.BlockSpec((4, 264, BLOCK), lambda i, at: (0, 0, i))
        out_specs = [whole, moving(1), still((1024, n))]
        out_shape = [shape((4, 264, rows), F32), shape((1, rows), F32), shape((1024, n), F32)]
        scratch = parts

    def body(*refs):
        pairs_kernel(first, last, refs)

    return pl.pallas_call(
        body,
        grid_spec=pltpu.PrefetchScalarGridSpec(
            num_scalar_prefetch=1,
            grid=(rows // BLOCK,),
            in_specs=in_specs,
            out_specs=out_specs,
            scratch_shapes=scratch,
        ),
        out_shape=out_shape,
        compiler_params=pltpu.CompilerParams(vmem_limit_bytes=VMEM),
        cost_estimate=pl.CostEstimate(
            flops=6 * 2 * rows * n * 1024, bytes_accessed=24 * MIB, transcendentals=3 * rows * n
        ),
        name="pairs_last" if last else "pairs_first",
    )(place, *operands)


def perm(inner, k):
    pairs_of = []
    for core in range(2):
        for y in range(4):
            for x in range(4):
                along_x = (core == 0) == inner
                to = (core, y, (x + k) % 4) if along_x else (core, (y + k) % 4, x)
                pairs_of.append((16 * core + 4 * y + x, 16 * to[0] + 4 * to[1] + to[2]))
    return pairs_of


def move(block, inner, k):
    return lax.ppermute(block, PLANE, perm(inner, k))


def after(arrays, late):
    spec = pl.BlockSpec(memory_space=pl.ANY)
    return pl.pallas_call(
        lambda *refs: None,
        in_specs=[spec] * (len(arrays) + len(late)),
        out_specs=[spec] * len(late),
        out_shape=[jax.ShapeDtypeStruct(a.shape, a.dtype) for a in late],
        input_output_aliases={len(arrays) + i: i for i in range(len(late))},
        name="after",
    )(*arrays, *late)


def local(audio, video, scale, bias):
    z, core, y, x = (lax.axis_index(a) for a in ("z", "core", "y", "x"))
    n = video.shape[0]
    audio_t = audio.T
    rows = audio_t.shape[1]
    scalars = jnp.stack([scale, bias])
    base = (2 * z + core) * rows - (4 * y + x) * n

    whole_video = lax.all_gather(video, ("z", "core"), axis=1, tiled=True)
    row = [audio_t] + [move(audio_t, True, k) for k in (1, 2, 3)]
    part = rows // 2
    near, late = (jnp.concatenate([r[:, c * part : (c + 1) * part] for r in row], axis=0) for c in (0, 1))
    near = [near] + [move(near, False, k) for k in (1, 2, 3)]
    late = [lax.all_gather(late, PLANE, axis=0, tiled=True, axis_index_groups=OUTER)]
    inv_v, *parts = prepare(whole_video, jnp.stack([core, y, x]).astype(jnp.int32))
    outer = jnp.where(core == 0, y, x)
    places = [jnp.stack([core, y, x, base + c * part, outer]).astype(jnp.int32) for c in (0, 1)]
    whole, inv_near, state = pairs(near, parts, places[0], scalars, None, False)
    *grads, inv_late, state = pairs(late, parts, places[1], scalars, state, True)
    whole = whole.reshape(1056, part)
    halves = [
        lax.psum_scatter(whole, PLANE, scatter_dimension=0, tiled=True, axis_index_groups=OUTER),
        grads[0] + sum(move(grads[k], False, 4 - k) for k in (1, 2, 3)),
    ]

    total_v = lax.psum_scatter(state.reshape(1088, n), ("z", "core"), scatter_dimension=0, tiled=True)
    grad_v = scale * (total_v[0:128] * inv_v - video.T * (inv_v * inv_v * total_v[128:129]))
    to = [
        jnp.concatenate(
            [jnp.concatenate([h[64 * k : 64 * k + 64], h[256:264]], axis=0) for h in halves], axis=1
        )
        for k in range(4)
    ]
    (kept,) = after([grad_v[:8]], [to[0]])
    total_a = kept + sum(move(to[k], True, 4 - k) for k in (1, 2, 3))
    inv_a = jnp.concatenate([inv_near, inv_late], axis=1)
    row_loss, inner_a = total_a[64], total_a[65:66]
    grad_a = scale * (total_a[0:64] * inv_a - audio_t * (inv_a * inv_a * inner_a))
    return row_loss, grad_a.T, grad_v.T


def solution(mesh):
    fine = Mesh(mesh.devices.reshape(4, 2, 4, 4), ("z", "core", "y", "x"))
    aud, vid = ("z", "core"), ("y", "x")
    return jax.shard_map(
        local,
        mesh=fine,
        in_specs=(P(aud, vid), P(vid, aud), P(), P()),
        out_specs=(P(aud), P(aud, vid), P(vid, aud)),
        check_vma=False,
    )
```

```python
import jax
import jax.numpy as jnp
from jax import lax
from jax.experimental import pallas as pl
from jax.experimental.pallas import tpu as pltpu
from jax.sharding import Mesh, PartitionSpec as P

F32 = jnp.float32
BF16 = jnp.bfloat16
F8 = jnp.float8_e4m3fn
UP_VALUE = 2.0**8
UP_REST = 2.0**17
DOWN = 2.0**-25
EPS = 1e-06
BLOCK = 512
SUBS = 2
VMEM = 56 * 2**20
PLANE = ("core", "y", "x")
MIB = 2**20
COLUMNS = [[4 * j + i for j in range(4)] for i in range(4)]
ROWS = [[16 + 4 * i + j for j in range(4)] for i in range(4)]
OUTER = COLUMNS + ROWS


def dot(a, b, dims):
    return lax.dot_general(a, b, (dims, ((), ())), preferred_element_type=F32)


def split(x, axis, value_first):
    high = x.astype(BF16)
    rest = ((x - high.astype(F32)) * UP_REST).astype(F8)
    value = (x * UP_VALUE).astype(F8)
    pair = (value, rest) if value_first else (rest, value)
    return high, jnp.concatenate(pair, axis=axis)


def product(a, b, dims):
    return dot(a[0], b[0], dims) + DOWN * dot(a[1], b[1], dims)


def prepare_kernel(place, video, inv_ref, unit_t_out, v_high_out, v_small_out, t_high_out, t_small_out, *scratch):
    whole, unit_t_ref, v_high, v_small, t_high, t_small, in_sems, sems, quarter_sems = scratch
    core, y, x = place[0], place[1], place[2]
    n = whole.shape[0]
    quarter = n // 4
    columns = [pl.ds(256 * row, 256) for row in range(4)]
    loads = [
        pltpu.make_async_copy(video.at[:, c], whole.at[:, c], in_sems.at[row]) for row, c in enumerate(columns)
    ]
    outs = (unit_t_out, t_high_out, t_small_out)
    copies = [
        pltpu.make_async_copy(ref, out, sems.at[k])
        for k, (ref, out) in enumerate(zip((unit_t_ref, t_high, t_small), outs))
    ]
    for load in loads:
        load.start()
    v_t = []
    for row, c in enumerate(columns):
        loads[row].wait()
        v_t.append(whole[:, c].T)
    inv = lax.rsqrt(sum(jnp.sum(v * v, axis=0, keepdims=True) for v in v_t) + EPS)
    inv_ref[...] = inv
    for row in range(4):
        for column in range(4):
            dy, dx = lax.rem(y + 4 - row, 4), lax.rem(x + 4 - column, 4)
            at = jnp.where(core == 0, 4 * dy + dx, 4 * dx + dy) * 64
            piece = v_t[row][64 * column : 64 * column + 64, :]
            unit_t_ref[pl.ds(pl.multiple_of(at, 64), 64), :] = piece * inv
    copies[0].start()
    t_high[...], t_small[...] = split(unit_t_ref[...], 1, True)
    copies[1].start()
    copies[2].start()
    for k in range(4):
        rows = pl.ds(quarter * k, quarter)
        v_high[rows, :], v_small[rows, :] = split(unit_t_ref[:, rows].T, 1, True)
        for j, (ref, out) in enumerate(((v_high, v_high_out), (v_small, v_small_out))):
            copies.append(pltpu.make_async_copy(ref.at[rows, :], out.at[rows, :], quarter_sems.at[2 * k + j]))
            copies[-1].start()
    for copy in copies:
        copy.wait()


def prepare(video, place):
    n = video.shape[0]
    whole = pl.BlockSpec(memory_space=pltpu.VMEM)
    shape = jax.ShapeDtypeStruct
    parts = [
        shape((1024, n), F32),
        shape((n, 1024), BF16),
        shape((n, 2048), F8),
        shape((1024, n), BF16),
        shape((1024, 2 * n), F8),
    ]
    return pl.pallas_call(
        prepare_kernel,
        in_specs=[pl.BlockSpec(memory_space=pltpu.SMEM), pl.BlockSpec(memory_space=pl.ANY)],
        out_specs=[whole] + [pl.BlockSpec(memory_space=pl.ANY)] * 5,
        out_shape=[shape((1, n), F32)] + parts,
        scratch_shapes=[pltpu.VMEM((n, 1024), F32)]
        + [pltpu.VMEM(p.shape, p.dtype) for p in parts]
        + [pltpu.SemaphoreType.DMA((4,)), pltpu.SemaphoreType.DMA((3,)), pltpu.SemaphoreType.DMA((8,))],
        compiler_params=pltpu.CompilerParams(vmem_limit_bytes=VMEM),
        cost_estimate=pl.CostEstimate(flops=0, bytes_accessed=16 * MIB, transcendentals=0),
        name="video_parts",
    )(place, video)


def inverse(d):
    r = pl.reciprocal(d, approx=True)
    return r * (2.0 - d * r)


def soft(power):
    return jnp.where(power < 1e-3, power - 0.5 * power * power, jnp.log(1.0 + power))


def pairs_kernel(first, last, refs):
    place, scalars, *refs = refs
    audio, refs = refs[:4], refs[4:]
    unit_t_hbm, *sources = refs[:5]
    sources.append(unit_t_hbm)
    refs = refs[5:]
    before = None
    if not first:
        before, *refs = refs
    if last:
        grads_a, refs = refs[:4], refs[4:]
    else:
        grads_a = [refs[0].at[lax.rem(place[4] + 4 - k, 4)] for k in range(4)]
        refs = refs[1:]
    inv_ref, *refs = refs
    if last:
        whole, *refs = refs
    state, near, v_high, v_small, t_high, t_small, sems = refs
    step = pl.program_id(0)
    scale, bias = scalars[0], scalars[1]
    n = v_high.shape[0]
    block = inv_ref.shape[1]
    sub = block // SUBS
    offset = place[3] + (step if first else step + pl.num_programs(0)) * block
    loads = [
        pltpu.make_async_copy(source, to, sems.at[k])
        for k, (source, to) in enumerate(zip(sources, (v_high, v_small, t_high, t_small, near)))
    ]
    if not first:
        loads.append(pltpu.make_async_copy(before, state, sems.at[5]))

    @pl.when(step == 0)
    def _():
        for load in loads:
            load.start()
        if first:
            state[...] = jnp.zeros_like(state)

    audio_t = jnp.concatenate([r[...] for r in audio], axis=0)
    inv = lax.rsqrt(jnp.sum(audio_t * audio_t, axis=0, keepdims=True) + EPS)
    inv_ref[...] = inv
    unit_t = audio_t * inv

    @pl.when(step == 0)
    def _():
        for load in loads[:2]:
            load.wait()

    def similar(k):
        part = split(unit_t[:, k * sub : (k + 1) * sub], 0, False)
        return scale * product((v_high[...], v_small[...]), part, ((1,), (0,)))

    def judge(k, scaled):
        power = jnp.exp(scaled + bias)
        sig = power * inverse(1.0 + power)
        paired = (
            lax.broadcasted_iota(jnp.int32, (n, sub), 0)
            - lax.broadcasted_iota(jnp.int32, (n, sub), 1)
        ) == offset + k * sub
        loss = jnp.sum(soft(power), axis=0, keepdims=True)
        return paired, split(jnp.where(paired, 0.0, sig), 0, False), loss

    def pull_rows(k, away, loss):
        lanes = slice(k * sub, (k + 1) * sub)
        grad_a = product((t_high[...], t_small[...]), away, ((1,), (0,)))
        inner = jnp.sum(grad_a * unit_t[:, lanes], axis=0, keepdims=True)
        for p, ref in enumerate(grads_a):
            ref[0:256, lanes] = grad_a[256 * p : 256 * p + 256, :]
            ref[256:257, lanes] = loss
            ref[257:258, lanes] = inner
            ref[258:264, lanes] = jnp.zeros((6, sub), F32)

    scores = [similar(k) for k in range(SUBS)]
    judged = [judge(0, scores[0])]

    @pl.when(step == 0)
    def _():
        for load in loads[2:]:
            load.wait()

    for k in range(SUBS):
        if k > 0:
            judged.append(judge(k, scores[k]))
        pull_rows(k, judged[k][1], judged[k][2])
    high = jnp.concatenate([j[1][0] for j in judged], axis=1)
    small = jnp.concatenate([j[1][1][:n] for j in judged] + [j[1][1][n:] for j in judged], axis=1)
    state[...] += product(split(unit_t, 1, True), (high, small), ((1,), (1,)))

    @pl.when((offset >= 0) & (offset < n))
    def _():
        at = pl.multiple_of(offset, block)
        own = jnp.concatenate(
            [jnp.sum(jnp.where(j[0], s, 0.0), axis=0, keepdims=True) for j, s in zip(judged, scores)],
            axis=1,
        )
        value = own + bias
        diag = -1.0 / (1.0 + jnp.exp(value))
        pull = near[:, pl.ds(at, block)] * diag
        inner_own = jnp.sum(pull * unit_t, axis=0, keepdims=True)
        for k, ref in enumerate(grads_a):
            ref[0:256, :] += pull[256 * k : 256 * k + 256, :]
            ref[256:257, :] += -value
            ref[257:258, :] += inner_own
        state[:, pl.ds(at, block)] += unit_t * diag

    if last:

        @pl.when(step == pl.num_programs(0) - 1)
        def _():
            core, y, x = place[0], place[1], place[2]
            for half in range(n // block):
                lanes = pl.ds(half * block, block)
                row = jnp.sum(near[:, lanes] * state[:, lanes], axis=0, keepdims=True)
                for owner in range(8):
                    whole[owner, 128:129, lanes] = row
            for owner in range(8):
                whole[owner, 129:136, :] = jnp.zeros((7, n), F32)
                for part in range(2):
                    dy = lax.rem(y + 4 - owner // 2, 4)
                    dx = lax.rem(x + 4 - 2 * (owner % 2) - part, 4)
                    at = jnp.where(core == 0, 4 * dy + dx, 4 * dx + dy) * 64
                    rows = pl.ds(pl.multiple_of(at, 64), 64)
                    whole[owner, 64 * part : 64 * part + 64, :] = state[rows, :]


def pairs(audio, video, place, scalars, before, last):
    rows = audio[0].shape[1]
    first = before is None
    n = video[1].shape[0]
    smem = pl.BlockSpec(memory_space=pltpu.SMEM)
    anywhere = pl.BlockSpec(memory_space=pl.ANY)
    shape = jax.ShapeDtypeStruct

    def still(shape):
        return pl.BlockSpec(shape, lambda i, at: (0,) * len(shape), pipeline_mode=pl.Buffered(1))

    def moving(height):
        return pl.BlockSpec((height, BLOCK), lambda i, at: (0, i))

    def turned(k):
        return pl.BlockSpec((256, BLOCK), lambda i, at: (lax.rem(at[4] + 4 - k, 4), i))

    if len(audio) == 1:
        blocks = [turned(k) for k in range(4)]
    else:
        blocks = [moving(256)] * 4
    in_specs = [smem] + blocks + [anywhere] * 5
    operands = [scalars, *(audio * (4 // len(audio))), *video]
    parts = [pltpu.VMEM(v.shape, v.dtype) for v in (video[0], *video[1:])]
    parts.append(pltpu.SemaphoreType.DMA((6,)))
    if not first:
        in_specs.append(anywhere)
        operands.append(before)
    if last:
        out_specs = [moving(264)] * 4 + [moving(1), still((8, 136, n))]
        out_shape = [shape((264, rows), F32)] * 4 + [shape((1, rows), F32), shape((8, 136, n), F32)]
        scratch = [pltpu.VMEM((1024, n), F32)] + parts
    else:
        whole = pl.BlockSpec((4, 264, BLOCK), lambda i, at: (0, 0, i))
        out_specs = [whole, moving(1), still((1024, n))]
        out_shape = [shape((4, 264, rows), F32), shape((1, rows), F32), shape((1024, n), F32)]
        scratch = parts

    def body(*refs):
        pairs_kernel(first, last, refs)

    return pl.pallas_call(
        body,
        grid_spec=pltpu.PrefetchScalarGridSpec(
            num_scalar_prefetch=1,
            grid=(rows // BLOCK,),
            in_specs=in_specs,
            out_specs=out_specs,
            scratch_shapes=scratch,
        ),
        out_shape=out_shape,
        compiler_params=pltpu.CompilerParams(vmem_limit_bytes=VMEM),
        cost_estimate=pl.CostEstimate(
            flops=6 * 2 * rows * n * 1024, bytes_accessed=24 * MIB, transcendentals=3 * rows * n
        ),
        name="pairs_last" if last else "pairs_first",
    )(place, *operands)


def perm(inner, k):
    pairs_of = []
    for core in range(2):
        for y in range(4):
            for x in range(4):
                along_x = (core == 0) == inner
                to = (core, y, (x + k) % 4) if along_x else (core, (y + k) % 4, x)
                pairs_of.append((16 * core + 4 * y + x, 16 * to[0] + 4 * to[1] + to[2]))
    return pairs_of


def move(block, inner, k):
    return lax.ppermute(block, PLANE, perm(inner, k))


def after(arrays, late):
    spec = pl.BlockSpec(memory_space=pl.ANY)
    return pl.pallas_call(
        lambda *refs: None,
        in_specs=[spec] * (len(arrays) + len(late)),
        out_specs=[spec] * len(late),
        out_shape=[jax.ShapeDtypeStruct(a.shape, a.dtype) for a in late],
        input_output_aliases={len(arrays) + i: i for i in range(len(late))},
        name="after",
    )(*arrays, *late)


def local(audio, video, scale, bias):
    z, core, y, x = (lax.axis_index(a) for a in ("z", "core", "y", "x"))
    n = video.shape[0]
    audio_t = audio.T
    rows = audio_t.shape[1]
    scalars = jnp.stack([scale, bias])
    base = (2 * z + core) * rows - (4 * y + x) * n

    whole_video = lax.all_gather(video, ("z", "core"), axis=1, tiled=True)
    row = [audio_t] + [move(audio_t, True, k) for k in (1, 2, 3)]
    part = rows // 2
    near, late = (jnp.concatenate([r[:, c * part : (c + 1) * part] for r in row], axis=0) for c in (0, 1))
    near = [near] + [move(near, False, k) for k in (1, 2, 3)]
    late = [lax.all_gather(late, PLANE, axis=0, tiled=True, axis_index_groups=OUTER)]
    outer = jnp.where(core == 0, y, x)
    place = jnp.stack([core, y, x, base, outer]).astype(jnp.int32)
    inv_v, *parts = prepare(whole_video, place)
    whole, inv_near, state = pairs(near, parts, place, scalars, None, False)
    *grads, inv_late, state = pairs(late, parts, place, scalars, state, True)
    whole = whole.reshape(1056, part)
    early = lax.psum_scatter(whole, PLANE, scatter_dimension=0, tiled=True, axis_index_groups=OUTER)
    came = [grads[0]] + [move(grads[k], False, 4 - k) for k in (1, 2, 3)]

    def rows_of(low, high):
        return jnp.concatenate([early[low:high], sum(c[low:high] for c in came)], axis=1)

    to = [
        jnp.concatenate([rows_of(64 * k, 64 * k + 64), rows_of(256, 264)], axis=0) for k in range(4)
    ]

    total_v = lax.psum_scatter(state.reshape(1088, n), ("z", "core"), scatter_dimension=0, tiled=True)
    grad_v = scale * (total_v[0:128] * inv_v - video.T * (inv_v * inv_v * total_v[128:129]))
    (kept,) = after([grad_v[:8]], [to[0]])
    blocks = [kept] + [move(to[k], True, 4 - k) for k in (1, 2, 3)]
    side, total_a = sum(t[64:] for t in blocks), sum(t[:64] for t in blocks)
    inv_a = jnp.concatenate([inv_near, inv_late], axis=1)
    row_loss, inner_a = side[0], side[1:2]
    grad_a = scale * (total_a * inv_a - audio_t * (inv_a * inv_a * inner_a))
    return row_loss, grad_a.T, grad_v.T


def solution(mesh):
    fine = Mesh(mesh.devices.reshape(4, 2, 4, 4), ("z", "core", "y", "x"))
    aud, vid = ("z", "core"), ("y", "x")
    return jax.shard_map(
        local,
        mesh=fine,
        in_specs=(P(aud, vid), P(vid, aud), P(), P()),
        out_specs=(P(aud), P(aud, vid), P(vid, aud)),
        check_vma=False,
    )
```

```python
import jax
import jax.numpy as jnp
from jax import lax
from jax.experimental import pallas as pl
from jax.experimental.pallas import tpu as pltpu
from jax.sharding import Mesh, PartitionSpec as P

F32 = jnp.float32
BF16 = jnp.bfloat16
F8 = jnp.float8_e4m3fn
UP_VALUE = 2.0**8
UP_REST = 2.0**17
DOWN = 2.0**-25
EPS = 1e-06
BLOCK = 512
SUBS = 2
VMEM = 56 * 2**20
PLANE = ("core", "y", "x")
MIB = 2**20
COLUMNS = [[4 * j + i for j in range(4)] for i in range(4)]
ROWS = [[16 + 4 * i + j for j in range(4)] for i in range(4)]
OUTER = COLUMNS + ROWS


def dot(a, b, dims):
    return lax.dot_general(a, b, (dims, ((), ())), preferred_element_type=F32)


def split(x, axis, value_first):
    high = x.astype(BF16)
    rest = ((x - high.astype(F32)) * UP_REST).astype(F8)
    value = (x * UP_VALUE).astype(F8)
    pair = (value, rest) if value_first else (rest, value)
    return high, jnp.concatenate(pair, axis=axis)


def product(a, b, dims):
    return dot(a[0], b[0], dims) + DOWN * dot(a[1], b[1], dims)


def prepare_kernel(place, video, inv_ref, unit_t_out, v_high_out, v_small_out, t_high_out, t_small_out, *scratch):
    whole, unit_t_ref, v_high, v_small, t_high, t_small, in_sems, sems, quarter_sems = scratch
    core, y, x = place[0], place[1], place[2]
    n = whole.shape[0]
    quarter = n // 4
    columns = [pl.ds(256 * row, 256) for row in range(4)]
    loads = [
        pltpu.make_async_copy(video.at[:, c], whole.at[:, c], in_sems.at[row]) for row, c in enumerate(columns)
    ]
    outs = (unit_t_out, t_high_out, t_small_out)
    copies = [
        pltpu.make_async_copy(ref, out, sems.at[k])
        for k, (ref, out) in enumerate(zip((unit_t_ref, t_high, t_small), outs))
    ]
    for load in loads:
        load.start()
    v_t = []
    for row, c in enumerate(columns):
        loads[row].wait()
        v_t.append(whole[:, c].T)
    inv = lax.rsqrt(sum(jnp.sum(v * v, axis=0, keepdims=True) for v in v_t) + EPS)
    inv_ref[...] = inv
    for row in range(4):
        for column in range(4):
            dy, dx = lax.rem(y + 4 - row, 4), lax.rem(x + 4 - column, 4)
            at = jnp.where(core == 0, 4 * dy + dx, 4 * dx + dy) * 64
            piece = v_t[row][64 * column : 64 * column + 64, :]
            unit_t_ref[pl.ds(pl.multiple_of(at, 64), 64), :] = piece * inv
    copies[0].start()
    t_high[...], t_small[...] = split(unit_t_ref[...], 1, True)
    copies[1].start()
    copies[2].start()
    for k in range(4):
        rows = pl.ds(quarter * k, quarter)
        v_high[rows, :], v_small[rows, :] = split(unit_t_ref[:, rows].T, 1, True)
        for j, (ref, out) in enumerate(((v_high, v_high_out), (v_small, v_small_out))):
            copies.append(pltpu.make_async_copy(ref.at[rows, :], out.at[rows, :], quarter_sems.at[2 * k + j]))
            copies[-1].start()
    for copy in copies:
        copy.wait()


def prepare(video, place):
    n = video.shape[0]
    whole = pl.BlockSpec(memory_space=pltpu.VMEM)
    shape = jax.ShapeDtypeStruct
    parts = [
        shape((1024, n), F32),
        shape((n, 1024), BF16),
        shape((n, 2048), F8),
        shape((1024, n), BF16),
        shape((1024, 2 * n), F8),
    ]
    return pl.pallas_call(
        prepare_kernel,
        in_specs=[pl.BlockSpec(memory_space=pltpu.SMEM), pl.BlockSpec(memory_space=pl.ANY)],
        out_specs=[whole] + [pl.BlockSpec(memory_space=pl.ANY)] * 5,
        out_shape=[shape((1, n), F32)] + parts,
        scratch_shapes=[pltpu.VMEM((n, 1024), F32)]
        + [pltpu.VMEM(p.shape, p.dtype) for p in parts]
        + [pltpu.SemaphoreType.DMA((4,)), pltpu.SemaphoreType.DMA((3,)), pltpu.SemaphoreType.DMA((8,))],
        compiler_params=pltpu.CompilerParams(vmem_limit_bytes=VMEM),
        cost_estimate=pl.CostEstimate(flops=0, bytes_accessed=16 * MIB, transcendentals=0),
        name="video_parts",
    )(place, video)


def inverse(d):
    r = pl.reciprocal(d, approx=True)
    return r * (2.0 - d * r)


def soft(power):
    return jnp.where(power < 1e-3, power - 0.5 * power * power, jnp.log(1.0 + power))


def pairs_kernel(first, last, refs):
    place, scalars, *refs = refs
    audio, refs = refs[:4], refs[4:]
    unit_t_hbm, *sources = refs[:5]
    sources.append(unit_t_hbm)
    refs = refs[5:]
    before = None
    if not first:
        before, *refs = refs
    if last:
        grads_a, refs = refs[:4], refs[4:]
    else:
        grads_a = [refs[0].at[lax.rem(place[4] + 4 - k, 4)] for k in range(4)]
        refs = refs[1:]
    inv_ref, *refs = refs
    if last:
        whole, *refs = refs
    state, near, v_high, v_small, t_high, t_small, sems = refs
    step = pl.program_id(0)
    scale, bias = scalars[0], scalars[1]
    n = v_high.shape[0]
    block = inv_ref.shape[1]
    sub = block // SUBS
    offset = place[3] + (step if first else step + pl.num_programs(0)) * block
    loads = [
        pltpu.make_async_copy(source, to, sems.at[k])
        for k, (source, to) in enumerate(zip(sources, (v_high, v_small, t_high, t_small, near)))
    ]
    if not first:
        loads.append(pltpu.make_async_copy(before, state, sems.at[5]))

    @pl.when(step == 0)
    def _():
        for load in loads:
            load.start()
        if first:
            state[...] = jnp.zeros_like(state)

    audio_t = jnp.concatenate([r[...] for r in audio], axis=0)
    inv = lax.rsqrt(jnp.sum(audio_t * audio_t, axis=0, keepdims=True) + EPS)
    inv_ref[...] = inv
    unit_t = audio_t * inv

    @pl.when(step == 0)
    def _():
        for load in loads[:2]:
            load.wait()

    def similar(k):
        part = split(unit_t[:, k * sub : (k + 1) * sub], 0, False)
        return scale * product((v_high[...], v_small[...]), part, ((1,), (0,)))

    def judge(k, scaled):
        power = jnp.exp(scaled + bias)
        sig = power * inverse(1.0 + power)
        paired = (
            lax.broadcasted_iota(jnp.int32, (n, sub), 0)
            - lax.broadcasted_iota(jnp.int32, (n, sub), 1)
        ) == offset + k * sub
        loss = jnp.sum(soft(power), axis=0, keepdims=True)
        return paired, split(jnp.where(paired, 0.0, sig), 0, False), loss

    def pull_rows(k, away, loss):
        lanes = slice(k * sub, (k + 1) * sub)
        grad_a = product((t_high[...], t_small[...]), away, ((1,), (0,)))
        inner = jnp.sum(grad_a * unit_t[:, lanes], axis=0, keepdims=True)
        for p, ref in enumerate(grads_a):
            ref[0:256, lanes] = grad_a[256 * p : 256 * p + 256, :]
            ref[256:257, lanes] = loss
            ref[257:258, lanes] = inner
            ref[258:264, lanes] = jnp.zeros((6, sub), F32)

    scores = [similar(k) for k in range(SUBS)]
    judged = [judge(0, scores[0])]

    @pl.when(step == 0)
    def _():
        for load in loads[2:]:
            load.wait()

    for k in range(SUBS):
        if k > 0:
            judged.append(judge(k, scores[k]))
        pull_rows(k, judged[k][1], judged[k][2])
    high = jnp.concatenate([j[1][0] for j in judged], axis=1)
    small = jnp.concatenate([j[1][1][:n] for j in judged] + [j[1][1][n:] for j in judged], axis=1)
    state[...] += product(split(unit_t, 1, True), (high, small), ((1,), (1,)))

    @pl.when((offset >= 0) & (offset < n))
    def _():
        at = pl.multiple_of(offset, block)
        own = jnp.concatenate(
            [jnp.sum(jnp.where(j[0], s, 0.0), axis=0, keepdims=True) for j, s in zip(judged, scores)],
            axis=1,
        )
        value = own + bias
        diag = -1.0 / (1.0 + jnp.exp(value))
        pull = near[:, pl.ds(at, block)] * diag
        inner_own = jnp.sum(pull * unit_t, axis=0, keepdims=True)
        for k, ref in enumerate(grads_a):
            ref[0:256, :] += pull[256 * k : 256 * k + 256, :]
            ref[256:257, :] += -value
            ref[257:258, :] += inner_own
        state[:, pl.ds(at, block)] += unit_t * diag

    if last:

        @pl.when(step == pl.num_programs(0) - 1)
        def _():
            core, y, x = place[0], place[1], place[2]
            for half in range(n // block):
                lanes = pl.ds(half * block, block)
                row = jnp.sum(near[:, lanes] * state[:, lanes], axis=0, keepdims=True)
                for owner in range(8):
                    whole[owner, 128:129, lanes] = row
            for owner in range(8):
                whole[owner, 129:136, :] = jnp.zeros((7, n), F32)
                for part in range(2):
                    dy = lax.rem(y + 4 - owner // 2, 4)
                    dx = lax.rem(x + 4 - 2 * (owner % 2) - part, 4)
                    at = jnp.where(core == 0, 4 * dy + dx, 4 * dx + dy) * 64
                    rows = pl.ds(pl.multiple_of(at, 64), 64)
                    whole[owner, 64 * part : 64 * part + 64, :] = state[rows, :]


def pairs(audio, video, place, scalars, before, last):
    rows = audio[0].shape[1]
    first = before is None
    n = video[1].shape[0]
    smem = pl.BlockSpec(memory_space=pltpu.SMEM)
    anywhere = pl.BlockSpec(memory_space=pl.ANY)
    shape = jax.ShapeDtypeStruct

    def still(shape):
        return pl.BlockSpec(shape, lambda i, at: (0,) * len(shape), pipeline_mode=pl.Buffered(1))

    def moving(height):
        return pl.BlockSpec((height, BLOCK), lambda i, at: (0, i))

    def turned(k):
        return pl.BlockSpec((256, BLOCK), lambda i, at: (lax.rem(at[4] + 4 - k, 4), i))

    if len(audio) == 1:
        blocks = [turned(k) for k in range(4)]
    else:
        blocks = [moving(256)] * 4
    in_specs = [smem] + blocks + [anywhere] * 5
    operands = [scalars, *(audio * (4 // len(audio))), *video]
    parts = [pltpu.VMEM(v.shape, v.dtype) for v in (video[0], *video[1:])]
    parts.append(pltpu.SemaphoreType.DMA((6,)))
    if not first:
        in_specs.append(anywhere)
        operands.append(before)
    if last:
        out_specs = [moving(264)] * 4 + [moving(1), still((8, 136, n))]
        out_shape = [shape((264, rows), F32)] * 4 + [shape((1, rows), F32), shape((8, 136, n), F32)]
        scratch = [pltpu.VMEM((1024, n), F32)] + parts
    else:
        whole = pl.BlockSpec((4, 264, BLOCK), lambda i, at: (0, 0, i))
        out_specs = [whole, moving(1), still((1024, n))]
        out_shape = [shape((4, 264, rows), F32), shape((1, rows), F32), shape((1024, n), F32)]
        scratch = parts

    def body(*refs):
        pairs_kernel(first, last, refs)

    return pl.pallas_call(
        body,
        grid_spec=pltpu.PrefetchScalarGridSpec(
            num_scalar_prefetch=1,
            grid=(rows // BLOCK,),
            in_specs=in_specs,
            out_specs=out_specs,
            scratch_shapes=scratch,
        ),
        out_shape=out_shape,
        compiler_params=pltpu.CompilerParams(vmem_limit_bytes=VMEM),
        cost_estimate=pl.CostEstimate(
            flops=6 * 2 * rows * n * 1024, bytes_accessed=24 * MIB, transcendentals=3 * rows * n
        ),
        name="pairs_last" if last else "pairs_first",
    )(place, *operands)


def perm(inner, k):
    pairs_of = []
    for core in range(2):
        for y in range(4):
            for x in range(4):
                along_x = (core == 0) == inner
                to = (core, y, (x + k) % 4) if along_x else (core, (y + k) % 4, x)
                pairs_of.append((16 * core + 4 * y + x, 16 * to[0] + 4 * to[1] + to[2]))
    return pairs_of


def move(block, inner, k):
    return lax.ppermute(block, PLANE, perm(inner, k))


def after(arrays, late):
    spec = pl.BlockSpec(memory_space=pl.ANY)
    return pl.pallas_call(
        lambda *refs: None,
        in_specs=[spec] * (len(arrays) + len(late)),
        out_specs=[spec] * len(late),
        out_shape=[jax.ShapeDtypeStruct(a.shape, a.dtype) for a in late],
        input_output_aliases={len(arrays) + i: i for i in range(len(late))},
        name="after",
    )(*arrays, *late)


def local(audio, video, scale, bias):
    z, core, y, x = (lax.axis_index(a) for a in ("z", "core", "y", "x"))
    n = video.shape[0]
    audio_t = audio.T
    rows = audio_t.shape[1]
    scalars = jnp.stack([scale, bias])
    base = (2 * z + core) * rows - (4 * y + x) * n

    whole_video = lax.all_gather(video, ("z", "core"), axis=1, tiled=True)
    row = [audio_t] + [move(audio_t, True, k) for k in (1, 2, 3)]
    part = rows // 2
    near, late = (jnp.concatenate([r[:, c * part : (c + 1) * part] for r in row], axis=0) for c in (0, 1))
    near = [near] + [move(near, False, k) for k in (1, 2, 3)]
    late = [lax.all_gather(late, PLANE, axis=0, tiled=True, axis_index_groups=OUTER)]
    outer = jnp.where(core == 0, y, x)
    place = jnp.stack([core, y, x, base, outer]).astype(jnp.int32)
    inv_v, *parts = prepare(whole_video, place)
    whole, inv_near, state = pairs(near, parts, place, scalars, None, False)
    *grads, inv_late, state = pairs(late, parts, place, scalars, state, True)
    whole = whole.reshape(1056, part)
    early = lax.psum_scatter(whole, PLANE, scatter_dimension=0, tiled=True, axis_index_groups=OUTER)
    came = [grads[0]] + [move(grads[k], False, 4 - k) for k in (2, 1, 3)]

    def rows_of(low, high):
        return jnp.concatenate([early[low:high], sum(c[low:high] for c in came)], axis=1)

    to = [
        jnp.concatenate([rows_of(64 * k, 64 * k + 64), rows_of(256, 264)], axis=0) for k in range(4)
    ]

    total_v = lax.psum_scatter(state.reshape(1088, n), ("z", "core"), scatter_dimension=0, tiled=True)
    grad_v = scale * (total_v[0:128] * inv_v - video.T * (inv_v * inv_v * total_v[128:129]))
    (kept,) = after([grad_v[:8]], [to[0]])
    blocks = [kept] + [move(to[k], True, 4 - k) for k in (1, 2, 3)]
    side, total_a = sum(t[64:] for t in blocks), sum(t[:64] for t in blocks)
    inv_a = jnp.concatenate([inv_near, inv_late], axis=1)
    row_loss, inner_a = side[0], side[1:2]
    grad_a = scale * (total_a * inv_a - audio_t * (inv_a * inv_a * inner_a))
    return row_loss, grad_a.T, grad_v.T


def solution(mesh):
    fine = Mesh(mesh.devices.reshape(4, 2, 4, 4), ("z", "core", "y", "x"))
    aud, vid = ("z", "core"), ("y", "x")
    return jax.shard_map(
        local,
        mesh=fine,
        in_specs=(P(aud, vid), P(vid, aud), P(), P()),
        out_specs=(P(aud), P(aud, vid), P(vid, aud)),
        check_vma=False,
    )
```
